32 devices in a mesh: dp: 16 (over z, y, x), tower: 2 (over core).
Axes of the slice: x: 2, y: 2, z: 4, core: 2. Of those that a mesh axis runs over, the one named last changes fastest.
Arguments:
- features: bfloat16 [16, 1364, 256], P('dp', None, 'tower'), may hold values from -6 to 6
- bn_mean: float32 [256], replicated, may hold values from -3 to 3
- bn_var: float32 [256], replicated, may hold values from 0.25 to 4
- tower_weight: bfloat16 [2, 4, 3, 3, 256, 256], P('tower'), may hold values from -0.125 to 0.125
- norm_gain: float32 [2, 4, 256], P('tower'), may hold values from 0.5 to 1.5
- norm_bias: float32 [2, 4, 256], P('tower'), may hold values from -1.5 to 1.5
- head_weight: bfloat16 [3, 3, 256, 85], replicated, may hold values from -0.0625 to 0.0625
- head_bias: float32 [85], replicated, may hold values from -2 to 2
- level_scale: float32 [5], replicated, may hold values from 0.5 to 1.5
- cls_cot: bfloat16 [16, 1364, 80], P('dp'), may hold values from -6 to 6
- reg_cot: bfloat16 [16, 1364, 5], P('dp'), may hold values from -6 to 6
- positive: int32 [16, 1364], P('dp'), may hold values from 0 to 1, as said below
Outputs:
- feature_grad: bfloat16 [16, 1364, 256], P('dp', None, 'tower')
- tower_weight_grad: float32 [2, 4, 3, 3, 256, 256], P('tower')
- norm_gain_grad: float32 [2, 4, 256], P('tower')
- norm_bias_grad: float32 [2, 4, 256], P('tower')
- head_weight_grad: float32 [3, 3, 256, 85], replicated
- head_bias_grad: float32 [85], replicated
- level_scale_grad: float32 [5], replicated
The draws below stay inside these ranges and needn't reach their ends.
Inputs may be any that keep to these rules, and one draw needn't show every extreme that they name: 1 marks a positive location, 0 any other.
All inputs are finite; a program needn't handle non-finite values.
Results may differ from the reference program's by a relative error of at most 0.017.
Values may be sent and summed in bfloat16 or wider, within the bound.
No kernel may reach another device: no remote copies, remote signals or barrier semaphores. Data moves between devices by JAX's collectives and lax.ppermute only.
A program may use at most 128 MiB of HBM per device.

```python
import math
import jax
import jax.numpy as jnp
from jax import lax

C = 256
GROUPS = 32
CLASSES = 80
LAYERS = 4
LEVELS = 5
H3 = 16
W3 = 64
HEAD = 85
PIX = 1364
IMAGES = 16


def draw_positive(key, part):
    key = jax.random.fold_in(key, 7)
    rolled = jax.random.randint(key, (IMAGES, PIX), 0, 10)
    pixel_index = jnp.arange(PIX)[None, :]
    return jnp.where(pixel_index < H3 * W3, rolled < 3, rolled < 1).astype(jnp.int32)


def levels(stream_key, extent, shards, least, high):
    level, own = 1.0, jax.random.fold_in(stream_key, 6)
    for position, blocks in shards:
        steps = jnp.exp(jax.random.uniform(jax.random.fold_in(own, position), (blocks,), jnp.float32, least / len(shards), high / len(shards)))
        level = level * jnp.repeat(steps, extent[position] // blocks).reshape([-1 if axis == position else 1 for axis in range(len(extent))])
    return level


def noise(own_key, extent, scale, reach, split=(), held_as=jnp.bfloat16):
    result = scale * jax.random.normal(own_key, extent, jnp.float32)
    if split:
        result = result * levels(own_key, extent, split, -0.22, 0.18)
    return jnp.clip(result, -reach, reach).astype(held_as)


def setup_inputs(seed: int = 0) -> dict:
    streams_of = jax.random.split(jax.random.key(seed), 13)
    return {
        "features": noise(streams_of[0], (IMAGES, PIX, C), 1.0, 6.0, ((0, 16), (2, 2))),
        "bn_mean": noise(streams_of[1], (C,), 0.5, 3.0, (), jnp.float32),
        "bn_var": jnp.clip(jnp.exp(jax.random.uniform(streams_of[2], (C,), jnp.float32, math.log(0.25), math.log(4.0))), 0.25, 4.0),
        "tower_weight": noise(streams_of[3], (2, LAYERS, 3, 3, C, C), (9 * C) ** -0.5, 0.125, ((0, 2),)),
        "norm_gain": jnp.clip(1.0 + 0.1 * jax.random.normal(streams_of[4], (2, LAYERS, C), jnp.float32), 0.5, 1.5),
        "norm_bias": noise(streams_of[5], (2, LAYERS, C), 0.3, 1.5, ((0, 2),), jnp.float32),
        "head_weight": noise(streams_of[6], (3, 3, C, HEAD), (4 * 9 * C) ** -0.5, 0.0625),
        "head_bias": noise(streams_of[7], (HEAD,), 0.5, 2.0, (), jnp.float32),
        "level_scale": jnp.clip(jnp.exp(jax.random.uniform(streams_of[8], (LEVELS,), jnp.float32, math.log(0.5), math.log(1.5))), 0.5, 1.5),
        "cls_cot": noise(streams_of[9], (IMAGES, PIX, CLASSES), 1.0, 6.0, ((0, 16),)),
        "reg_cot": noise(streams_of[10], (IMAGES, PIX, 5), 1.0, 6.0, ((0, 16),)),
        "positive": draw_positive(jax.random.fold_in(streams_of[12], 71), 0),
    }


@jax.custom_vjp
def low(v):
    return lax.optimization_barrier(v.astype(jnp.bfloat16)).astype(jnp.float32)

@jax.custom_vjp
def low_back(v):
    return v

def low_keep(v):
    return (low(v), None)

def low_pass(kept, grad):
    return (grad,)

def back_keep(v):
    return (v, None)

def back_low(kept, grad):
    return (low(grad),)
low.defvjp(low_keep, low_pass)
low_back.defvjp(back_keep, back_low)
norm_epsilon = 1e-05

def convolve(values, kernel):
    return lax.conv_general_dilated(values, kernel, (1, 1), 'SAME', dimension_numbers=('NHWC', 'HWIO', 'NHWC'), precision=lax.Precision.HIGHEST)

def group_act(pre_norm, gain, shift):
    batch, grid_rows, grid_cols, channels = pre_norm.shape
    grouped = pre_norm.reshape(batch, grid_rows * grid_cols, GROUPS, channels // GROUPS)
    center = lax.optimization_barrier(jnp.mean(grouped, axis=(1, 3), keepdims=True))
    spread = lax.optimization_barrier(jnp.mean(jnp.square(grouped - center), axis=(1, 3), keepdims=True))
    normed = ((grouped - center) * lax.rsqrt(spread + norm_epsilon)).reshape(pre_norm.shape)
    return jax.nn.silu(normed * gain + shift)

def level_slices(flat):
    pieces = []
    offset = 0
    for level_index in range(LEVELS):
        grid_rows = H3 // 2 ** level_index
        grid_cols = W3 // 2 ** level_index
        pieces.append(flat[:, offset:offset + grid_rows * grid_cols].reshape(flat.shape[0], grid_rows, grid_cols, flat.shape[2]))
        offset = offset + grid_rows * grid_cols
    return pieces

def reference(features, bn_mean, bn_var, tower_weight, norm_gain, norm_bias, head_weight, head_bias, level_scale, cls_cot, reg_cot, positive):
    cls_levels = level_slices(cls_cot.astype(jnp.float32))
    reg_levels = level_slices(reg_cot.astype(jnp.float32))
    pos_levels = level_slices(positive.astype(jnp.float32)[:, :, None])

    def objective(feature_in, tower_in, gain_in, shift_in, head_in, bias_in, scale_in):
        base = low((feature_in - bn_mean) * lax.rsqrt(bn_var + norm_epsilon))
        base_levels = level_slices(base)
        total = jnp.zeros((), jnp.float32)
        for level_index in range(LEVELS):
            for tower_index in range(2):
                acts = base_levels[level_index]
                for layer_index in range(LAYERS):
                    pre_norm = low_back(convolve(acts, tower_in[tower_index, layer_index]))
                    acts = low(group_act(pre_norm, gain_in[tower_index, layer_index], shift_in[tower_index, layer_index]))
                if tower_index == 0:
                    logits = low_back(convolve(acts, head_in[..., :CLASSES]) + bias_in[:CLASSES])
                    total = total + jnp.sum(logits * cls_levels[level_index])
                else:
                    raw_out = low_back(convolve(acts, head_in[..., CLASSES:]) + bias_in[CLASSES:])
                    distance = jnp.exp(scale_in[level_index] * raw_out[..., :4])
                    outputs = jnp.concatenate([distance, raw_out[..., 4:]], axis=-1)
                    total = total + jnp.sum(outputs * reg_levels[level_index] * pos_levels[level_index])
        return total
    primals = (features.astype(jnp.float32), tower_weight.astype(jnp.float32), norm_gain, norm_bias, head_weight.astype(jnp.float32), head_bias, level_scale)
    _, pull = jax.vjp(objective, *primals)
    grads_all = pull(jnp.ones((), jnp.float32))
    return (grads_all[0].astype(jnp.bfloat16), grads_all[1], grads_all[2], grads_all[3], grads_all[4], grads_all[5], grads_all[6])
```

```python
import functools

import jax
import jax.numpy as jnp
from jax import lax
from jax.experimental import pallas as pl
from jax.experimental.pallas import tpu as pltpu
from jax.sharding import PartitionSpec as P

C = 256
GROUP = 8
CLASSES = 80
HEAD = 85
LANES = 128
LAYERS = 4
CELLS = 1408
PIX = 1364
COUNTS = (1024, 256, 64, 16, 4)
PARTS = ((0, 1024, 64, 64), (1024, 256, 1152, 32), (1280, 128, 1440, 16))
PADDED = 1584
GAPS = ((0, 64), (1088, 64), (1408, 32), (1568, 16))
TILE = 64
EPS = 1e-05
f32 = jnp.float32
bf16 = jnp.bfloat16
VMEM = pl.BlockSpec(memory_space=pltpu.VMEM)
SMEM = pl.BlockSpec(memory_space=pltpu.SMEM)
ANY = pl.BlockSpec(memory_space=pl.ANY)


def params():
    return pltpu.CompilerParams(vmem_limit_bytes=56 << 20)


def tail_masks():
    row = lax.broadcasted_iota(jnp.int32, (TILE, C), 0)
    third = ((row >= 16) & (row < 24)) | ((row >= 32) & (row < 40))
    fourth = (row >= 26) & (row < 30)
    return third, fourth


def pick(third, fourth, vec):
    return jnp.where(third, vec[3:4], jnp.where(fourth, vec[4:5], 0.0))


def fold(tile):
    return jnp.sum(tile.reshape(TILE // 8, 8, tile.shape[1]), axis=0)


def group_sum(vec):
    lane = lax.broadcasted_iota(jnp.int32, vec.shape, 1)
    for step in (1, 2, 4):
        up = pltpu.roll(vec, vec.shape[1] - step, 1)
        down = pltpu.roll(vec, step, 1)
        vec = vec + jnp.where((lane & step) == 0, up, down)
    return vec


def counts_column():
    row = lax.broadcasted_iota(jnp.int32, (8, C), 0)
    out = jnp.full((8, C), 1.0, f32)
    for level, cells in enumerate(COUNTS):
        out = jnp.where(row == level, 1.0 / (cells * GROUP), out)
    return out


def stack_rows(rows):
    row = lax.broadcasted_iota(jnp.int32, (8, rows[0].shape[1]), 0)
    out = jnp.zeros((8, rows[0].shape[1]), f32)
    for place, value in enumerate(rows):
        out = jnp.where(row == place, jnp.sum(value, axis=0, keepdims=True), out)
    return out


def each_tile(step, init):
    results = []
    for level, (tiles, cell, row, width) in enumerate(((16, 0, 64, 64), (4, 1024, 1152, 32), (1, 1280, 1440, 16))):
        carry = init

        def run(i, carry, level=level, cell=cell, row=row, width=width):
            at = pl.multiple_of(i * TILE, TILE)
            return step(level, cell + at, row + at, width, carry)

        if tiles == 1:
            carry = step(level, cell, row, width, carry)
        else:
            carry = lax.fori_loop(0, tiles, run, carry, unroll=2)
        results.append(carry)
    results.append(step(3, 1344, 1504, 16, init))
    return results


def write_shifted(buf, row, width, tile, lanes, flip):
    at = lax.broadcasted_iota(jnp.int32, tile.shape, 0) & (width - 1)
    before = jnp.where(at == 0, 0.0, pltpu.roll(tile, 1, 0))
    after = jnp.where(at == width - 1, 0.0, pltpu.roll(tile, TILE - 1, 0))
    if flip:
        before, after = after, before
    rows = pl.ds(row, TILE)
    buf[rows, 0:lanes] = before.astype(bf16)
    buf[rows, lanes : 2 * lanes] = tile.astype(bf16)
    buf[rows, 2 * lanes : 3 * lanes] = after.astype(bf16)


def clear_gaps(buf):
    for row, rows in GAPS:
        buf[row : row + rows, :] = jnp.zeros((rows, buf.shape[1]), bf16)


def conv_into(out, buf, weight, lanes):
    for cell, cells, row, width in PARTS:
        for first in range(0, cells, 256):
            size = min(256, cells - first)
            at = row + first
            left = jnp.concatenate([buf[at + d * width : at + d * width + size, :] for d in (-1, 0, 1)], axis=1)
            out[cell + first : cell + first + size, :] = jnp.dot(left, weight, preferred_element_type=f32)


def conv_back_into(out, buf, weight, lanes):
    for cell, cells, row, width in PARTS:
        for first in range(0, cells, 256):
            size = min(256, cells - first)
            total = None
            for i in range(3):
                at = row + first - (i - 1) * width
                for j in range(3):
                    term = lax.dot_general(
                        buf[at : at + size, j * lanes : (j + 1) * lanes],
                        weight(i * 3 + j),
                        (((1,), (1,)), ((), ())),
                        preferred_element_type=f32,
                    )
                    total = term if total is None else total + term
            out[cell + first : cell + first + size, :] = total


def kernel_grad(turned, buf, i):
    total = None
    for cell, cells, row, width in PARTS:
        at = row - (i - 1) * width
        term = jnp.dot(turned[:, cell : cell + cells], buf[at : at + cells, :], preferred_element_type=f32)
        total = term if total is None else total + term
    return total


def norm_stats(z):
    third, fourth = tail_masks()

    def sums(level, cell, row, width, carry):
        tile = z[pl.ds(cell, TILE), :]
        if level < 3:
            return carry + fold(tile)
        return (fold(jnp.where(third, tile, 0.0)), fold(jnp.where(fourth, tile, 0.0)))

    zero = jnp.zeros((8, C), f32)
    inv_counts = counts_column()
    r = each_tile(sums, zero)
    mean = group_sum(stack_rows([r[0], r[1], r[2], r[3][0], r[3][1]])) * inv_counts

    def squares(level, cell, row, width, carry):
        tile = z[pl.ds(cell, TILE), :]
        if level < 3:
            d = tile - mean[level : level + 1]
            return carry + fold(d * d)
        d3 = jnp.where(third, tile - mean[3:4], 0.0)
        d4 = jnp.where(fourth, tile - mean[4:5], 0.0)
        return (fold(d3 * d3), fold(d4 * d4))

    r = each_tile(squares, zero)
    var = group_sum(stack_rows([r[0], r[1], r[2], r[3][0], r[3][1]])) * inv_counts
    return mean, lax.rsqrt(var + EPS)


def forward_act(z, mean, rstd, gain, shift, buf):
    scale = rstd * gain
    offset = shift - mean * scale
    third, fourth = tail_masks()

    def act(level, cell, row, width, carry):
        tile = z[pl.ds(cell, TILE), :]
        if level < 3:
            y = tile * scale[level : level + 1] + offset[level : level + 1]
        else:
            y = tile * pick(third, fourth, scale) + pick(third, fourth, offset)
        a = y * (0.5 * jnp.tanh(0.5 * y) + 0.5)
        if level == 3:
            a = jnp.where(third | fourth, a, 0.0)
        write_shifted(buf, row, width, a, C, False)
        return carry

    each_tile(act, jnp.int32(0))


def backward_norm(da, z, mean, rstd, gain, shift, buf):
    third, fourth = tail_masks()
    neg = -mean * rstd
    zero = jnp.zeros((8, C), f32)

    def rows(level, vec):
        if level < 3:
            return vec[level : level + 1]
        return pick(third, fourth, vec)

    def first(level, cell, row, width, carry):
        zhat = z[pl.ds(cell, TILE), :] * rows(level, rstd) + rows(level, neg)
        y = zhat * gain + shift
        s = 0.5 * jnp.tanh(0.5 * y) + 0.5
        dy = da[pl.ds(cell, TILE), :] * (s * (1.0 + y * (1.0 - s)))
        da[pl.ds(cell, TILE), :] = dy
        dyz = dy * zhat
        if level < 3:
            return (carry[0] + fold(dy), carry[1] + fold(dyz))
        return tuple(fold(jnp.where(m, v, 0.0)) for v in (dy, dyz) for m in (third, fourth))

    r = each_tile(first, (zero, zero))
    sum_dy = stack_rows([r[0][0], r[1][0], r[2][0], r[3][0], r[3][1]])
    sum_dyz = stack_rows([r[0][1], r[1][1], r[2][1], r[3][2], r[3][3]])
    inv_counts = counts_column()
    mean_e = group_sum(sum_dy * gain) * inv_counts
    mean_ez = group_sum(sum_dyz * gain) * inv_counts
    on_dy = rstd * gain
    on_zhat = rstd * mean_ez
    on_z = -on_zhat * rstd
    flat = -rstd * mean_e - on_zhat * neg

    def second(level, cell, row, width, carry):
        dz = (
            da[pl.ds(cell, TILE), :] * rows(level, on_dy)
            + z[pl.ds(cell, TILE), :] * rows(level, on_z)
            + rows(level, flat)
        )
        write_shifted(buf, row, width, dz, C, True)
        return carry

    each_tile(second, jnp.int32(0))
    return jnp.sum(sum_dyz, axis=0, keepdims=True), jnp.sum(sum_dy, axis=0, keepdims=True)


def center(buf, cell, cells, row, lanes):
    return buf[row : row + cells, lanes : 2 * lanes]


def layer_back(da, z, a, stats, gain, shift, weight, buf, turned, dw, vec):
    turned[...] = a.T
    dgain, dshift = backward_norm(da, z, stats[0:8], stats[8:16], gain, shift, buf)
    row = lax.broadcasted_iota(jnp.int32, (8, C), 0)
    vec[...] = jnp.where(row == 0, dgain, jnp.where(row == 1, dshift, 0.0))
    for i in range(3):
        grad = kernel_grad(turned, buf, i).astype(bf16)
        for j in range(3):
            dw[i * 3 + j] = grad[:, j * C : (j + 1) * C]
    conv_back_into(da, buf, lambda tap: weight[tap * C : (tap + 1) * C, :], C)


def first_kernel(
    tower, scale, x, bn, w_hbm, gains, shifts, head, head_bias, cot,
    z_out, a_out, stats_out, da_out, dw_out, vec_out, dhead_out, hvec_out,
    w, buf, zs, hw, hg, hbuf, u, turned, sems,
):
    loads = [pltpu.make_async_copy(w_hbm.at[l], w.at[l], sems.at[l]) for l in range(LAYERS)]
    for load in loads:
        load.start()
    clear_gaps(buf)
    clear_gaps(hbuf)
    hw[...] = jnp.zeros(hw.shape, bf16)
    hw[:, 0:HEAD] = head[...]
    inverse = lax.rsqrt(bn[8:9] + EPS)
    mean0 = bn[0:1]

    def base(level, cell, row, width, carry):
        tile = (x[pl.ds(cell, TILE), :].astype(f32) - mean0) * inverse
        if level == 3:
            third, fourth = tail_masks()
            tile = jnp.where(third | fourth, tile, 0.0)
        write_shifted(buf, row, width, tile, C, False)
        return carry

    each_tile(base, jnp.int32(0))
    stats = None
    for l in range(LAYERS):
        if l < LAYERS - 1:
            for cell, cells, row, width in PARTS:
                a_out[l, cell : cell + cells, :] = center(buf, cell, cells, row, C)
        else:
            for cell, cells, row, width in PARTS:
                turned[:, cell : cell + cells] = center(buf, cell, cells, row, C).T
        loads[l].wait()
        z = zs.at[...] if l == LAYERS - 1 else z_out.at[l]
        conv_into(z, buf, w[l], C)
        mean, rstd = norm_stats(z)
        if l < LAYERS - 1:
            stats_out[l, 0:8, :] = mean
            stats_out[l, 8:16, :] = rstd
        else:
            stats = jnp.concatenate([mean, rstd], axis=0)
        forward_act(z, mean, rstd, gains[l : l + 1], shifts[l : l + 1], buf)

    hvec_out[...] = jnp.zeros(hvec_out.shape, f32)
    for cell in range(0, CELLS, TILE):
        hg[cell : cell + TILE, :] = cot[cell : cell + TILE, :].astype(f32)

    @pl.when(tower[0] == 1)
    def _():
        conv_into(u, buf, hw[...], C)
        lane = lax.broadcasted_iota(jnp.int32, (TILE, LANES), 1)
        dist_lane = (lane >= CLASSES) & (lane < CLASSES + 4)
        row = lax.broadcasted_iota(jnp.int32, (TILE, LANES), 0)
        third = ((row >= 16) & (row < 24)) | ((row >= 32) & (row < 40))
        fourth = (row >= 26) & (row < 30)

        def box(level, cell, row, width, carry):
            raw = u[pl.ds(cell, TILE), :] + head_bias[...]
            g = hg[pl.ds(cell, TILE), :]
            if level < 3:
                ls = scale[level]
                use = dist_lane
            else:
                ls = jnp.where(third, scale[3], scale[4])
                use = dist_lane & (third | fourth)
            weighted = jnp.where(use, g * jnp.exp(ls * raw), 0.0)
            hg[pl.ds(cell, TILE), :] = jnp.where(dist_lane, weighted * ls, g)
            term = weighted * raw
            if level < 3:
                return carry + fold(term)
            return (fold(jnp.where(third, term, 0.0)), fold(jnp.where(fourth, term, 0.0)))

        r = each_tile(box, jnp.zeros((8, LANES), f32))
        hvec_out[0:8, :] = stack_rows([r[0], r[1], r[2], r[3][0], r[3][1]])

    def head_rows(level, cell, row, width, carry):
        tile = hg[pl.ds(cell, TILE), :].astype(bf16).astype(f32)
        write_shifted(hbuf, row, width, tile, LANES, True)
        return carry + fold(tile)

    r = each_tile(head_rows, jnp.zeros((8, LANES), f32))
    total = jnp.sum(r[0] + r[1] + r[2] + r[3], axis=0, keepdims=True)
    hvec_out[8:16, :] = jnp.where(lax.broadcasted_iota(jnp.int32, (8, LANES), 0) == 0, total, 0.0)

    a4t = jnp.concatenate([center(buf, c, n, r, C).T for c, n, r, _ in PARTS], axis=1)
    for i in range(3):
        grad = kernel_grad(a4t, hbuf, i).astype(bf16)
        for j in range(3):
            dhead_out[i * 3 + j] = grad[:, j * LANES : (j + 1) * LANES]
    conv_back_into(da_out, hbuf, lambda tap: hw[tap * C : (tap + 1) * C, :], LANES)

    l = LAYERS - 1
    dgain, dshift = backward_norm(da_out, zs, stats[0:8], stats[8:16], gains[l : l + 1], shifts[l : l + 1], buf)
    row = lax.broadcasted_iota(jnp.int32, (8, C), 0)
    vec_out[...] = jnp.where(row == 0, dgain, jnp.where(row == 1, dshift, 0.0))
    for i in range(3):
        grad = kernel_grad(turned, buf, i).astype(bf16)
        for j in range(3):
            dw_out[i * 3 + j] = grad[:, j * C : (j + 1) * C]
    conv_back_into(da_out, buf, lambda tap: w[l, tap * C : (tap + 1) * C, :], C)


def middle_kernel(l, da_in, z, a, stats, gains, shifts, w, da_out, dw_out, vec_out, buf, turned):
    clear_gaps(buf)
    da_out[...] = da_in[...]
    layer_back(
        da_out, z.at[0], a[0], stats[0], gains[l : l + 1], shifts[l : l + 1], w.at[0], buf, turned, dw_out, vec_out
    )


def shape(dims, dtype):
    return jax.ShapeDtypeStruct(dims, dtype)


def run_first(tower, scale, x, bn, w, gains, shifts, head, head_bias, cot):
    return pl.pallas_call(
        first_kernel,
        out_shape=[
            shape((LAYERS - 1, CELLS, C), f32),
            shape((LAYERS - 1, CELLS, C), bf16),
            shape((LAYERS - 1, 16, C), f32),
            shape((CELLS, C), f32),
            shape((9, C, C), bf16),
            shape((8, C), f32),
            shape((9, C, LANES), bf16),
            shape((16, LANES), f32),
        ],
        in_specs=[SMEM, SMEM, VMEM, VMEM, ANY, VMEM, VMEM, VMEM, VMEM, VMEM],
        out_specs=[VMEM] * 8,
        scratch_shapes=[
            pltpu.VMEM((LAYERS, 9 * C, C), bf16),
            pltpu.VMEM((PADDED, 3 * C), bf16),
            pltpu.VMEM((CELLS, C), f32),
            pltpu.VMEM((9 * C, LANES), bf16),
            pltpu.VMEM((CELLS, LANES), f32),
            pltpu.VMEM((PADDED, 3 * LANES), bf16),
            pltpu.VMEM((CELLS, LANES), f32),
            pltpu.VMEM((C, CELLS), bf16),
            pltpu.SemaphoreType.DMA((LAYERS,)),
        ],
        compiler_params=params(),
        name="forward_and_heads",
    )(tower, scale, x, bn, w, gains, shifts, head, head_bias, cot)


def run_middle(l, da, z, a, stats, gains, shifts, w):
    one = lambda dims: pl.BlockSpec((1,) + dims, lambda i: (l,) + (0,) * len(dims))
    whole = lambda dims: pl.BlockSpec(dims, lambda i: (0,) * len(dims))
    return pl.pallas_call(
        functools.partial(middle_kernel, l),
        grid=(1,),
        out_shape=[shape((CELLS, C), f32), shape((9, C, C), bf16), shape((8, C), f32)],
        in_specs=[
            whole((CELLS, C)),
            one((CELLS, C)),
            one((CELLS, C)),
            one((16, C)),
            whole((LAYERS, C)),
            whole((LAYERS, C)),
            one((9 * C, C)),
        ],
        out_specs=[whole((CELLS, C)), whole((9, C, C)), whole((8, C))],
        scratch_shapes=[pltpu.VMEM((PADDED, 3 * C), bf16), pltpu.VMEM((C, CELLS), bf16)],
        compiler_params=params(),
        name=f"layer_gradients_{l}",
    )(da, z, a, stats, gains, shifts, w)


def to_cells(flat):
    gap = lambda rows: jnp.zeros((rows, flat.shape[1]), flat.dtype)
    return jnp.concatenate(
        [flat[:1344], gap(16), flat[1344:1352], gap(2), flat[1360:1364], gap(2), flat[1352:1360], gap(24)], axis=0
    )


def to_flat(cells):
    return jnp.concatenate([cells[:1344], cells[1360:1368], cells[1376:1384], cells[1370:1374]], axis=0)


def body(
    features, bn_mean, bn_var, tower_weight, norm_gain, norm_bias, head_weight, head_bias, level_scale,
    cls_cot, reg_cot, positive, *, dp,
):
    tower = lax.axis_index("tower")
    whole = lax.all_gather(features, "tower", axis=2, tiled=True)[0]
    x = to_cells(whole)
    cls = jnp.where(tower == 0, cls_cot[0], 0)
    box = jnp.where((tower == 1) & (positive[0] == 1)[:, None], reg_cot[0], 0)
    cot = to_cells(jnp.concatenate([cls, box, jnp.zeros((PIX, LANES - HEAD), bf16)], axis=1))
    bn = jnp.concatenate([jnp.broadcast_to(bn_mean, (8, C)), jnp.broadcast_to(bn_var, (8, C))], axis=0)
    w = tower_weight[0].reshape(LAYERS, 9 * C, C)
    bias = jnp.pad(head_bias, (0, LANES - HEAD))[None]
    gains, shifts = norm_gain[0], norm_bias[0]
    z, a, stats, da, dw3, vec3, dhead, hvec = run_first(
        tower.reshape(1), level_scale, x, bn, w, gains, shifts, head_weight.reshape(9 * C, HEAD), bias, cot
    )
    dws, vecs = [None] * LAYERS, [None] * LAYERS
    dws[3], vecs[3] = dw3, vec3
    for l in (2, 1, 0):
        da, dws[l], vecs[l] = run_middle(l, da, z, a, stats, gains, shifts, w)

    kernel_sum = lax.psum(jnp.stack(dws), "dp").astype(f32).reshape(1, LAYERS, 3, 3, C, C)
    vec_sum = lax.psum(jnp.stack(vecs), "dp")
    head_sum, hvec_sum = lax.psum((dhead, hvec), ("dp", "tower"))
    grad = lax.psum_scatter(to_flat(da).astype(bf16), "tower", scatter_dimension=1, tiled=True).astype(f32)
    inverse = lax.rsqrt(lax.dynamic_slice_in_dim(bn_var, tower * (C // 2), C // 2) + EPS)
    feature_grad = (grad * inverse).astype(bf16)[None]
    return (
        feature_grad,
        kernel_sum,
        vec_sum[None, :, 0],
        vec_sum[None, :, 1],
        head_sum[..., :HEAD].astype(f32).reshape(3, 3, C, HEAD),
        hvec_sum[8, :HEAD],
        jnp.sum(hvec_sum[:5], axis=1),
    )


def solution(mesh):
    return jax.shard_map(
        functools.partial(body, dp=mesh.shape["dp"]),
        mesh=mesh,
        in_specs=(
            P("dp", None, "tower"),
            P(),
            P(),
            P("tower", None, None, None, None, None),
            P("tower", None, None),
            P("tower", None, None),
            P(),
            P(),
            P(),
            P("dp", None, None),
            P("dp", None, None),
            P("dp", None),
        ),
        out_specs=(
            P("dp", None, "tower"),
            P("tower", None, None, None, None, None),
            P("tower", None, None),
            P("tower", None, None),
            P(),
            P(),
            P(),
        ),
        check_vma=False,
    )
```

```python
import functools

import jax
import jax.numpy as jnp
from jax import lax
from jax.experimental import pallas as pl
from jax.experimental.pallas import tpu as pltpu
from jax.sharding import PartitionSpec as P

C = 256
GROUP = 8
CLASSES = 80
HEAD = 85
LANES = 128
LAYERS = 4
CELLS = 1408
PIX = 1364
COUNTS = (1024, 256, 64, 16, 4)
PARTS = ((0, 1024, 64, 64), (1024, 256, 1152, 32), (1280, 128, 1440, 16))
PADDED = 1584
GAPS = ((0, 64), (1088, 64), (1408, 32), (1568, 16))
TILE = 64
EPS = 1e-05
f32 = jnp.float32
bf16 = jnp.bfloat16
VMEM = pl.BlockSpec(memory_space=pltpu.VMEM)
SMEM = pl.BlockSpec(memory_space=pltpu.SMEM)
ANY = pl.BlockSpec(memory_space=pl.ANY)


VEC = 32
SPLITS = 3


def params(mib=56):
    return pltpu.CompilerParams(vmem_limit_bytes=mib << 20)


def tail_masks():
    row = lax.broadcasted_iota(jnp.int32, (TILE, C), 0)
    third = ((row >= 16) & (row < 24)) | ((row >= 32) & (row < 40))
    fourth = (row >= 26) & (row < 30)
    return third, fourth


def pick(third, fourth, vec):
    return jnp.where(third, vec[3:4], jnp.where(fourth, vec[4:5], 0.0))


def fold(tile):
    return jnp.sum(tile.reshape(TILE // 8, 8, tile.shape[1]), axis=0)


def group_sum(vec):
    lane = lax.broadcasted_iota(jnp.int32, vec.shape, 1)
    for step in (1, 2, 4):
        up = pltpu.roll(vec, vec.shape[1] - step, 1)
        down = pltpu.roll(vec, step, 1)
        vec = vec + jnp.where((lane & step) == 0, up, down)
    return vec


def counts_column():
    row = lax.broadcasted_iota(jnp.int32, (8, C), 0)
    out = jnp.full((8, C), 1.0, f32)
    for level, cells in enumerate(COUNTS):
        out = jnp.where(row == level, 1.0 / (cells * GROUP), out)
    return out


def stack_rows(rows):
    row = lax.broadcasted_iota(jnp.int32, (8, rows[0].shape[1]), 0)
    out = jnp.zeros((8, rows[0].shape[1]), f32)
    for place, value in enumerate(rows):
        out = jnp.where(row == place, jnp.sum(value, axis=0, keepdims=True), out)
    return out


def each_tile(step, init):
    results = []
    for level, (tiles, cell, row, width) in enumerate(((16, 0, 64, 64), (4, 1024, 1152, 32), (1, 1280, 1440, 16))):
        carry = init

        def run(i, carry, level=level, cell=cell, row=row, width=width):
            at = pl.multiple_of(i * TILE, TILE)
            return step(level, cell + at, row + at, width, carry)

        if tiles == 1:
            carry = step(level, cell, row, width, carry)
        else:
            carry = lax.fori_loop(0, tiles, run, carry, unroll=2)
        results.append(carry)
    results.append(step(3, 1344, 1504, 16, init))
    return results


def write_shifted(buf, row, width, tile, lanes, flip):
    at = lax.broadcasted_iota(jnp.int32, tile.shape, 0) & (width - 1)
    before = jnp.where(at == 0, 0.0, pltpu.roll(tile, 1, 0))
    after = jnp.where(at == width - 1, 0.0, pltpu.roll(tile, TILE - 1, 0))
    if flip:
        before, after = after, before
    rows = pl.ds(row, TILE)
    buf[rows, 0:lanes] = before.astype(bf16)
    buf[rows, lanes : 2 * lanes] = tile.astype(bf16)
    buf[rows, 2 * lanes : 3 * lanes] = after.astype(bf16)


def clear_gaps(buf):
    for row, rows in GAPS:
        buf[row : row + rows, :] = jnp.zeros((rows, buf.shape[1]), bf16)


def conv_into(out, buf, weight, lanes):
    for cell, cells, row, width in PARTS:
        for first in range(0, cells, 256):
            size = min(256, cells - first)
            at = row + first
            left = jnp.concatenate([buf[at + d * width : at + d * width + size, :] for d in (-1, 0, 1)], axis=1)
            out[cell + first : cell + first + size, :] = jnp.dot(left, weight, preferred_element_type=f32)


def conv_back_into(out, buf, weight, lanes):
    for cell, cells, row, width in PARTS:
        for first in range(0, cells, 256):
            size = min(256, cells - first)
            total = None
            for i in range(3):
                at = row + first - (i - 1) * width
                for j in range(3):
                    term = lax.dot_general(
                        buf[at : at + size, j * lanes : (j + 1) * lanes],
                        weight(i * 3 + j),
                        (((1,), (1,)), ((), ())),
                        preferred_element_type=f32,
                    )
                    total = term if total is None else total + term
            out[cell + first : cell + first + size, :] = total


def kernel_grad(turned, buf, i):
    total = None
    for cell, cells, row, width in PARTS:
        at = row - (i - 1) * width
        term = jnp.dot(turned[:, cell : cell + cells], buf[at : at + cells, :], preferred_element_type=f32)
        total = term if total is None else total + term
    return total


def norm_stats(z):
    third, fourth = tail_masks()

    def sums(level, cell, row, width, carry):
        tile = z[pl.ds(cell, TILE), :]
        if level < 3:
            return carry + fold(tile)
        return (fold(jnp.where(third, tile, 0.0)), fold(jnp.where(fourth, tile, 0.0)))

    zero = jnp.zeros((8, C), f32)
    inv_counts = counts_column()
    r = each_tile(sums, zero)
    mean = group_sum(stack_rows([r[0], r[1], r[2], r[3][0], r[3][1]])) * inv_counts

    def squares(level, cell, row, width, carry):
        tile = z[pl.ds(cell, TILE), :]
        if level < 3:
            d = tile - mean[level : level + 1]
            return carry + fold(d * d)
        d3 = jnp.where(third, tile - mean[3:4], 0.0)
        d4 = jnp.where(fourth, tile - mean[4:5], 0.0)
        return (fold(d3 * d3), fold(d4 * d4))

    r = each_tile(squares, zero)
    var = group_sum(stack_rows([r[0], r[1], r[2], r[3][0], r[3][1]])) * inv_counts
    return mean, lax.rsqrt(var + EPS)


def forward_act(z, mean, rstd, gain, shift, buf):
    scale = rstd * gain
    offset = shift - mean * scale
    third, fourth = tail_masks()

    def act(level, cell, row, width, carry):
        tile = z[pl.ds(cell, TILE), :]
        if level < 3:
            y = tile * scale[level : level + 1] + offset[level : level + 1]
        else:
            y = tile * pick(third, fourth, scale) + pick(third, fourth, offset)
        a = y * (0.5 * jnp.tanh(0.5 * y) + 0.5)
        if level == 3:
            a = jnp.where(third | fourth, a, 0.0)
        write_shifted(buf, row, width, a, C, False)
        return carry

    each_tile(act, jnp.int32(0))


def backward_norm(da, z, mean, rstd, gain, shift, buf):
    third, fourth = tail_masks()
    neg = -mean * rstd
    zero = jnp.zeros((8, C), f32)

    def rows(level, vec):
        if level < 3:
            return vec[level : level + 1]
        return pick(third, fourth, vec)

    def first(level, cell, row, width, carry):
        zhat = z[pl.ds(cell, TILE), :] * rows(level, rstd) + rows(level, neg)
        y = zhat * gain + shift
        s = 0.5 * jnp.tanh(0.5 * y) + 0.5
        dy = da[pl.ds(cell, TILE), :] * (s * (1.0 + y * (1.0 - s)))
        da[pl.ds(cell, TILE), :] = dy
        dyz = dy * zhat
        if level < 3:
            return (carry[0] + fold(dy), carry[1] + fold(dyz))
        return tuple(fold(jnp.where(m, v, 0.0)) for v in (dy, dyz) for m in (third, fourth))

    r = each_tile(first, (zero, zero))
    sum_dy = stack_rows([r[0][0], r[1][0], r[2][0], r[3][0], r[3][1]])
    sum_dyz = stack_rows([r[0][1], r[1][1], r[2][1], r[3][2], r[3][3]])
    inv_counts = counts_column()
    mean_e = group_sum(sum_dy * gain) * inv_counts
    mean_ez = group_sum(sum_dyz * gain) * inv_counts
    on_dy = rstd * gain
    on_zhat = rstd * mean_ez
    on_z = -on_zhat * rstd
    flat = -rstd * mean_e - on_zhat * neg

    def second(level, cell, row, width, carry):
        dz = (
            da[pl.ds(cell, TILE), :] * rows(level, on_dy)
            + z[pl.ds(cell, TILE), :] * rows(level, on_z)
            + rows(level, flat)
        )
        write_shifted(buf, row, width, dz, C, True)
        return carry

    each_tile(second, jnp.int32(0))
    return jnp.sum(sum_dyz, axis=0, keepdims=True), jnp.sum(sum_dy, axis=0, keepdims=True)


def center(buf, cells, row, lanes):
    return buf[row : row + cells, lanes : 2 * lanes]


def shape(dims, dtype):
    return jax.ShapeDtypeStruct(dims, dtype)


def pack(vec):
    high = vec.astype(bf16).astype(f32)
    middle = (vec - high).astype(bf16).astype(f32)
    low = vec - high - middle
    return jnp.concatenate([high, middle, low, jnp.zeros_like(vec)], axis=0).astype(bf16)


def unpack(block):
    parts = block.astype(f32)
    return parts[0:8] + parts[8:16] + parts[16:24]


def bit_of(place, order, step):
    return jnp.where(place[1] == 0, place[0] >> order[0][step], place[0] >> order[1][step]) & 1


def split_store(bit, tap, grad, keep, send):
    half = C // 2
    low, high = grad[:half], grad[half:]
    keep[tap * half : (tap + 1) * half, :] = jnp.where(bit == 1, high, low).astype(bf16)
    send[tap * half : (tap + 1) * half, :] = jnp.where(bit == 1, low, high).astype(bf16)


def halve_kernel(taps, rows, order, step, place, keep, got, vec, keep_out, send_out, vec_out):
    bit = bit_of(place, order, step)
    half = rows // 2

    def one(t, _):
        for out, side in ((keep_out, bit), (send_out, 1 - bit)):
            at = pl.ds(pl.multiple_of(t * rows + side * half, half), half)
            to = pl.ds(pl.multiple_of(t * half, half), half)
            out[to, :] = (keep[at, :].astype(f32) + got[at, :].astype(f32)).astype(bf16)
        return 0

    lax.fori_loop(0, taps, one, 0)
    total = vec[...] + unpack(got[taps * rows :, :])
    vec_out[...] = total
    send_out[taps * half :, :] = pack(total)


def add_kernel(taps, rows, keep, got, vec, sum_out, vec_out):
    def one(t, _):
        at = pl.ds(pl.multiple_of(t * rows, rows), rows)
        sum_out[at, :] = (keep[at, :].astype(f32) + got[at, :].astype(f32)).astype(bf16)
        return 0

    lax.fori_loop(0, taps, one, 0)
    total = vec[...] + unpack(got[taps * rows :, :])
    vec_out[...] = total
    sum_out[taps * rows :, :] = pack(total)


def join_kernel(taps, rows, order, step, place, own, got, out):
    bit = bit_of(place, order, step)

    def one(t, _):
        at = pl.ds(pl.multiple_of(t * rows, rows), rows)
        out[pl.ds(pl.multiple_of((2 * t + bit) * rows, rows), rows), :] = own[at, :]
        out[pl.ds(pl.multiple_of((2 * t + 1 - bit) * rows, rows), rows), :] = got[at, :]
        return 0

    lax.fori_loop(0, taps, one, 0)


def final_kernel(layer, order, first, extra, *refs):
    if first:
        place, own, got, vec, out, rest, wide, sems = refs
    else:
        place, own, got, _, out, wide, sems = refs
    bit = bit_of(place, order, 0)
    half = C // 2
    copies = []
    for t in range(9):
        wide[pl.ds(pl.multiple_of(t * C + bit * half, half), half), :] = own[t * half : (t + 1) * half, :].astype(f32)
        wide[pl.ds(pl.multiple_of(t * C + (1 - bit) * half, half), half), :] = got[t * half : (t + 1) * half, :].astype(f32)
        copy = pltpu.make_async_copy(
            wide.at[t * C : (t + 1) * C], out.at[(layer * 9 + t) * C : (layer * 9 + t + 1) * C], sems.at[t]
        )
        copy.start()
        copies.append(copy)
    if first:
        for t in range(extra):
            rest[pl.ds(pl.multiple_of(t * C + bit * half, half), half), :] = own[(9 + t) * half : (10 + t) * half, :]
            rest[pl.ds(pl.multiple_of(t * C + (1 - bit) * half, half), half), :] = got[(9 + t) * half : (10 + t) * half, :]
        rest[extra * C :, :] = pack(vec[...])
    for copy in copies:
        copy.wait()


def heads_kernel(own, got, vec, dhead_out, vec_out):
    for i in range(3):
        at = slice(i * C, (i + 1) * C)
        turned = (own[at, :].astype(f32) + got[at, :].astype(f32)).T
        for j in range(3):
            dhead_out[i, j] = turned[j * HEAD : (j + 1) * HEAD, :]
    vec_out[...] = vec[...] + unpack(got[3 * C :, :])


def features_kernel(place, keep, got, var, out):
    half = C // 2
    inverse = lax.rsqrt(jnp.where(place[1] == 0, var[:, :half], var[:, half:]) + EPS)

    def scaled(cell, cells):
        return (keep[pl.ds(cell, cells), :].astype(f32) + got[pl.ds(cell, cells), :].astype(f32)) * inverse

    def one(t, _):
        at = pl.multiple_of(t * TILE, TILE)
        out[pl.ds(at, TILE), :] = scaled(at, TILE).astype(bf16)
        return 0

    lax.fori_loop(0, 1344 // TILE, one, 0)
    tail = scaled(1344, TILE)
    out[1344:PIX, :] = jnp.concatenate([tail[16:24], tail[32:40], tail[26:30]], axis=0).astype(bf16)


def gradients_out(bit, turned, buf, keep, send):
    for i in range(3):
        grad = kernel_grad(turned, buf, i)
        for j in range(3):
            split_store(bit, i * 3 + j, grad[:, j * C : (j + 1) * C], keep, send)


def vector_rows(rows):
    row = lax.broadcasted_iota(jnp.int32, (8, C), 0)
    out = jnp.zeros((8, C), f32)
    for at, value in enumerate(rows):
        out = jnp.where(row == at, value, out)
    return out


def spread_tail(tile, scratch):
    scratch[...] = jnp.zeros(scratch.shape, f32)
    scratch[16:24, :] = tile[0:8]
    scratch[32:40, :] = tile[8:16]
    scratch[26:30, :] = tile[16:20]


def first_kernel(
    order, place, scale, own, other, bn_mean, bn_var, w_hbm, gains, shifts, head, head_bias, cls, reg, pos,
    z_hbm, a_hbm, stats_out, da_out, keep_out, send_out, vec_out,
    w, buf, zs, acts, hw, hg, hbuf, u, turned, tail, sems,
):
    loads = [pltpu.make_async_copy(w_hbm.at[l], w.at[l], sems.at[l]) for l in range(LAYERS)]
    for load in loads:
        load.start()
    saves = []
    half = C // 2
    tower = place[1]
    clear_gaps(buf)
    clear_gaps(hbuf)
    inverse = lax.rsqrt(bn_var[...] + EPS)
    mean0 = bn_mean[...]

    def halves(rows):
        left = jnp.where(tower == 0, own[rows, :].astype(f32), other[rows, :].astype(f32))
        right = jnp.where(tower == 0, other[rows, :].astype(f32), own[rows, :].astype(f32))
        return (jnp.concatenate([left, right], axis=1) - mean0) * inverse

    def base(level, cell, row, width, carry):
        if level < 3:
            tile = halves(pl.ds(cell, TILE))
        else:
            spread_tail(halves(slice(1344, PIX)), tail)
            tile = tail[...]
        write_shifted(buf, row, width, tile, C, False)
        return carry

    each_tile(base, jnp.int32(0))
    stats = None
    for l in range(LAYERS):
        if l < LAYERS - 1:
            for cell, cells, row, width in PARTS:
                acts[l, cell : cell + cells, :] = center(buf, cells, row, C)
            saves.append(pltpu.make_async_copy(acts.at[l], a_hbm.at[l], sems.at[LAYERS + l]))
            saves[-1].start()
        else:
            for cell, cells, row, width in PARTS:
                turned[:, cell : cell + cells] = center(buf, cells, row, C).T
        loads[l].wait()
        z = zs.at[l]
        conv_into(z, buf, w[l], C)
        if l < LAYERS - 1:
            saves.append(pltpu.make_async_copy(z, z_hbm.at[l], sems.at[2 * LAYERS + l]))
            saves[-1].start()
        mean, rstd = norm_stats(z)
        if l < LAYERS - 1:
            stats_out[l, 0:8, :] = mean
            stats_out[l, 8:16, :] = rstd
        forward_act(z, mean, rstd, gains[l : l + 1], shifts[l : l + 1], buf)

    box = reg[...].astype(f32) * pos[...].astype(f32)
    is_class = tower == 0
    rows = jnp.concatenate(
        [
            jnp.where(is_class, cls[...].astype(f32), 0.0),
            jnp.where(is_class, 0.0, jnp.concatenate([box, jnp.zeros((3, PIX), f32)], axis=0)),
            jnp.zeros((LANES - CLASSES - 8, PIX), f32),
        ],
        axis=0,
    )
    rows = jnp.concatenate([rows, jnp.zeros((LANES, CELLS - PIX), f32)], axis=1)
    hg[...] = rows.T
    spread_tail(jnp.concatenate([hg[1344:PIX, :]] * 2, axis=1), tail)
    hg[1344:CELLS, :] = tail[:, 0:LANES]

    hw[...] = jnp.zeros(hw.shape, bf16)
    for i in range(3):
        three = jnp.concatenate([head[i, j].astype(f32) for j in range(3)] + [jnp.zeros((1, C), f32)], axis=0)
        hw[i * C : (i + 1) * C, :] = three.astype(bf16)

    lane = lax.broadcasted_iota(jnp.int32, (TILE, LANES), 1)
    row = lax.broadcasted_iota(jnp.int32, (TILE, LANES), 0)
    third = ((row >= 16) & (row < 24)) | ((row >= 32) & (row < 40))
    fourth = (row >= 26) & (row < 30)
    hvec = jnp.zeros((1, LANES), f32)
    u[...] = jnp.zeros(u.shape, f32)

    @pl.when(tower == 1)
    def _():
        for cell, cells, first, width in PARTS:
            for at in range(0, cells, 256):
                size = min(256, cells - at)
                total = None
                for i in range(3):
                    from_row = first + at + (i - 1) * width
                    for j in range(3):
                        kernel = jnp.concatenate([head[i, j], jnp.zeros((LANES - HEAD, C), bf16)], axis=0)
                        term = lax.dot_general(
                            buf[from_row : from_row + size, j * C : (j + 1) * C],
                            kernel,
                            (((1,), (1,)), ((), ())),
                            preferred_element_type=f32,
                        )
                        total = term if total is None else total + term
                u[cell + at : cell + at + size, :] = total
        bias = jnp.concatenate([head_bias[...], jnp.zeros((1, LANES - HEAD), f32)], axis=1)
        dist_lane = (lane >= CLASSES) & (lane < CLASSES + 4)

        def boxes(level, cell, row, width, carry):
            raw = u[pl.ds(cell, TILE), :] + bias
            g = hg[pl.ds(cell, TILE), :]
            if level < 3:
                ls = scale[level]
                use = dist_lane
            else:
                ls = jnp.where(third, scale[3], scale[4])
                use = dist_lane & (third | fourth)
            weighted = jnp.where(use, g * jnp.exp(ls * raw), 0.0)
            hg[pl.ds(cell, TILE), :] = jnp.where(dist_lane, weighted * ls, g)
            u[pl.ds(cell, TILE), :] = weighted * raw
            return carry

        each_tile(boxes, jnp.int32(0))

    def scale_sums(level, cell, row, width, carry):
        term = u[pl.ds(cell, TILE), :]
        if level < 3:
            return carry + fold(term)
        return (fold(jnp.where(third, term, 0.0)), fold(jnp.where(fourth, term, 0.0)))

    r = each_tile(scale_sums, jnp.zeros((8, LANES), f32))
    scale_rows = [jnp.sum(v, axis=0, keepdims=True) for v in (r[0], r[1], r[2], r[3][0], r[3][1])]

    def head_rows(level, cell, row, width, carry):
        tile = hg[pl.ds(cell, TILE), :].astype(bf16).astype(f32)
        at = lax.broadcasted_iota(jnp.int32, tile.shape, 0) & (width - 1)
        after = jnp.where(at == 0, 0.0, pltpu.roll(tile, 1, 0))
        before = jnp.where(at == width - 1, 0.0, pltpu.roll(tile, TILE - 1, 0))
        middle = pltpu.roll(tile, HEAD, 1)
        after = pltpu.roll(after, 2 * HEAD - LANES, 1)
        rows = pl.ds(row, TILE)
        hbuf[rows, 0:LANES] = jnp.where(lane < HEAD, before, middle).astype(bf16)
        hbuf[rows, LANES : 2 * LANES] = jnp.where(lane < 2 * HEAD - LANES, middle, after).astype(bf16)
        return carry + fold(tile)

    r = each_tile(head_rows, jnp.zeros((8, LANES), f32))
    bias_row = jnp.sum(r[0] + r[1] + r[2] + r[3], axis=0, keepdims=True)

    bit = bit_of(place, order, 0)
    a4t = jnp.concatenate([center(buf, n, r, C).T for _, n, r, _ in PARTS], axis=1)
    for i in range(3):
        split_store(bit, 9 + i, kernel_grad(a4t, hbuf, i), keep_out, send_out)
    for cell, cells, first, width in PARTS:
        for at in range(0, cells, 256):
            size = min(256, cells - at)
            left = jnp.concatenate([hbuf[first + at - d * width : first + at - d * width + size, :] for d in (-1, 0, 1)], axis=1)
            da_out[cell + at : cell + at + size, :] = jnp.dot(left, hw[...], preferred_element_type=f32)

    l = LAYERS - 1
    dgain, dshift = backward_norm(da_out, zs.at[l], mean, rstd, gains[l : l + 1], shifts[l : l + 1], buf)
    wide = lambda v: jnp.concatenate([v, jnp.zeros_like(v)], axis=1)
    vec = vector_rows([dgain, dshift, wide(bias_row)] + [wide(v) for v in scale_rows])
    vec_out[...] = vec
    send_out[12 * half :, :] = pack(vec)
    gradients_out(bit, turned, buf, keep_out, send_out)
    conv_back_into(da_out, buf, lambda tap: w[l, tap * C : (tap + 1) * C, :], C)
    for save in saves:
        save.wait()


def middle_kernel(
    l, order, place, da_hbm, z_hbm, a_hbm, stats, gains, shifts, w_hbm, *refs,
):
    if l:
        da_out, keep_out, send_out, vec_out, z, a, w, buf, turned, sems = refs
        da = da_out
    else:
        keep_half, send_half, keep_out, send_out, vec_out, z, a, w, buf, turned, da, sems = refs
    loads = [
        pltpu.make_async_copy(src, dst, sems.at[k])
        for k, (src, dst) in enumerate(((da_hbm, da), (z_hbm.at[l], z), (a_hbm.at[l], a), (w_hbm.at[l], w)))
    ]
    for load in loads:
        load.start()
    half = C // 2
    bit = bit_of(place, order, 0)
    clear_gaps(buf)
    loads[0].wait()
    loads[1].wait()
    dgain, dshift = backward_norm(
        da, z, stats[l, 0:8, :], stats[l, 8:16, :], gains[l : l + 1], shifts[l : l + 1], buf
    )
    vec = vector_rows([dgain, dshift])
    vec_out[...] = vec
    send_out[9 * half :, :] = pack(vec)
    loads[2].wait()
    turned[...] = a[...].T
    gradients_out(bit, turned, buf, keep_out, send_out)
    loads[3].wait()
    conv_back_into(da, buf, lambda tap: w[tap * C : (tap + 1) * C, :], C)
    if not l:
        mine = place[1]
        keep_half[...] = jnp.where(mine == 0, da[:, :half], da[:, half:])
        send_half[...] = jnp.where(mine == 0, da[:, half:], da[:, :half]).astype(bf16)


def run_first(order, place, scale, own, other, mean, var, w, gains, shifts, head, bias, cls, reg, pos):
    half = C // 2
    return pl.pallas_call(
        functools.partial(first_kernel, order),
        out_shape=[
            shape((LAYERS - 1, CELLS, C), f32),
            shape((LAYERS - 1, CELLS, C), bf16),
            shape((LAYERS - 1, 16, C), f32),
            shape((CELLS, C), f32),
            shape((12 * half, C), bf16),
            shape((12 * half + VEC, C), bf16),
            shape((8, C), f32),
        ],
        in_specs=[SMEM, SMEM, VMEM, VMEM, VMEM, VMEM, ANY] + [VMEM] * 7,
        out_specs=[ANY, ANY] + [VMEM] * 5,
        scratch_shapes=[
            pltpu.VMEM((LAYERS, 9 * C, C), bf16),
            pltpu.VMEM((PADDED, 3 * C), bf16),
            pltpu.VMEM((LAYERS, CELLS, C), f32),
            pltpu.VMEM((LAYERS - 1, CELLS, C), bf16),
            pltpu.VMEM((3 * C, C), bf16),
            pltpu.VMEM((CELLS, LANES), f32),
            pltpu.VMEM((PADDED, 2 * LANES), bf16),
            pltpu.VMEM((CELLS, LANES), f32),
            pltpu.VMEM((C, CELLS), bf16),
            pltpu.VMEM((TILE, C), f32),
            pltpu.SemaphoreType.DMA((3 * LAYERS,)),
        ],
        compiler_params=params(),
        name="forward_and_heads",
    )(place, scale, own, other, mean, var, w, gains, shifts, head, bias, cls, reg, pos)


def run_middle(l, order, place, da, z, a, stats, gains, shifts, w):
    half = C // 2
    outs = [shape((CELLS, C), f32)] if l else [shape((CELLS, half), f32), shape((CELLS, half), bf16)]
    outs += [shape((9 * half, C), bf16), shape((9 * half + VEC, C), bf16), shape((8, C), f32)]
    scratch = [
        pltpu.VMEM((CELLS, C), f32),
        pltpu.VMEM((CELLS, C), bf16),
        pltpu.VMEM((9 * C, C), bf16),
        pltpu.VMEM((PADDED, 3 * C), bf16),
        pltpu.VMEM((C, CELLS), bf16),
    ]
    if not l:
        scratch.append(pltpu.VMEM((CELLS, C), f32))
    return pl.pallas_call(
        functools.partial(middle_kernel, l, order),
        out_shape=outs,
        in_specs=[SMEM, ANY, ANY, ANY, VMEM, VMEM, VMEM, ANY],
        out_specs=[VMEM] * len(outs),
        scratch_shapes=scratch + [pltpu.SemaphoreType.DMA((4,))],
        compiler_params=params(40),
        name=f"layer_gradients_{l}",
    )(place, da, z, a, stats, gains, shifts, w)


def small_call(kernel, outs, name, ins, **more):
    return pl.pallas_call(
        kernel,
        out_shape=outs,
        in_specs=[SMEM] * more.pop("scalars", 0) + [VMEM] * more.pop("blocks"),
        out_specs=[VMEM] * len(outs),
        compiler_params=params(16),
        name=name,
    )(*ins)


class Sum:
    def __init__(self, layer, taps, order, bits, place, keep, send, vec):
        self.layer, self.taps, self.order, self.bits, self.place = layer, taps, order, bits, place
        self.keep, self.vec = keep, vec
        self.splits = min(SPLITS, bits)
        self.rows = C // 2
        self.send = send
        self.step = 0

    def partner(self, value, step):
        pairs = []
        for d in range(1 << self.bits):
            for t in range(2):
                pairs.append((2 * d + t, 2 * (d ^ (1 << self.order[t][step])) + t))
        return lax.ppermute(value, ("dp", "tower"), pairs)

    def reduce(self):
        taps, name = self.taps, f"sum_{self.layer}"
        got = self.partner(self.send, 0)
        for step in range(1, self.bits + 1):
            rows = self.rows
            vec = shape((8, C), f32)
            if step < self.splits:
                half = rows // 2
                self.keep, self.send, self.vec = small_call(
                    functools.partial(halve_kernel, taps, rows, self.order, step),
                    [shape((taps * half, C), bf16), shape((taps * half + VEC, C), bf16), vec],
                    name, (self.place, self.keep, got, self.vec), scalars=1, blocks=3,
                )
                self.rows = half
            else:
                self.send, self.vec = small_call(
                    functools.partial(add_kernel, taps, rows),
                    [shape((taps * rows + VEC, C), bf16), vec],
                    name, (self.keep, got, self.vec), blocks=3,
                )
                self.keep = self.send
            if step < self.bits:
                got = self.partner(self.send, step)
        self.own = self.send

    def gather(self):
        for step in range(self.splits - 1, 0, -1):
            got = self.partner(self.own, step)
            (self.own,) = small_call(
                functools.partial(join_kernel, self.taps, self.rows, self.order, step),
                [shape((self.taps * 2 * self.rows, C), bf16)],
                f"gather_{self.layer}", (self.place, self.own, got), scalars=1, blocks=2,
            )
            self.rows *= 2
        self.got = self.partner(self.own, 0)

    def finish(self, out):
        first = out is None
        extra = self.taps - 9
        half = C // 2
        outs = [shape((LAYERS * 9 * C, C), f32)]
        ins = [self.place, self.own, self.got]
        if first:
            outs.append(shape((extra * C + VEC, C), bf16))
            ins.append(self.vec)
        else:
            ins.append(out)
        return pl.pallas_call(
            functools.partial(final_kernel, self.layer, self.order, first, extra),
            out_shape=outs,
            in_specs=[SMEM, VMEM, VMEM, VMEM if first else ANY],
            out_specs=[ANY, VMEM] if first else [ANY],
            scratch_shapes=[pltpu.VMEM((9 * C, C), f32), pltpu.SemaphoreType.DMA((9,))],
            input_output_aliases={} if first else {3: 0},
            compiler_params=params(24),
            name=f"write_{self.layer}",
        )(*ins)


def orders(bits):
    if bits == 4:
        p = ((0, 2, 1, 3), (1, 0, 2, 3))
        q = ((1, 0, 2, 3), (2, 1, 0, 3))
        r = ((2, 1, 0, 3), (0, 2, 1, 3))
        return (q, p, r, r)
    line = tuple(range(bits))
    return (((line, line[1:] + line[:1]),) * LAYERS)


def body(
    features, bn_mean, bn_var, tower_weight, norm_gain, norm_bias, head_weight, head_bias, level_scale,
    cls_cot, reg_cot, positive, *, dp,
):
    bits = dp.bit_length() - 1
    assert dp == 1 << bits and bits >= 1
    order = orders(bits)
    place = jnp.stack([lax.axis_index("dp"), lax.axis_index("tower")])
    own = features[0]
    other = lax.ppermute(own, "tower", [(0, 1), (1, 0)])
    w = tower_weight[0].reshape(LAYERS, 9 * C, C)
    gains, shifts = norm_gain[0], norm_bias[0]
    mean, var = bn_mean[None], bn_var[None]
    z, a, stats, da, keep, send, vec = run_first(
        order[3], place, level_scale, own, other, mean, var, w, gains, shifts,
        jnp.swapaxes(head_weight, 2, 3), head_bias[None],
        jnp.swapaxes(cls_cot[0], 0, 1), jnp.swapaxes(reg_cot[0], 0, 1), positive,
    )
    sums = [None] * LAYERS
    sums[3] = Sum(3, 12, order[3], bits, place, keep, send, vec)
    for l in (2, 1):
        da, keep, send, vec = run_middle(l, order[l], place, da, z, a, stats, gains, shifts, w)
        sums[l] = Sum(l, 9, order[l], bits, place, keep, send, vec)
    keep_half, send_half, keep, send, vec = run_middle(0, order[0], place, da, z, a, stats, gains, shifts, w)
    sums[0] = Sum(0, 9, order[0], bits, place, keep, send, vec)
    got_half = lax.ppermute(send_half, "tower", [(0, 1), (1, 0)])
    (feature_grad,) = small_call(
        features_kernel, [shape((PIX, C // 2), bf16)], "feature_gradient",
        (place, keep_half, got_half, var), scalars=1, blocks=3,
    )
    for one in sums[::-1]:
        one.reduce()
        one.gather()
    out, heads = sums[3].finish(None)
    got_heads = lax.ppermute(heads, "tower", [(0, 1), (1, 0)])
    dhead, hvec = small_call(
        heads_kernel, [shape((3, 3, HEAD, C), f32), shape((8, C), f32)], "head_gradients",
        (heads, got_heads, sums[3].vec), blocks=3,
    )
    for l in (2, 1, 0):
        (out,) = sums[l].finish(out)
    vecs = jnp.stack([s.vec for s in sums])
    return (
        feature_grad[None],
        out.reshape(1, LAYERS, 3, 3, C, C),
        vecs[None, :, 0],
        vecs[None, :, 1],
        jnp.swapaxes(dhead, 2, 3),
        hvec[2, :HEAD],
        jnp.sum(hvec[3:8], axis=1),
    )


def solution(mesh):
    return jax.shard_map(
        functools.partial(body, dp=mesh.shape["dp"]),
        mesh=mesh,
        in_specs=(
            P("dp", None, "tower"),
            P(),
            P(),
            P("tower", None, None, None, None, None),
            P("tower", None, None),
            P("tower", None, None),
            P(),
            P(),
            P(),
            P("dp", None, None),
            P("dp", None, None),
            P("dp", None),
        ),
        out_specs=(
            P("dp", None, "tower"),
            P("tower", None, None, None, None, None),
            P("tower", None, None),
            P("tower", None, None),
            P(),
            P(),
            P(),
        ),
        check_vma=False,
    )
```

```python
import functools

import jax
import jax.numpy as jnp
from jax import lax
from jax.experimental import pallas as pl
from jax.experimental.pallas import tpu as pltpu
from jax.sharding import PartitionSpec as P

C = 256
GROUP = 8
CLASSES = 80
HEAD = 85
LANES = 128
LAYERS = 4
CELLS = 1408
PIX = 1364
COUNTS = (1024, 256, 64, 16, 4)
PARTS = ((0, 1024, 64, 64), (1024, 256, 1152, 32), (1280, 128, 1440, 16))
PADDED = 1584
GAPS = ((0, 64), (1088, 64), (1408, 32), (1568, 16))
TILE = 64
BLOCKS = tuple((256 * i, 256, 64 + 256 * i, 64, 0) for i in range(4)) + ((1024, 256, 1152, 32, 1), (1280, 128, 1440, 16, 2))
EPS = 1e-05
f32 = jnp.float32
bf16 = jnp.bfloat16
VMEM = pl.BlockSpec(memory_space=pltpu.VMEM)
SMEM = pl.BlockSpec(memory_space=pltpu.SMEM)
HBM = pl.BlockSpec(memory_space=pltpu.HBM)


VEC = 32
FEATURES, HEADS = 8, 9
COST = 300000000
COSTS = {
    "add_3_3": 3000000000,
    "join_0_5": 2000000000,
    "add_3_4": 3000000000,
    "halve_3_2": 1000000000,
    "join_1_6": 300000000,
    "add_2_4": 300000000,
    "feature_gradient": 3000000000,
    "join_2_5": 1000000000,
    "write_1_got": 1000000,
    "add_1_4": 2000000000,
    "join_2_6": 1000000,
    "write_3_got": 300000000,
    "layer_gradients_1": 1000000,
    "write_0_own": 3000000000,
    "write_2_own": 1500000000,
    "halve_2_1": 1000000,
    "halve_1_2": 100000000,
    "add_1_3": 100000000,
    "head_gradients": 1000000,
    "halve_0_2": 1000000,
    "add_0_3": 100000000,
    "write_1_own": 2000000000,
    "layer_gradients_2": 1000000,
    "join_3_6": 2000000000,
    "join_3_5": 1000000000,
    "halve_3_1": 5000000000,
    "layer_gradients_0": 100000000,
}
FIRST_MIB = 32
MIDDLE_MIB = 24
SPLITS = 3


def params(mib=56):
    return pltpu.CompilerParams(vmem_limit_bytes=mib << 20)


def tail_masks():
    row = lax.broadcasted_iota(jnp.int32, (TILE, C), 0)
    third = ((row >= 16) & (row < 24)) | ((row >= 32) & (row < 40))
    fourth = (row >= 26) & (row < 30)
    return third, fourth


def pick(third, fourth, vec):
    return jnp.where(third, vec[3:4], jnp.where(fourth, vec[4:5], 0.0))


def fold(tile):
    return jnp.sum(tile.reshape(TILE // 8, 8, tile.shape[1]), axis=0)


def group_sum(vec):
    lane = lax.broadcasted_iota(jnp.int32, vec.shape, 1)
    for step in (1, 2, 4):
        up = pltpu.roll(vec, vec.shape[1] - step, 1)
        down = pltpu.roll(vec, step, 1)
        vec = vec + jnp.where((lane & step) == 0, up, down)
    return vec


def counts_column():
    row = lax.broadcasted_iota(jnp.int32, (8, C), 0)
    out = jnp.full((8, C), 1.0, f32)
    for level, cells in enumerate(COUNTS):
        out = jnp.where(row == level, 1.0 / (cells * GROUP), out)
    return out


def stack_rows(rows):
    row = lax.broadcasted_iota(jnp.int32, (8, rows[0].shape[1]), 0)
    out = jnp.zeros((8, rows[0].shape[1]), f32)
    for place, value in enumerate(rows):
        out = jnp.where(row == place, jnp.sum(value, axis=0, keepdims=True), out)
    return out


def each_tile(step, init):
    results = []
    for level, (tiles, cell, row, width) in enumerate(((16, 0, 64, 64), (4, 1024, 1152, 32), (1, 1280, 1440, 16))):
        carry = init

        def run(i, carry, level=level, cell=cell, row=row, width=width):
            at = pl.multiple_of(i * TILE, TILE)
            return step(level, cell + at, row + at, width, carry)

        if tiles == 1:
            carry = step(level, cell, row, width, carry)
        else:
            carry = lax.fori_loop(0, tiles, run, carry, unroll=2)
        results.append(carry)
    results.append(step(3, 1344, 1504, 16, init))
    return results


def write_shifted(buf, row, width, tile, lanes, flip):
    at = lax.broadcasted_iota(jnp.int32, tile.shape, 0) & (width - 1)
    before = jnp.where(at == 0, 0.0, pltpu.roll(tile, 1, 0))
    after = jnp.where(at == width - 1, 0.0, pltpu.roll(tile, TILE - 1, 0))
    if flip:
        before, after = after, before
    rows = pl.ds(row, TILE)
    buf[rows, 0:lanes] = before.astype(bf16)
    buf[rows, lanes : 2 * lanes] = tile.astype(bf16)
    buf[rows, 2 * lanes : 3 * lanes] = after.astype(bf16)


def clear_gaps(buf):
    for row, rows in GAPS:
        buf[row : row + rows, :] = jnp.zeros((rows, buf.shape[1]), bf16)


def conv_block(block, buf, weight):
    _, cells, row, width, _ = block
    left = jnp.concatenate([buf[row + d * width : row + d * width + cells, :] for d in (-1, 0, 1)], axis=1)
    return jnp.dot(left, weight, preferred_element_type=f32)


def conv_back_block(block, buf, weight):
    _, cells, row, width, _ = block
    total = None
    for i in range(3):
        at = row - (i - 1) * width
        for j in range(3):
            term = lax.dot_general(
                buf[at : at + cells, j * C : (j + 1) * C],
                weight(i * 3 + j),
                (((1,), (1,)), ((), ())),
                preferred_element_type=f32,
            )
            total = term if total is None else total + term
    return total


def kernel_grad(turned, buf, i):
    total = None
    for cell, cells, row, width in PARTS:
        at = row - (i - 1) * width
        term = jnp.dot(turned[:, cell : cell + cells], buf[at : at + cells, :], preferred_element_type=f32)
        total = term if total is None else total + term
    return total


def tiles_of(block):
    cell, cells, row, width, level = block
    return [(level if at == 0 or level < 2 else 3, cell + at, row + at, width, at) for at in range(0, cells, TILE)]


def pipelined(produce, consume):
    produce(BLOCKS[0])
    for i, block in enumerate(BLOCKS):
        if i + 1 < len(BLOCKS):
            produce(BLOCKS[i + 1])
        consume(block)


class Stats:
    def __init__(self):
        self.center = None
        self.sums = [jnp.zeros((8, C), f32), jnp.zeros((8, C), f32)]
        self.rows = []

    def own(self, tile, cells, mask=None):
        kept = tile if mask is None else jnp.where(mask, tile, 0.0)
        mean = jnp.sum(kept, axis=0, keepdims=True) * (1.0 / cells)
        d = tile - mean
        d = d if mask is None else jnp.where(mask, d, 0.0)
        self.rows.append((mean, jnp.sum(d * d, axis=0, keepdims=True)))

    def add(self, block, z):
        level = block[4]
        if level == 0:
            if self.center is None:
                self.center = jnp.sum(z, axis=0, keepdims=True) * (1.0 / z.shape[0])
            d = z - self.center
            wide = lambda v: jnp.sum(v.reshape(z.shape[0] // 8, 8, C), axis=0)
            self.sums = [self.sums[0] + wide(d), self.sums[1] + wide(d * d)]
        elif level == 1:
            self.own(z, COUNTS[1])
        else:
            third, fourth = tail_masks()
            self.own(z[:TILE], COUNTS[2])
            self.own(z[TILE:], COUNTS[3], third)
            self.own(z[TILE:], COUNTS[4], fourth)

    def finish(self):
        first, second = (jnp.sum(v, axis=0, keepdims=True) for v in self.sums)
        shift = first * (1.0 / COUNTS[0])
        rows = [(self.center + shift, second - first * shift)] + self.rows
        means = stack_rows([r[0] for r in rows])
        squares = stack_rows([r[1] for r in rows])
        inv_counts = counts_column()
        mean = group_sum(means) * (1.0 / GROUP)
        d = means - mean
        var = group_sum(squares * inv_counts + d * d * (1.0 / GROUP))
        return mean, lax.rsqrt(var + EPS)


def level_rows(level, vec, masks):
    if level < 3:
        return vec[level : level + 1]
    return pick(*masks, vec)


def act_tiles(block, z, scale, offset, buf, keep=None):
    masks = tail_masks()
    for level, cell, row, width, _ in tiles_of(block):
        y = z[cell : cell + TILE, :] * level_rows(level, scale, masks) + level_rows(level, offset, masks)
        a = y * (0.5 * jnp.tanh(0.5 * y) + 0.5)
        if level == 3:
            a = jnp.where(masks[0] | masks[1], a, 0.0)
        write_shifted(buf, row, width, a, C, False)
        if keep is not None:
            keep[cell : cell + TILE, :] = a.astype(bf16)


class Upward:
    def __init__(self, dy_out, z, mean, rstd, gain, shift):
        self.dy_out, self.z, self.rstd, self.neg, self.gain, self.shift = dy_out, z, rstd, -mean * rstd, gain, shift
        self.sums = [[jnp.zeros((8, C), f32), jnp.zeros((8, C), f32)] for _ in COUNTS]

    def add(self, block, da):
        masks = tail_masks()
        for level, cell, _, _, at in tiles_of(block):
            zhat = self.z[cell : cell + TILE, :] * level_rows(level, self.rstd, masks) + level_rows(level, self.neg, masks)
            y = zhat * self.gain + self.shift
            s = 0.5 * jnp.tanh(0.5 * y) + 0.5
            dy = da[at : at + TILE] * (s * (1.0 + y * (1.0 - s)))
            self.dy_out[cell : cell + TILE, :] = dy
            dyz = dy * zhat
            if level < 3:
                parts = [(level, dy, dyz)]
            else:
                parts = [(3 + k, jnp.where(m, dy, 0.0), jnp.where(m, dyz, 0.0)) for k, m in enumerate(masks)]
            for to, one, two in parts:
                self.sums[to] = [self.sums[to][0] + fold(one), self.sums[to][1] + fold(two)]

    def finish(self, sums_out):
        sums_out[0:8, :] = stack_rows([v[0] for v in self.sums])
        sums_out[8:16, :] = stack_rows([v[1] for v in self.sums])


def norm_back(dy, z, mean, rstd, gain, sums, buf):
    sum_dy, sum_dyz = sums[0:8, :], sums[8:16, :]
    inv_counts = counts_column()
    mean_e = group_sum(sum_dy * gain) * inv_counts
    mean_ez = group_sum(sum_dyz * gain) * inv_counts
    on_dy = rstd * gain
    on_zhat = rstd * mean_ez
    on_z = -on_zhat * rstd
    flat = on_zhat * mean * rstd - rstd * mean_e

    def produce(block):
        masks = tail_masks()
        for level, cell, row, width, _ in tiles_of(block):
            at = slice(cell, cell + TILE)
            dz = (
                dy[at, :] * level_rows(level, on_dy, masks)
                + z[at, :] * level_rows(level, on_z, masks)
                + level_rows(level, flat, masks)
            )
            write_shifted(buf, row, width, dz, C, True)

    return produce, [jnp.sum(v, axis=0, keepdims=True) for v in (sum_dyz, sum_dy)]


def center(buf, cells, row, lanes):
    return buf[row : row + cells, lanes : 2 * lanes]


def shape(dims, dtype):
    return jax.ShapeDtypeStruct(dims, dtype)


def pack(vec):
    high = vec.astype(bf16).astype(f32)
    middle = (vec - high).astype(bf16).astype(f32)
    low = vec - high - middle
    return jnp.concatenate([high, middle, low, jnp.zeros_like(vec)], axis=0).astype(bf16)


def unpack(block):
    parts = block.astype(f32)
    return parts[0:8] + parts[8:16] + parts[16:24]


def bit_of(order, step):
    dp = lax.axis_index("dp")
    return jnp.where(lax.axis_index("tower") == 0, dp >> order[0][step], dp >> order[1][step]) & 1


def call(kernel, token, ins, in_specs, outs, out_specs, name, scratch=(), mib=16, alias=None):
    n_in, n_out = len(ins), len(outs)

    def ordered(*refs):
        kernel(*refs[:n_in], *refs[n_in + 1 : n_in + 1 + n_out], *refs[n_in + n_out + 2 :])

    *results, token = pl.pallas_call(
        ordered,
        out_shape=list(outs) + [shape((8, LANES), f32)],
        in_specs=list(in_specs) + [HBM],
        out_specs=list(out_specs) + [HBM],
        scratch_shapes=list(scratch),
        input_output_aliases=alias or {},
        compiler_params=params(mib),
        cost_estimate=pl.CostEstimate(flops=COSTS.get(name, COST), bytes_accessed=1, transcendentals=0),
        name=name,
    )(*ins, token)
    return results, token


def split_store(bit, tap, grad, keep, send):
    half = C // 2
    low, high = grad[:half], grad[half:]
    keep[tap * half : (tap + 1) * half, :] = jnp.where(bit == 1, high, low).astype(bf16)
    send[tap * half : (tap + 1) * half, :] = jnp.where(bit == 1, low, high).astype(bf16)


def halve_kernel(taps, rows, order, step, keep, got, vec, keep_out, send_out, vec_out):
    bit = bit_of(order, step)
    half = rows // 2

    def one(t, _):
        for out, side in ((keep_out, bit), (send_out, 1 - bit)):
            at = pl.ds(pl.multiple_of(t * rows + side * half, half), half)
            to = pl.ds(pl.multiple_of(t * half, half), half)
            out[to, :] = (keep[at, :].astype(f32) + got[at, :].astype(f32)).astype(bf16)
        return 0

    lax.fori_loop(0, taps, one, 0)
    total = vec[...] + unpack(got[taps * rows :, :])
    vec_out[...] = total
    send_out[taps * half :, :] = pack(total)


def add_kernel(taps, rows, keep, got, vec, sum_out, vec_out):
    def one(t, _):
        at = pl.ds(pl.multiple_of(t * rows, rows), rows)
        sum_out[at, :] = (keep[at, :].astype(f32) + got[at, :].astype(f32)).astype(bf16)
        return 0

    lax.fori_loop(0, taps, one, 0)
    total = vec[...] + unpack(got[taps * rows :, :])
    vec_out[...] = total
    sum_out[taps * rows :, :] = pack(total)


def join_kernel(taps, rows, order, step, own, got, out):
    bit = bit_of(order, step)

    def one(t, _):
        at = pl.ds(pl.multiple_of(t * rows, rows), rows)
        out[pl.ds(pl.multiple_of((2 * t + bit) * rows, rows), rows), :] = own[at, :]
        out[pl.ds(pl.multiple_of((2 * t + 1 - bit) * rows, rows), rows), :] = got[at, :]
        return 0

    lax.fori_loop(0, taps, one, 0)


def write_half(layer, side, half_rows, out, wide, sems):
    half = C // 2
    copies = []
    for t in range(9):
        rows = slice(t * half, (t + 1) * half)
        wide[rows, :] = half_rows[rows, :].astype(f32)
        to = pl.multiple_of((layer * 9 + t) * C + side * half, half)
        copies.append(pltpu.make_async_copy(wide.at[rows], out.at[pl.ds(to, half)], sems.at[t]))
        copies[-1].start()
    return copies


def write_own_kernel(layer, order, own, *refs):
    out, wide, sems = refs[-3:]
    for copy in write_half(layer, bit_of(order, 0), own, out, wide, sems):
        copy.wait()


def write_got_kernel(layer, order, extra, got, *refs):
    bit = bit_of(order, 0)
    out, wide, sems = refs[-3 - (1 if extra else 2 if not layer else 0) :][:1] + refs[-2:]
    copies = write_half(layer, 1 - bit, got, out, wide, sems)
    half = C // 2
    if extra:
        own, vec, _, _, rest, _, _ = refs
        for t in range(extra):
            rest[pl.ds(pl.multiple_of(t * C + bit * half, half), half), :] = own[(9 + t) * half : (10 + t) * half, :]
            rest[pl.ds(pl.multiple_of(t * C + (1 - bit) * half, half), half), :] = got[(9 + t) * half : (10 + t) * half, :]
        rest[extra * C :, :] = pack(vec[...])
    elif not layer:
        *vecs, _, _, gains_out, shifts_out, _, _ = refs
        gains_out[...] = jnp.concatenate([v[0:1, :] for v in vecs], axis=0)
        shifts_out[...] = jnp.concatenate([v[1:2, :] for v in vecs], axis=0)
    for copy in copies:
        copy.wait()


def heads_kernel(own, got, vec, dhead_out, bias_out, scale_out):
    for i in range(3):
        at = slice(i * C, (i + 1) * C)
        turned = (own[at, :].astype(f32) + got[at, :].astype(f32)).T
        for j in range(3):
            dhead_out[i, j] = turned[j * HEAD : (j + 1) * HEAD, :]
    both = vec[...] + unpack(got[3 * C :, :])
    bias_out[...] = both[2:3, 0:HEAD]
    lane = lax.broadcasted_iota(jnp.int32, (8, LANES), 1)
    row = lax.broadcasted_iota(jnp.int32, (8, LANES), 0)
    sums = jnp.sum(both[:, 0:LANES], axis=1, keepdims=True)
    line = jnp.sum(jnp.where((row >= 3) & (lane == row - 3), sums, 0.0), axis=0, keepdims=True)
    scale_out[...] = line[:, 0 : len(COUNTS)]


def features_kernel(keep, got, var, out):
    half = C // 2
    inverse = lax.rsqrt(jnp.where(lax.axis_index("tower") == 0, var[:, :half], var[:, half:]) + EPS)

    def scaled(cell, cells):
        return (keep[pl.ds(cell, cells), :].astype(f32) + got[pl.ds(cell, cells), :].astype(f32)) * inverse

    def one(t, _):
        at = pl.multiple_of(t * TILE, TILE)
        out[pl.ds(at, TILE), :] = scaled(at, TILE).astype(bf16)
        return 0

    lax.fori_loop(0, 1344 // TILE, one, 0)
    tail = scaled(1344, TILE)
    out[1344:PIX, :] = jnp.concatenate([tail[16:24], tail[32:40], tail[26:30]], axis=0).astype(bf16)


def gradients_out(bit, turned, buf, keep, send):
    for i in range(3):
        grad = kernel_grad(turned, buf, i)
        for j in range(3):
            split_store(bit, i * 3 + j, grad[:, j * C : (j + 1) * C], keep, send)


def vector_rows(rows):
    row = lax.broadcasted_iota(jnp.int32, (8, C), 0)
    out = jnp.zeros((8, C), f32)
    for at, value in enumerate(rows):
        out = jnp.where(row == at, value, out)
    return out


def spread_tail(tile, scratch):
    scratch[...] = jnp.zeros(scratch.shape, f32)
    scratch[16:24, :] = tile[0:8]
    scratch[32:40, :] = tile[8:16]
    scratch[26:30, :] = tile[16:20]


def prepare_kernel(head, cls, reg, pos, hw, hg, tail):
    box = reg[...].astype(f32) * pos[...].astype(f32)
    is_class = lax.axis_index("tower") == 0
    rows = jnp.concatenate(
        [
            jnp.where(is_class, cls[...].astype(f32), 0.0),
            jnp.where(is_class, 0.0, jnp.concatenate([box, jnp.zeros((3, PIX), f32)], axis=0)),
            jnp.zeros((LANES - CLASSES - 8, PIX), f32),
        ],
        axis=0,
    )
    rows = jnp.concatenate([rows, jnp.zeros((LANES, CELLS - PIX), f32)], axis=1)
    hg[...] = rows.T
    spread_tail(jnp.concatenate([hg[1344:PIX, :]] * 2, axis=1), tail)
    hg[1344:CELLS, :] = tail[:, 0:LANES]
    for i in range(3):
        three = jnp.concatenate([head[i, j].astype(f32) for j in range(3)] + [jnp.zeros((1, C), f32)], axis=0)
        hw[i * C : (i + 1) * C, :] = three.astype(bf16)


def first_kernel(
    order, scale, own, other, bn_mean, bn_var, w_hbm, gains, shifts, head, head_bias, hw, hg_in,
    w, z_out, a_out, stats_out, dy_out, sums_out, keep_out, send_out, vec_out,
    buf, z_last, a_last, dy, sums, hg, hbuf, u, turned, tail, scale_sums, sems,
):
    loads = [pltpu.make_async_copy(w_hbm.at[l], w.at[l], sems.at[l]) for l in range(LAYERS)]
    for load in loads:
        load.start()
    half = C // 2
    tower = lax.axis_index("tower")
    clear_gaps(buf)
    clear_gaps(hbuf)
    inverse = lax.rsqrt(bn_var[...] + EPS)
    mean0 = bn_mean[...]

    def halves(rows):
        left = jnp.where(tower == 0, own[rows, :].astype(f32), other[rows, :].astype(f32))
        right = jnp.where(tower == 0, other[rows, :].astype(f32), own[rows, :].astype(f32))
        return (jnp.concatenate([left, right], axis=1) - mean0) * inverse

    def base(level, cell, row, width, carry):
        if level < 3:
            tile = halves(pl.ds(cell, TILE))
        else:
            spread_tail(halves(slice(1344, PIX)), tail)
            tile = tail[...]
        write_shifted(buf, row, width, tile, C, False)
        return carry

    each_tile(base, jnp.int32(0))
    for cell, cells, row, width in PARTS:
        a_out[0, cell : cell + cells, :] = center(buf, cells, row, C)
    scale_rows = offset_rows = None
    for l in range(LAYERS):
        z = z_out.at[l] if l < LAYERS - 1 else z_last
        stats = Stats()
        loads[l].wait()

        def consume(block, l=l, z=z, stats=stats):
            out = conv_block(block, buf, w[l])
            z[block[0] : block[0] + block[1], :] = out
            stats.add(block, out)

        if l == 0:
            for block in BLOCKS:
                consume(block)
        else:
            keep = a_out.at[l] if l < LAYERS - 1 else a_last
            before = z_out.at[l - 1]
            produce = lambda block: act_tiles(block, before, scale_rows, offset_rows, buf, keep)
            pipelined(produce, consume)
        mean, rstd = stats.finish()
        if l < LAYERS - 1:
            stats_out[l, 0:8, :] = mean
            stats_out[l, 8:16, :] = rstd
        scale_rows = rstd * gains[l : l + 1]
        offset_rows = shifts[l : l + 1] - mean * scale_rows
    for block in BLOCKS:
        act_tiles(block, z_last, scale_rows, offset_rows, buf)

    lane = lax.broadcasted_iota(jnp.int32, (TILE, LANES), 1)
    row = lax.broadcasted_iota(jnp.int32, (TILE, LANES), 0)
    third = ((row >= 16) & (row < 24)) | ((row >= 32) & (row < 40))
    fourth = (row >= 26) & (row < 30)

    @pl.when(tower == 0)
    def _():
        hg[...] = hg_in[...]
        scale_sums[...] = jnp.zeros(scale_sums.shape, f32)

    @pl.when(tower == 1)
    def _():
        for cell, cells, first, width in PARTS:
            for at in range(0, cells, 256):
                size = min(256, cells - at)
                total = None
                for i in range(3):
                    from_row = first + at + (i - 1) * width
                    for j in range(3):
                        kernel = jnp.concatenate([head[i, j], jnp.zeros((LANES - HEAD, C), bf16)], axis=0)
                        term = lax.dot_general(
                            buf[from_row : from_row + size, j * C : (j + 1) * C],
                            kernel,
                            (((1,), (1,)), ((), ())),
                            preferred_element_type=f32,
                        )
                        total = term if total is None else total + term
                u[cell + at : cell + at + size, :] = total
        bias = jnp.concatenate([head_bias[...], jnp.zeros((1, LANES - HEAD), f32)], axis=1)
        dist_lane = (lane >= CLASSES) & (lane < CLASSES + 4)

        def boxes(level, cell, row, width, carry):
            raw = u[pl.ds(cell, TILE), :] + bias
            g = hg_in[pl.ds(cell, TILE), :]
            if level < 3:
                ls = scale[0:1, level : level + 1]
                use = dist_lane
            else:
                ls = jnp.where(third, scale[0:1, 3:4], scale[0:1, 4:5])
                use = dist_lane & (third | fourth)
            weighted = jnp.where(use, g * jnp.exp(ls * raw), 0.0)
            hg[pl.ds(cell, TILE), :] = jnp.where(dist_lane, weighted * ls, g)
            term = weighted * raw
            if level < 3:
                return carry + fold(term)
            return (fold(jnp.where(third, term, 0.0)), fold(jnp.where(fourth, term, 0.0)))

        r = each_tile(boxes, jnp.zeros((8, LANES), f32))
        scale_sums[...] = stack_rows([r[0], r[1], r[2], r[3][0], r[3][1]])

    scale_sum_rows = [scale_sums[k : k + 1, :] for k in range(len(COUNTS))]

    def head_rows(level, cell, row, width, carry):
        tile = hg[pl.ds(cell, TILE), :].astype(bf16).astype(f32)
        at = lax.broadcasted_iota(jnp.int32, tile.shape, 0) & (width - 1)
        after = jnp.where(at == 0, 0.0, pltpu.roll(tile, 1, 0))
        before = jnp.where(at == width - 1, 0.0, pltpu.roll(tile, TILE - 1, 0))
        middle = pltpu.roll(tile, HEAD, 1)
        after = pltpu.roll(after, 2 * HEAD - LANES, 1)
        rows = pl.ds(row, TILE)
        hbuf[rows, 0:LANES] = jnp.where(lane < HEAD, before, middle).astype(bf16)
        hbuf[rows, LANES : 2 * LANES] = jnp.where(lane < 2 * HEAD - LANES, middle, after).astype(bf16)
        return carry + fold(tile)

    r = each_tile(head_rows, jnp.zeros((8, LANES), f32))
    bias_row = jnp.sum(r[0] + r[1] + r[2] + r[3], axis=0, keepdims=True)

    bit = bit_of(order, 0)
    a4t = jnp.concatenate([center(buf, n, r, C).T for _, n, r, _ in PARTS], axis=1)
    for i in range(3):
        split_store(bit, 9 + i, kernel_grad(a4t, hbuf, i), keep_out, send_out)
    l = LAYERS - 1
    up = Upward(dy, z_last, mean, rstd, gains[l : l + 1], shifts[l : l + 1])
    for block in BLOCKS:
        _, cells, row, width, _ = block
        left = jnp.concatenate([hbuf[row - d * width : row - d * width + cells, :] for d in (-1, 0, 1)], axis=1)
        up.add(block, jnp.dot(left, hw[...], preferred_element_type=f32))
    up.finish(sums)
    produce, norm_sums = norm_back(dy, z_last, mean, rstd, gains[l : l + 1], sums, buf)
    wide = lambda v: jnp.concatenate([v, jnp.zeros_like(v)], axis=1)
    vec = vector_rows(norm_sums + [wide(bias_row)] + [wide(v) for v in scale_sum_rows])
    vec_out[...] = vec
    send_out[12 * half :, :] = pack(vec)
    turned[...] = a_last[...].T
    layer_down(l, produce, buf, lambda tap: w[l, tap * C : (tap + 1) * C, :], z_out, stats_out, gains, shifts, dy_out, sums_out)
    gradients_out(bit, turned, buf, keep_out, send_out)


def layer_down(l, produce, buf, weight, z, stats, gains, shifts, dy_out, sums_out):
    k = l - 1
    up = Upward(dy_out, z.at[k], stats[k, 0:8, :], stats[k, 8:16, :], gains[k : k + 1], shifts[k : k + 1])
    pipelined(produce, lambda block: up.add(block, conv_back_block(block, buf, weight)))
    up.finish(sums_out)


def middle_kernel(l, order, dy, sums, z, a, stats, gains, shifts, w, *refs):
    if l:
        dy_out, sums_out, keep_out, send_out, vec_out, buf, turned = refs
    else:
        keep_half, send_half, keep_out, send_out, vec_out, buf, turned = refs
    half = C // 2
    bit = bit_of(order, 0)
    clear_gaps(buf)
    produce, norm_sums = norm_back(
        dy, z.at[l], stats[l, 0:8, :], stats[l, 8:16, :], gains[l : l + 1], sums, buf
    )
    vec = vector_rows(norm_sums)
    vec_out[...] = vec
    send_out[9 * half :, :] = pack(vec)
    turned[...] = a[l].T
    weight = lambda tap: w[l, tap * C : (tap + 1) * C, :]
    if l:
        layer_down(l, produce, buf, weight, z, stats, gains, shifts, dy_out, sums_out)
    else:
        mine = lax.axis_index("tower")

        def consume(block):
            da = conv_back_block(block, buf, weight)
            at = slice(block[0], block[0] + block[1])
            keep_half[at, :] = jnp.where(mine == 0, da[:, :half], da[:, half:])
            send_half[at, :] = jnp.where(mine == 0, da[:, half:], da[:, :half]).astype(bf16)

        pipelined(produce, consume)
    gradients_out(bit, turned, buf, keep_out, send_out)


def run_prepare(token, head, cls, reg, pos):
    return call(
        prepare_kernel,
        token,
        (head, cls, reg, pos),
        [VMEM] * 4,
        [pltpu.VMEM((3 * C, C), bf16), pltpu.VMEM((CELLS, LANES), f32)],
        [VMEM] * 2,
        "prepare",
        [pltpu.VMEM((TILE, C), f32)],
        16,
    )


def run_first(order, token, scale, own, other, mean, var, w, gains, shifts, head, bias, hw, hg):
    half = C // 2
    return call(
        functools.partial(first_kernel, order),
        token,
        (scale, own, other, mean, var, w, gains, shifts, head, bias, hw, hg),
        [VMEM] * 5 + [HBM] + [VMEM] * 6,
        [
            pltpu.VMEM((LAYERS, 9 * C, C), bf16),
            pltpu.VMEM((LAYERS - 1, CELLS, C), f32),
            pltpu.VMEM((LAYERS - 1, CELLS, C), bf16),
            pltpu.VMEM((LAYERS - 1, 16, C), f32),
            pltpu.VMEM((CELLS, C), f32),
            pltpu.VMEM((16, C), f32),
            pltpu.VMEM((12 * half, C), bf16),
            pltpu.VMEM((12 * half + VEC, C), bf16),
            pltpu.VMEM((8, C), f32),
        ],
        [VMEM] * 9,
        "forward_and_heads",
        [
            pltpu.VMEM((PADDED, 3 * C), bf16),
            pltpu.VMEM((CELLS, C), f32),
            pltpu.VMEM((CELLS, C), bf16),
            pltpu.VMEM((CELLS, C), f32),
            pltpu.VMEM((16, C), f32),
            pltpu.VMEM((CELLS, LANES), f32),
            pltpu.VMEM((PADDED, 2 * LANES), bf16),
            pltpu.VMEM((CELLS, LANES), f32),
            pltpu.VMEM((C, CELLS), bf16),
            pltpu.VMEM((TILE, C), f32),
            pltpu.VMEM((8, LANES), f32),
            pltpu.SemaphoreType.DMA((LAYERS,)),
        ],
        FIRST_MIB,
    )


def run_middle(l, order, token, dy, sums, z, a, stats, gains, shifts, w):
    half = C // 2
    outs = [shape((CELLS, C), f32), shape((16, C), f32)] if l else [shape((CELLS, half), f32), shape((CELLS, half), bf16)]
    outs += [shape((9 * half, C), bf16), shape((9 * half + VEC, C), bf16), shape((8, C), f32)]
    scratch = [
        pltpu.VMEM((PADDED, 3 * C), bf16),
        pltpu.VMEM((C, CELLS), bf16),
    ]
    return call(
        functools.partial(middle_kernel, l, order),
        token,
        (dy, sums, z, a, stats, gains, shifts, w),
        [VMEM] * 8,
        outs,
        [VMEM] * len(outs),
        f"layer_gradients_{l}",
        scratch,
        MIDDLE_MIB,
    )


class Sum:
    def __init__(self, layer, taps, order, bits, keep, send, vec):
        self.layer, self.taps, self.order, self.bits = layer, taps, order, bits
        self.keep, self.vec = keep, vec
        self.splits = min(SPLITS, bits)
        self.rows = C // 2
        self.steps = bits + self.splits - 1
        self.got = self.partner(send, 0)

    def partner(self, value, step):
        pairs = []
        for d in range(1 << self.bits):
            for t in range(2):
                pairs.append((2 * d + t, 2 * (d ^ (1 << self.order[t][step])) + t))
        return lax.ppermute(value, ("dp", "tower"), pairs)

    def advance(self, step, token):
        taps, rows = self.taps, self.rows
        vec = shape((8, C), f32)
        if step < self.splits:
            half = rows // 2
            (self.keep, send, self.vec), token = call(
                functools.partial(halve_kernel, taps, rows, self.order, step),
                token, (self.keep, self.got, self.vec), [VMEM] * 3,
                [shape((taps * half, C), bf16), shape((taps * half + VEC, C), bf16), vec], [VMEM] * 3,
                f"halve_{self.layer}_{step}",
            )
            self.rows = half
            bit = step
        elif step <= self.bits:
            (send, self.vec), token = call(
                functools.partial(add_kernel, taps, rows),
                token, (self.keep, self.got, self.vec), [VMEM] * 3,
                [shape((taps * rows + VEC, C), bf16), vec], [VMEM] * 2,
                f"add_{self.layer}_{step}",
            )
            self.keep = send
            bit = step if step < self.bits else self.splits - 1
        else:
            bit = self.steps - step
            (send,), token = call(
                functools.partial(join_kernel, taps, rows, self.order, bit + 1),
                token, (self.keep, self.got), [VMEM] * 2,
                [shape((taps * 2 * rows, C), bf16)], [VMEM],
                f"join_{self.layer}_{step}",
            )
            self.keep = send
            self.rows = 2 * rows
        self.got = self.partner(send, bit)
        return token

    def finish(self, token, out, own, vecs):
        extra = 0 if own else self.taps - 9
        outs, out_specs = [shape((LAYERS * 9 * C, C), f32)], [HBM]
        ins, specs = [self.keep if own else self.got], [VMEM]
        if extra:
            ins, specs = ins + [self.keep, self.vec], specs + [VMEM] * 2
            outs.append(shape((extra * C + VEC, C), bf16))
            out_specs.append(VMEM)
        elif not own and not self.layer:
            ins, specs = ins + vecs, specs + [VMEM] * LAYERS
            outs += [shape((LAYERS, C), f32)] * 2
            out_specs += [VMEM] * 2
        alias = {}
        if out is not None:
            alias = {len(ins): 0}
            ins, specs = ins + [out], specs + [HBM]
        if own:
            kernel = functools.partial(write_own_kernel, self.layer, self.order)
        else:
            kernel = functools.partial(write_got_kernel, self.layer, self.order, extra)
        return call(
            kernel, token, ins, specs, outs, out_specs, f"write_{self.layer}_{'own' if own else 'got'}",
            [pltpu.VMEM((9 * C // 2, C), f32), pltpu.SemaphoreType.DMA((9,))], 16, alias,
        )


TIMELINE = (
    (2, 0), (1, 0), (3, 1), (0, 0), (3, 2), (1, 1), (2, 1), (3, 3), (1, 2), (0, 1), (1, 3), (2, 2),
    (3, 4), (0, 2), (1, 4), (2, 3), (0, 3), (3, 5), (0, 4), (1, 5), (2, 4), (8, 0), (3, 6), (0, 5),
    (1, 6), (2, 5), (0, 6), (3, 7), (2, 6), (0, 7), (1, 7), (3, 8), (2, 7), (9, 0), (1, 8), (0, 8),
    (2, 8),
)
ORDERS = (
    ((1, 2, 0, 3), (0, 1, 2, 3)),
    ((2, 0, 1, 3), (1, 2, 0, 3)),
    ((0, 1, 2, 3), (2, 0, 1, 3)),
    ((0, 1, 2, 3), (2, 0, 1, 3)),
)


def orders(bits):
    if bits == 4:
        return ORDERS
    line = tuple(range(bits))
    return (((line, line[1:] + line[:1]),) * LAYERS)


def timeline(bits, steps):
    if bits == 4:
        return TIMELINE
    late = [(l, step) for step in range(1, steps + 3) for l in (3, 2, 1, 0)]
    return [(2, 0), (1, 0), (0, 0)] + late + [(FEATURES, 0), (HEADS, 0)]


def body(
    features, bn_mean, bn_var, tower_weight, norm_gain, norm_bias, head_weight, head_bias, level_scale,
    cls_cot, reg_cot, positive, *, dp,
):
    bits = dp.bit_length() - 1
    assert dp == 1 << bits and bits >= 1
    order = orders(bits)
    in_hbm = lambda v: pltpu.with_memory_space_constraint(v, pltpu.HBM)
    own = features[0]
    swap = [(0, 1), (1, 0)]
    other = lax.ppermute(own, "tower", swap)
    w = in_hbm(tower_weight[0].reshape(LAYERS, 9 * C, C))
    gains, shifts = in_hbm(norm_gain[0]), in_hbm(norm_bias[0])
    mean, var = in_hbm(bn_mean[None]), in_hbm(bn_var[None])
    head = in_hbm(jnp.swapaxes(head_weight, 2, 3))
    (hw, hg), token = run_prepare(
        mean, head, in_hbm(jnp.swapaxes(cls_cot[0], 0, 1)), in_hbm(jnp.swapaxes(reg_cot[0], 0, 1)), in_hbm(positive)
    )
    (w, z, a, stats, dy, dy_sums, keep, send, vec), token = run_first(
        order[3], token, in_hbm(level_scale[None]), in_hbm(own), other, mean, var, w, gains, shifts, head,
        in_hbm(head_bias[None]), hw, hg,
    )
    sums = [None] * LAYERS
    sums[3] = Sum(3, 12, order[3], bits, keep, send, vec)
    out = None
    for l, step in timeline(bits, sums[3].steps):
        if l == FEATURES:
            (feature_grad,), token = call(
                features_kernel, token, (keep_half, got_half, var), [VMEM] * 3,
                [shape((PIX, C // 2), bf16)], [VMEM], "feature_gradient",
            )
        elif l == HEADS:
            (dhead, dbias, dscale), token = call(
                heads_kernel, token, (heads, got_heads, sums[3].vec), [VMEM] * 3,
                [shape((3, 3, HEAD, C), f32), shape((1, HEAD), f32), shape((1, len(COUNTS)), f32)], [VMEM] * 3,
                "head_gradients",
            )
        elif step == 0:
            (*grads, keep, send, vec), token = run_middle(l, order[l], token, dy, dy_sums, z, a, stats, gains, shifts, w)
            sums[l] = Sum(l, 9, order[l], bits, keep, send, vec)
            if l:
                dy, dy_sums = grads
            else:
                keep_half, send_half = grads
                got_half = lax.ppermute(send_half, "tower", swap)
        elif step <= sums[l].steps:
            token = sums[l].advance(step, token)
        elif step == sums[l].steps + 1:
            (out,), token = sums[l].finish(token, out, True, None)
        else:
            (out, *more), token = sums[l].finish(token, out, False, [one.vec for one in sums])
            if l == 3:
                (heads,) = more
                got_heads = lax.ppermute(heads, "tower", swap)
            elif l == 0:
                dgain, dshift = more
    return (
        feature_grad[None],
        out.reshape(1, LAYERS, 3, 3, C, C),
        dgain[None],
        dshift[None],
        jnp.swapaxes(dhead, 2, 3),
        dbias[0],
        dscale[0],
    )


def solution(mesh):
    return jax.shard_map(
        functools.partial(body, dp=mesh.shape["dp"]),
        mesh=mesh,
        in_specs=(
            P("dp", None, "tower"),
            P(),
            P(),
            P("tower", None, None, None, None, None),
            P("tower", None, None),
            P("tower", None, None),
            P(),
            P(),
            P(),
            P("dp", None, None),
            P("dp", None, None),
            P("dp", None),
        ),
        out_specs=(
            P("dp", None, "tower"),
            P("tower", None, None, None, None, None),
            P("tower", None, None),
            P("tower", None, None),
            P(),
            P(),
            P(),
        ),
        check_vma=False,
    )
```

```python
import functools

import jax
import jax.numpy as jnp
from jax import lax
from jax.experimental import pallas as pl
from jax.experimental.pallas import tpu as pltpu
from jax.sharding import PartitionSpec as P

C = 256
GROUP = 8
CLASSES = 80
HEAD = 85
LANES = 128
LAYERS = 4
CELLS = 1408
PIX = 1364
COUNTS = (1024, 256, 64, 16, 4)
PARTS = ((0, 1024, 64, 64), (1024, 256, 1152, 32), (1280, 128, 1440, 16))
PADDED = 1584
GAPS = ((0, 64), (1088, 64), (1408, 32), (1568, 16))
TILE = 64
BLOCKS = tuple((256 * i, 256, 64 + 256 * i, 64, 0) for i in range(4)) + ((1024, 256, 1152, 32, 1), (1280, 128, 1440, 16, 2))
EPS = 1e-05
f32 = jnp.float32
bf16 = jnp.bfloat16
VMEM = pl.BlockSpec(memory_space=pltpu.VMEM)
SMEM = pl.BlockSpec(memory_space=pltpu.SMEM)
HBM = pl.BlockSpec(memory_space=pltpu.HBM)


VEC = 32
FEATURES, HEADS = 8, 9
COST = 1500000000
COSTS = {
    "write_3_own": 100000000,
    "layer_gradients_2": 3000000000,
    "join_1_6": 1000000000,
    "halve_1_1": 2000000000,
    "add_1_3": 300000000,
    "write_2_own": 3000000000,
    "join_2_6": 3000000000,
    "halve_0_1": 300000000,
    "feature_gradient": 100000000,
    "halve_3_1": 1500000000,
    "halve_2_1": 2000000000,
    "write_1_own": 100000000,
    "add_0_4": 1000000000,
    "head_gradients": 1500000000,
    "layer_gradients_1": 5000000000,
    "add_0_3": 5000000000,
    "layer_gradients_0": 2000000000,
    "write_0_got": 3000000000,
    "write_3_got": 1000000,
    "join_3_6": 1000000000,
    "halve_0_2": 1500000000,
    "write_1_got": 2000000000,
    "join_0_5": 1000000,
    "join_1_5": 1000000000,
    "halve_2_2": 2000000000,
    "join_0_6": 3000000000,
    "add_3_4": 300000000,
    "join_3_5": 3000000000,
    "add_1_4": 100000000,
    "halve_3_2": 2000000000,
    "halve_1_2": 1500000000,
}
FIRST_MIB = 32
MIDDLE_MIB = 24
SPLITS = 3


def params(mib=56):
    return pltpu.CompilerParams(vmem_limit_bytes=mib << 20)


def tail_masks():
    row = lax.broadcasted_iota(jnp.int32, (TILE, C), 0)
    third = ((row >= 16) & (row < 24)) | ((row >= 32) & (row < 40))
    fourth = (row >= 26) & (row < 30)
    return third, fourth


def pick(third, fourth, vec):
    return jnp.where(third, vec[3:4], jnp.where(fourth, vec[4:5], 0.0))


def fold(tile):
    return jnp.sum(tile.reshape(TILE // 8, 8, tile.shape[1]), axis=0)


def group_sum(vec):
    lane = lax.broadcasted_iota(jnp.int32, vec.shape, 1)
    for step in (1, 2, 4):
        up = pltpu.roll(vec, vec.shape[1] - step, 1)
        down = pltpu.roll(vec, step, 1)
        vec = vec + jnp.where((lane & step) == 0, up, down)
    return vec


def counts_column():
    row = lax.broadcasted_iota(jnp.int32, (8, C), 0)
    out = jnp.full((8, C), 1.0, f32)
    for level, cells in enumerate(COUNTS):
        out = jnp.where(row == level, 1.0 / (cells * GROUP), out)
    return out


def stack_rows(rows):
    row = lax.broadcasted_iota(jnp.int32, (8, rows[0].shape[1]), 0)
    out = jnp.zeros((8, rows[0].shape[1]), f32)
    for place, value in enumerate(rows):
        out = jnp.where(row == place, jnp.sum(value, axis=0, keepdims=True), out)
    return out


def moved(tile, width):
    row = lax.broadcasted_iota(jnp.int32, (8, tile.shape[1]), 0)
    before, after = pltpu.roll(tile, 1, 0), pltpu.roll(tile, TILE - 1, 0)
    first, last = [], []
    for at in range(0, TILE, 8):
        one, two = before[at : at + 8], after[at : at + 8]
        first.append(jnp.where(row == 0, 0.0, one) if at % width == 0 else one)
        last.append(jnp.where(row == 7, 0.0, two) if (at + 8) % width == 0 else two)
    return jnp.concatenate(first, axis=0), jnp.concatenate(last, axis=0)


def write_shifted(buf, row, width, tile, lanes, flip):
    before, after = moved(tile, width)
    if flip:
        before, after = after, before
    rows = pl.ds(row, TILE)
    buf[rows, 0:lanes] = before.astype(bf16)
    buf[rows, lanes : 2 * lanes] = tile.astype(bf16)
    buf[rows, 2 * lanes : 3 * lanes] = after.astype(bf16)


def clear_gaps(buf):
    for row, rows in GAPS:
        buf[row : row + rows, :] = jnp.zeros((rows, buf.shape[1]), bf16)


def conv_block(block, buf, weight):
    _, cells, row, width, _ = block
    left = jnp.concatenate([buf[row + d * width : row + d * width + cells, :] for d in (-1, 0, 1)], axis=1)
    return jnp.dot(left, weight, preferred_element_type=f32)


def conv_back_block(block, buf, weight):
    _, cells, row, width, _ = block
    total = None
    for i in range(3):
        at = row - (i - 1) * width
        for j in range(3):
            term = lax.dot_general(
                buf[at : at + cells, j * C : (j + 1) * C],
                weight(i * 3 + j),
                (((1,), (1,)), ((), ())),
                preferred_element_type=f32,
            )
            total = term if total is None else total + term
    return total


def kernel_grad(turned, buf, i):
    total = None
    for cell, cells, row, width in PARTS:
        at = row - (i - 1) * width
        term = jnp.dot(turned[:, cell : cell + cells], buf[at : at + cells, :], preferred_element_type=f32)
        total = term if total is None else total + term
    return total


def tiles_of(block):
    cell, cells, row, width, level = block
    return [(level if at == 0 or level < 2 else 3, cell + at, row + at, width, at) for at in range(0, cells, TILE)]


def pipelined(produce, consume, ready=lambda: None):
    produce(BLOCKS[0])
    for i, block in enumerate(BLOCKS):
        if i + 1 < len(BLOCKS):
            produce(BLOCKS[i + 1])
        if i == 0:
            ready()
        consume(block)


class Stats:
    def __init__(self):
        self.center = None
        self.sums = [jnp.zeros((8, C), f32), jnp.zeros((8, C), f32)]
        self.rows = []

    def own(self, tile, cells, mask=None):
        kept = tile if mask is None else jnp.where(mask, tile, 0.0)
        mean = jnp.sum(kept, axis=0, keepdims=True) * (1.0 / cells)
        d = tile - mean
        d = d if mask is None else jnp.where(mask, d, 0.0)
        self.rows.append((mean, jnp.sum(d * d, axis=0, keepdims=True)))

    def add(self, block, z):
        level = block[4]
        if level == 0:
            if self.center is None:
                self.center = jnp.sum(z, axis=0, keepdims=True) * (1.0 / z.shape[0])
            d = z - self.center
            wide = lambda v: jnp.sum(v.reshape(z.shape[0] // 8, 8, C), axis=0)
            self.sums = [self.sums[0] + wide(d), self.sums[1] + wide(d * d)]
        elif level == 1:
            self.own(z, COUNTS[1])
        else:
            third, fourth = tail_masks()
            self.own(z[:TILE], COUNTS[2])
            self.own(z[TILE:], COUNTS[3], third)
            self.own(z[TILE:], COUNTS[4], fourth)

    def finish(self):
        first, second = (jnp.sum(v, axis=0, keepdims=True) for v in self.sums)
        shift = first * (1.0 / COUNTS[0])
        rows = [(self.center + shift, second - first * shift)] + self.rows
        means = stack_rows([r[0] for r in rows])
        squares = stack_rows([r[1] for r in rows])
        inv_counts = counts_column()
        mean = group_sum(means) * (1.0 / GROUP)
        d = means - mean
        var = group_sum(squares * inv_counts + d * d * (1.0 / GROUP))
        return mean, lax.rsqrt(var + EPS)


def level_rows(level, vec, masks):
    if level < 3:
        return vec[level : level + 1]
    return pick(*masks, vec)


def act_tiles(block, z, scale, offset, buf, keep=None):
    masks = tail_masks()
    for level, cell, row, width, _ in tiles_of(block):
        h = z[cell : cell + TILE, :] * level_rows(level, scale, masks) + level_rows(level, offset, masks)
        a = h * jnp.tanh(h) + h
        if level == 3:
            a = jnp.where(masks[0] | masks[1], a, 0.0)
        write_shifted(buf, row, width, a, C, False)
        if keep is not None:
            keep[cell : cell + TILE, :] = a.astype(bf16)


class Upward:
    def __init__(self, dy_out, z, mean, rstd, gain, shift):
        self.dy_out, self.z, self.rstd, self.neg, self.gain, self.shift = dy_out, z, rstd, -mean * rstd, 0.5 * gain, 0.5 * shift
        self.sums = [[jnp.zeros((8, C), f32), jnp.zeros((8, C), f32)] for _ in COUNTS]

    def add(self, block, da):
        masks = tail_masks()
        for level, cell, _, _, at in tiles_of(block):
            zhat = self.z[cell : cell + TILE, :] * level_rows(level, self.rstd, masks) + level_rows(level, self.neg, masks)
            h = zhat * self.gain + self.shift
            t = jnp.tanh(h)
            dy = da[at : at + TILE] * ((1.0 + t) * (1.0 + h * (1.0 - t)))
            self.dy_out[cell : cell + TILE, :] = dy
            dyz = dy * zhat
            if level < 3:
                parts = [(level, dy, dyz)]
            else:
                parts = [(3 + k, jnp.where(m, dy, 0.0), jnp.where(m, dyz, 0.0)) for k, m in enumerate(masks)]
            for to, one, two in parts:
                self.sums[to] = [self.sums[to][0] + fold(one), self.sums[to][1] + fold(two)]

    def finish(self, sums_out):
        sums_out[0:8, :] = 0.5 * stack_rows([v[0] for v in self.sums])
        sums_out[8:16, :] = 0.5 * stack_rows([v[1] for v in self.sums])


def norm_back(dy, z, mean, rstd, gain, sums, buf):
    sum_dy, sum_dyz = sums[0:8, :], sums[8:16, :]
    inv_counts = counts_column()
    mean_e = group_sum(sum_dy * gain) * inv_counts
    mean_ez = group_sum(sum_dyz * gain) * inv_counts
    on_dy = 0.5 * rstd * gain
    on_zhat = rstd * mean_ez
    on_z = -on_zhat * rstd
    flat = on_zhat * mean * rstd - rstd * mean_e

    def produce(block):
        masks = tail_masks()
        for level, cell, row, width, _ in tiles_of(block):
            at = slice(cell, cell + TILE)
            dz = (
                dy[at, :] * level_rows(level, on_dy, masks)
                + z[at, :] * level_rows(level, on_z, masks)
                + level_rows(level, flat, masks)
            )
            write_shifted(buf, row, width, dz, C, True)

    return produce, [jnp.sum(v, axis=0, keepdims=True) for v in (sum_dyz, sum_dy)]


def center(buf, cells, row, lanes):
    return buf[row : row + cells, lanes : 2 * lanes]


def shape(dims, dtype):
    return jax.ShapeDtypeStruct(dims, dtype)


def pack(vec):
    high = vec.astype(bf16).astype(f32)
    middle = (vec - high).astype(bf16).astype(f32)
    low = vec - high - middle
    return jnp.concatenate([high, middle, low, jnp.zeros_like(vec)], axis=0).astype(bf16)


def unpack(block):
    parts = block.astype(f32)
    return parts[0:8] + parts[8:16] + parts[16:24]


def bit_of(order, step):
    dp = lax.axis_index("dp")
    return jnp.where(lax.axis_index("tower") == 0, dp >> order[0][step], dp >> order[1][step]) & 1


def call(kernel, token, ins, in_specs, outs, out_specs, name, scratch=(), mib=16, alias=None):
    n_in, n_out = len(ins), len(outs)

    def ordered(*refs):
        kernel(*refs[:n_in], *refs[n_in + 1 : n_in + 1 + n_out], *refs[n_in + n_out + 2 :])

    *results, token = pl.pallas_call(
        ordered,
        out_shape=list(outs) + [shape((8, LANES), f32)],
        in_specs=list(in_specs) + [HBM],
        out_specs=list(out_specs) + [HBM],
        scratch_shapes=list(scratch),
        input_output_aliases=alias or {},
        compiler_params=params(mib),
        cost_estimate=pl.CostEstimate(flops=COSTS.get(name, COST), bytes_accessed=1, transcendentals=0),
        name=name,
    )(*ins, token)
    return results, token


def split_store(bit, tap, grad, keep, send):
    half = C // 2
    low, high = grad[:half], grad[half:]
    keep[tap * half : (tap + 1) * half, :] = jnp.where(bit == 1, high, low).astype(bf16)
    send[tap * half : (tap + 1) * half, :] = jnp.where(bit == 1, low, high).astype(bf16)


def halve_kernel(taps, rows, order, step, keep, got, vec, keep_out, send_out, vec_out):
    bit = bit_of(order, step)
    half = rows // 2

    def one(t, _):
        for out, side in ((keep_out, bit), (send_out, 1 - bit)):
            at = pl.ds(pl.multiple_of(t * rows + side * half, half), half)
            to = pl.ds(pl.multiple_of(t * half, half), half)
            out[to, :] = (keep[at, :].astype(f32) + got[at, :].astype(f32)).astype(bf16)
        return 0

    lax.fori_loop(0, taps, one, 0)
    total = vec[...] + unpack(got[taps * rows :, :])
    vec_out[...] = total
    send_out[taps * half :, :] = pack(total)


def add_kernel(taps, rows, keep, got, vec, sum_out, vec_out):
    def one(t, _):
        at = pl.ds(pl.multiple_of(t * rows, rows), rows)
        sum_out[at, :] = (keep[at, :].astype(f32) + got[at, :].astype(f32)).astype(bf16)
        return 0

    lax.fori_loop(0, taps, one, 0)
    total = vec[...] + unpack(got[taps * rows :, :])
    vec_out[...] = total
    sum_out[taps * rows :, :] = pack(total)


def join_kernel(taps, rows, order, step, own, got, out):
    bit = bit_of(order, step)

    def one(t, _):
        at = pl.ds(pl.multiple_of(t * rows, rows), rows)
        out[pl.ds(pl.multiple_of((2 * t + bit) * rows, rows), rows), :] = own[at, :]
        out[pl.ds(pl.multiple_of((2 * t + 1 - bit) * rows, rows), rows), :] = got[at, :]
        return 0

    lax.fori_loop(0, taps, one, 0)


def write_half(layer, side, half_rows, out, wide, sems):
    half = C // 2
    copies = []
    for t in range(9):
        rows = slice(t * half, (t + 1) * half)
        wide[rows, :] = half_rows[rows, :].astype(f32)
        to = pl.multiple_of((layer * 9 + t) * C + side * half, half)
        copies.append(pltpu.make_async_copy(wide.at[rows], out.at[pl.ds(to, half)], sems.at[t]))
        copies[-1].start()
    return copies


def write_own_kernel(layer, order, own, *refs):
    out, wide, sems = refs[-3 - (2 if not layer else 0) :][:1] + refs[-2:]
    copies = write_half(layer, bit_of(order, 0), own, out, wide, sems)
    if not layer:
        vecs, (gains_out, shifts_out) = refs[:LAYERS], refs[-4:-2]
        gains_out[...] = jnp.concatenate([v[0:1, :] for v in vecs], axis=0)
        shifts_out[...] = jnp.concatenate([v[1:2, :] for v in vecs], axis=0)
    for copy in copies:
        copy.wait()


def write_got_kernel(layer, order, extra, got, *refs):
    bit = bit_of(order, 0)
    out, wide, sems = refs[-3 - (1 if extra else 0) :][:1] + refs[-2:]
    copies = write_half(layer, 1 - bit, got, out, wide, sems)
    half = C // 2
    if extra:
        own, vec, _, _, rest, _, _ = refs
        for t in range(extra):
            rest[pl.ds(pl.multiple_of(t * C + bit * half, half), half), :] = own[(9 + t) * half : (10 + t) * half, :]
            rest[pl.ds(pl.multiple_of(t * C + (1 - bit) * half, half), half), :] = got[(9 + t) * half : (10 + t) * half, :]
        rest[extra * C :, :] = pack(vec[...])
    for copy in copies:
        copy.wait()


def heads_kernel(own, got, vec, dhead_out, bias_out, scale_out):
    for i in range(3):
        at = slice(i * C, (i + 1) * C)
        turned = (own[at, :].astype(f32) + got[at, :].astype(f32)).T
        for j in range(3):
            dhead_out[i, j] = turned[j * HEAD : (j + 1) * HEAD, :]
    both = vec[...] + unpack(got[3 * C :, :])
    bias_out[...] = both[2:3, 0:HEAD]
    lane = lax.broadcasted_iota(jnp.int32, (8, LANES), 1)
    row = lax.broadcasted_iota(jnp.int32, (8, LANES), 0)
    sums = jnp.sum(both[:, 0:LANES], axis=1, keepdims=True)
    line = jnp.sum(jnp.where((row >= 3) & (lane == row - 3), sums, 0.0), axis=0, keepdims=True)
    scale_out[...] = line[:, 0 : len(COUNTS)]


def features_kernel(keep, got, var, out):
    half = C // 2
    inverse = lax.rsqrt(jnp.where(lax.axis_index("tower") == 0, var[:, :half], var[:, half:]) + EPS)

    def scaled(cell, cells):
        return (keep[pl.ds(cell, cells), :].astype(f32) + got[pl.ds(cell, cells), :].astype(f32)) * inverse

    def one(t, _):
        at = pl.multiple_of(t * TILE, TILE)
        out[pl.ds(at, TILE), :] = scaled(at, TILE).astype(bf16)
        return 0

    lax.fori_loop(0, 1344 // TILE, one, 0)
    tail = scaled(1344, TILE)
    out[1344:PIX, :] = jnp.concatenate([tail[16:24], tail[32:40], tail[26:30]], axis=0).astype(bf16)


def gradients_out(bit, turned, buf, keep, send):
    for i in range(3):
        grad = kernel_grad(turned, buf, i)
        for j in range(3):
            split_store(bit, i * 3 + j, grad[:, j * C : (j + 1) * C], keep, send)


def vector_rows(rows):
    row = lax.broadcasted_iota(jnp.int32, (8, C), 0)
    out = jnp.zeros((8, C), f32)
    for at, value in enumerate(rows):
        out = jnp.where(row == at, value, out)
    return out


def spread_tail(tile, scratch):
    scratch[...] = jnp.zeros(scratch.shape, f32)
    scratch[16:24, :] = tile[0:8]
    scratch[32:40, :] = tile[8:16]
    scratch[26:30, :] = tile[16:20]


class Heads:
    def __init__(self, hg, hk, hbuf, bias, scale):
        self.hg, self.hk, self.hbuf, self.scale = hg, hk, hbuf, scale
        self.bias = jnp.concatenate([bias[...], jnp.zeros((1, LANES - HEAD), f32)], axis=1)
        self.total = jnp.zeros((8, LANES), f32)
        self.scales = [jnp.zeros((8, LANES), f32) for _ in COUNTS]

    def add(self, block, buf):
        _, cells, first, width, _ = block
        raw_block = None
        for i in range(3):
            at = first + (i - 1) * width
            for j in range(3):
                tap = (i * 3 + j) * LANES
                term = lax.dot_general(
                    buf[at : at + cells, j * C : (j + 1) * C],
                    self.hk[tap : tap + LANES, :],
                    (((1,), (1,)), ((), ())),
                    preferred_element_type=f32,
                )
                raw_block = term if raw_block is None else raw_block + term
        lane = lax.broadcasted_iota(jnp.int32, (TILE, LANES), 1)
        dist = (lane >= CLASSES) & (lane < CLASSES + 4) & (lax.axis_index("tower") == 1)
        third, fourth = (m[:, :LANES] for m in tail_masks())
        for level, cell, row, width, at in tiles_of(block):
            raw = raw_block[at : at + TILE] + self.bias
            g = self.hg[cell : cell + TILE, :]
            if level < 3:
                ls, use = self.scale[0:1, level : level + 1], dist
            else:
                ls = jnp.where(third, self.scale[0:1, 3:4], self.scale[0:1, 4:5])
                use = dist & (third | fourth)
            weighted = jnp.where(use, g * jnp.exp(ls * raw), 0.0)
            term = weighted * raw
            parts = [(level, term)] if level < 3 else [(3, jnp.where(third, term, 0.0)), (4, jnp.where(fourth, term, 0.0))]
            for to, value in parts:
                self.scales[to] = self.scales[to] + fold(value)
            tile = jnp.where(dist, weighted * ls, g).astype(bf16).astype(f32)
            self.total = self.total + fold(tile)
            after, before = moved(tile, width)
            middle = pltpu.roll(tile, HEAD, 1)
            after = pltpu.roll(after, 2 * HEAD - LANES, 1)
            rows = slice(row, row + TILE)
            self.hbuf[rows, 0:LANES] = jnp.where(lane < HEAD, before, middle).astype(bf16)
            self.hbuf[rows, LANES : 2 * LANES] = jnp.where(lane < 2 * HEAD - LANES, middle, after).astype(bf16)

    def rows(self):
        return [jnp.sum(v, axis=0, keepdims=True) for v in [self.total] + self.scales]


def prepare_kernel(head, cls, reg, pos, hw, hk, hg, tail):
    box = reg[...].astype(f32) * pos[...].astype(f32)
    is_class = lax.axis_index("tower") == 0
    rows = jnp.concatenate(
        [
            jnp.where(is_class, cls[...].astype(f32), 0.0),
            jnp.where(is_class, 0.0, jnp.concatenate([box, jnp.zeros((3, PIX), f32)], axis=0)),
            jnp.zeros((LANES - CLASSES - 8, PIX), f32),
        ],
        axis=0,
    )
    rows = jnp.concatenate([rows, jnp.zeros((LANES, CELLS - PIX), f32)], axis=1)
    hg[...] = rows.T
    spread_tail(jnp.concatenate([hg[1344:PIX, :]] * 2, axis=1), tail)
    hg[1344:CELLS, :] = tail[:, 0:LANES]
    for i in range(3):
        three = jnp.concatenate([head[i, j].astype(f32) for j in range(3)] + [jnp.zeros((1, C), f32)], axis=0)
        hw[i * C : (i + 1) * C, :] = three.astype(bf16)
        for j in range(3):
            one = jnp.concatenate([head[i, j].astype(f32), jnp.zeros((LANES - HEAD, C), f32)], axis=0)
            hk[(i * 3 + j) * LANES : (i * 3 + j + 1) * LANES, :] = one.astype(bf16)


def first_kernel(
    order, scale, own, other, bn_mean, bn_var, w_hbm, gains, shifts, head_bias, hw, hk, hg,
    w, z_out, a_out, stats_out, dy_out, sums_out, keep_out, send_out, vec_out,
    buf, z_last, a_last, dy, sums, hbuf, turned, tail, sems,
):
    loads = [pltpu.make_async_copy(w_hbm.at[l], w.at[l], sems.at[l]) for l in range(LAYERS)]
    for load in loads:
        load.start()
    half = C // 2
    tower = lax.axis_index("tower")
    clear_gaps(buf)
    clear_gaps(hbuf)
    inverse = lax.rsqrt(bn_var[...] + EPS)
    mean0 = bn_mean[...]

    def halves(rows):
        left = jnp.where(tower == 0, own[rows, :].astype(f32), other[rows, :].astype(f32))
        right = jnp.where(tower == 0, other[rows, :].astype(f32), own[rows, :].astype(f32))
        return (jnp.concatenate([left, right], axis=1) - mean0) * inverse

    def base(block):
        for level, cell, row, width, _ in tiles_of(block):
            if level < 3:
                tile = halves(slice(cell, cell + TILE))
            else:
                spread_tail(halves(slice(1344, PIX)), tail)
                tile = tail[...]
            write_shifted(buf, row, width, tile, C, False)
            a_out[0, cell : cell + TILE, :] = tile.astype(bf16)

    scale_rows = offset_rows = None
    for l in range(LAYERS):
        z = z_out.at[l] if l < LAYERS - 1 else z_last
        stats = Stats()

        def consume(block, l=l, z=z, stats=stats):
            out = conv_block(block, buf, w[l])
            z[block[0] : block[0] + block[1], :] = out
            stats.add(block, out)

        if l == 0:
            produce = base
        else:
            keep = a_out.at[l] if l < LAYERS - 1 else a_last
            before = z_out.at[l - 1]
            produce = lambda block: act_tiles(block, before, scale_rows, offset_rows, buf, keep)
        pipelined(produce, consume, loads[l].wait)
        mean, rstd = stats.finish()
        if l < LAYERS - 1:
            stats_out[l, 0:8, :] = mean
            stats_out[l, 8:16, :] = rstd
        scale_rows = 0.5 * rstd * gains[l : l + 1]
        offset_rows = 0.5 * shifts[l : l + 1] - mean * scale_rows
    l = LAYERS - 1
    heads = Heads(hg, hk, hbuf, head_bias, scale)
    up = Upward(dy, z_last, mean, rstd, gains[l : l + 1], shifts[l : l + 1])
    for i in range(len(BLOCKS) + 2):
        if i < len(BLOCKS):
            act_tiles(BLOCKS[i], z_last, scale_rows, offset_rows, buf)
        if 1 <= i <= len(BLOCKS):
            heads.add(BLOCKS[i - 1], buf)
        if i >= 2:
            _, cells, row, width, _ = BLOCKS[i - 2]
            left = jnp.concatenate([hbuf[row - d * width : row - d * width + cells, :] for d in (-1, 0, 1)], axis=1)
            up.add(BLOCKS[i - 2], jnp.dot(left, hw[...], preferred_element_type=f32))
    up.finish(sums)
    bit = bit_of(order, 0)
    a4t = jnp.concatenate([center(buf, n, r, C).T for _, n, r, _ in PARTS], axis=1)
    for i in range(3):
        split_store(bit, 9 + i, kernel_grad(a4t, hbuf, i), keep_out, send_out)
    produce, norm_sums = norm_back(dy, z_last, mean, rstd, gains[l : l + 1], sums, buf)
    wide = lambda v: jnp.concatenate([v, jnp.zeros_like(v)], axis=1)
    vec = vector_rows(norm_sums + [wide(row) for row in heads.rows()])
    vec_out[...] = vec
    send_out[12 * half :, :] = pack(vec)
    turned[...] = a_last[...].T
    layer_down(l, produce, buf, lambda tap: w[l, tap * C : (tap + 1) * C, :], z_out, stats_out, gains, shifts, dy_out, sums_out)
    gradients_out(bit, turned, buf, keep_out, send_out)


def layer_down(l, produce, buf, weight, z, stats, gains, shifts, dy_out, sums_out):
    k = l - 1
    up = Upward(dy_out, z.at[k], stats[k, 0:8, :], stats[k, 8:16, :], gains[k : k + 1], shifts[k : k + 1])
    pipelined(produce, lambda block: up.add(block, conv_back_block(block, buf, weight)))
    up.finish(sums_out)


def middle_kernel(l, order, dy, sums, z, a, stats, gains, shifts, w, *refs):
    if l:
        dy_out, sums_out, keep_out, send_out, vec_out, buf, turned = refs
    else:
        keep_half, send_half, keep_out, send_out, vec_out, buf, turned = refs
    half = C // 2
    bit = bit_of(order, 0)
    clear_gaps(buf)
    produce, norm_sums = norm_back(
        dy, z.at[l], stats[l, 0:8, :], stats[l, 8:16, :], gains[l : l + 1], sums, buf
    )
    vec = vector_rows(norm_sums)
    vec_out[...] = vec
    send_out[9 * half :, :] = pack(vec)
    turned[...] = a[l].T
    weight = lambda tap: w[l, tap * C : (tap + 1) * C, :]
    if l:
        layer_down(l, produce, buf, weight, z, stats, gains, shifts, dy_out, sums_out)
    else:
        mine = lax.axis_index("tower")

        def consume(block):
            da = conv_back_block(block, buf, weight)
            at = slice(block[0], block[0] + block[1])
            keep_half[at, :] = jnp.where(mine == 0, da[:, :half], da[:, half:])
            send_half[at, :] = jnp.where(mine == 0, da[:, half:], da[:, :half]).astype(bf16)

        pipelined(produce, consume)
    gradients_out(bit, turned, buf, keep_out, send_out)


def run_prepare(token, head, cls, reg, pos):
    return call(
        prepare_kernel,
        token,
        (head, cls, reg, pos),
        [VMEM] * 4,
        [pltpu.VMEM((3 * C, C), bf16), pltpu.VMEM((9 * LANES, C), bf16), pltpu.VMEM((CELLS, LANES), f32)],
        [VMEM] * 3,
        "prepare",
        [pltpu.VMEM((TILE, C), f32)],
        16,
    )


def run_first(order, token, scale, own, other, mean, var, w, gains, shifts, bias, hw, hk, hg):
    half = C // 2
    return call(
        functools.partial(first_kernel, order),
        token,
        (scale, own, other, mean, var, w, gains, shifts, bias, hw, hk, hg),
        [VMEM] * 5 + [HBM] + [VMEM] * 6,
        [
            pltpu.VMEM((LAYERS, 9 * C, C), bf16),
            pltpu.VMEM((LAYERS - 1, CELLS, C), f32),
            pltpu.VMEM((LAYERS - 1, CELLS, C), bf16),
            pltpu.VMEM((LAYERS - 1, 16, C), f32),
            pltpu.VMEM((CELLS, C), f32),
            pltpu.VMEM((16, C), f32),
            pltpu.VMEM((12 * half, C), bf16),
            pltpu.VMEM((12 * half + VEC, C), bf16),
            pltpu.VMEM((8, C), f32),
        ],
        [VMEM] * 9,
        "forward_and_heads",
        [
            pltpu.VMEM((PADDED, 3 * C), bf16),
            pltpu.VMEM((CELLS, C), f32),
            pltpu.VMEM((CELLS, C), bf16),
            pltpu.VMEM((CELLS, C), f32),
            pltpu.VMEM((16, C), f32),
            pltpu.VMEM((PADDED, 2 * LANES), bf16),
            pltpu.VMEM((C, CELLS), bf16),
            pltpu.VMEM((TILE, C), f32),
            pltpu.SemaphoreType.DMA((LAYERS,)),
        ],
        FIRST_MIB,
    )


def run_middle(l, order, token, dy, sums, z, a, stats, gains, shifts, w):
    half = C // 2
    outs = [shape((CELLS, C), f32), shape((16, C), f32)] if l else [shape((CELLS, half), f32), shape((CELLS, half), bf16)]
    outs += [shape((9 * half, C), bf16), shape((9 * half + VEC, C), bf16), shape((8, C), f32)]
    scratch = [
        pltpu.VMEM((PADDED, 3 * C), bf16),
        pltpu.VMEM((C, CELLS), bf16),
    ]
    return call(
        functools.partial(middle_kernel, l, order),
        token,
        (dy, sums, z, a, stats, gains, shifts, w),
        [VMEM] * 8,
        outs,
        [VMEM] * len(outs),
        f"layer_gradients_{l}",
        scratch,
        MIDDLE_MIB,
    )


class Sum:
    def __init__(self, layer, taps, order, bits, keep, send, vec):
        self.layer, self.taps, self.order, self.bits = layer, taps, order, bits
        self.keep, self.vec = keep, vec
        self.splits = min(SPLITS, bits)
        self.rows = C // 2
        self.steps = bits + self.splits - 1
        self.got = self.partner(send, 0)

    def partner(self, value, step):
        pairs = []
        for d in range(1 << self.bits):
            for t in range(2):
                pairs.append((2 * d + t, 2 * (d ^ (1 << self.order[t][step])) + t))
        return lax.ppermute(value, ("dp", "tower"), pairs)

    def advance(self, step, token):
        taps, rows = self.taps, self.rows
        self.done = step
        vec = shape((8, C), f32)
        if step < self.splits:
            half = rows // 2
            (self.keep, send, self.vec), token = call(
                functools.partial(halve_kernel, taps, rows, self.order, step),
                token, (self.keep, self.got, self.vec), [VMEM] * 3,
                [shape((taps * half, C), bf16), shape((taps * half + VEC, C), bf16), vec], [VMEM] * 3,
                f"halve_{self.layer}_{step}",
            )
            self.rows = half
            bit = step
        elif step <= self.bits:
            (send, self.vec), token = call(
                functools.partial(add_kernel, taps, rows),
                token, (self.keep, self.got, self.vec), [VMEM] * 3,
                [shape((taps * rows + VEC, C), bf16), vec], [VMEM] * 2,
                f"add_{self.layer}_{step}",
            )
            self.keep = send
            bit = step if step < self.bits else self.splits - 1
        else:
            bit = self.steps - step
            (send,), token = call(
                functools.partial(join_kernel, taps, rows, self.order, bit + 1),
                token, (self.keep, self.got), [VMEM] * 2,
                [shape((taps * 2 * rows, C), bf16)], [VMEM],
                f"join_{self.layer}_{step}",
            )
            self.keep = send
            self.rows = 2 * rows
        self.got = self.partner(send, bit)
        return token

    def finish(self, token, out, own, vecs):
        extra = 0 if own else self.taps - 9
        outs, out_specs = [shape((LAYERS * 9 * C, C), f32)], [HBM]
        ins, specs = [self.keep if own else self.got], [VMEM]
        if extra:
            ins, specs = ins + [self.keep, self.vec], specs + [VMEM] * 2
            outs.append(shape((extra * C + VEC, C), bf16))
            out_specs.append(VMEM)
        elif own and not self.layer:
            ins, specs = ins + vecs, specs + [VMEM] * LAYERS
            outs += [shape((LAYERS, C), f32)] * 2
            out_specs += [VMEM] * 2
        alias = {}
        if out is not None:
            alias = {len(ins): 0}
            ins, specs = ins + [out], specs + [HBM]
        if own:
            kernel = functools.partial(write_own_kernel, self.layer, self.order)
        else:
            kernel = functools.partial(write_got_kernel, self.layer, self.order, extra)
        return call(
            kernel, token, ins, specs, outs, out_specs, f"write_{self.layer}_{'own' if own else 'got'}",
            [pltpu.VMEM((9 * C // 2, C), f32), pltpu.SemaphoreType.DMA((9,))], 16, alias,
        )


TIMELINE = (
    (2, 0), (1, 0), (3, 1), (0, 0), (2, 1), (3, 2), (2, 2), (3, 3), (1, 1), (0, 1), (3, 4), (2, 3),
    (1, 2), (3, 5), (0, 2), (2, 4), (1, 3), (0, 3), (3, 6), (1, 4), (2, 5), (0, 4), (1, 5), (3, 7),
    (0, 5), (2, 6), (3, 8), (1, 6), (8, 0), (0, 6), (9, 0), (0, 7), (1, 7), (2, 7), (2, 8), (1, 8),
    (0, 8),
)
ORDERS = (
    ((2, 0, 1, 3), (0, 1, 2, 3)),
    ((0, 2, 1, 3), (1, 0, 2, 3)),
    ((1, 2, 0, 3), (2, 0, 1, 3)),
    ((0, 2, 1, 3), (1, 0, 2, 3)),
)


def orders(bits):
    if bits == 4:
        return ORDERS
    line = tuple(range(bits))
    return (((line, line[1:] + line[:1]),) * LAYERS)


def timeline(bits, steps):
    if bits == 4:
        return TIMELINE
    late = [(l, step) for step in range(1, steps + 3) for l in (3, 2, 1, 0)]
    return [(2, 0), (1, 0), (0, 0)] + late + [(FEATURES, 0), (HEADS, 0)]


def body(
    features, bn_mean, bn_var, tower_weight, norm_gain, norm_bias, head_weight, head_bias, level_scale,
    cls_cot, reg_cot, positive, *, dp,
):
    bits = dp.bit_length() - 1
    assert dp == 1 << bits and bits >= 1
    order = orders(bits)
    in_hbm = lambda v: pltpu.with_memory_space_constraint(v, pltpu.HBM)
    own = features[0]
    swap = [(0, 1), (1, 0)]
    other = lax.ppermute(own, "tower", swap)
    w = in_hbm(tower_weight[0].reshape(LAYERS, 9 * C, C))
    gains, shifts = in_hbm(norm_gain[0]), in_hbm(norm_bias[0])
    mean, var = in_hbm(bn_mean[None]), in_hbm(bn_var[None])
    head = in_hbm(jnp.swapaxes(head_weight, 2, 3))
    (hw, hk, hg), token = run_prepare(
        mean, head, in_hbm(jnp.swapaxes(cls_cot[0], 0, 1)), in_hbm(jnp.swapaxes(reg_cot[0], 0, 1)), in_hbm(positive)
    )
    (w, z, a, stats, dy, dy_sums, keep, send, vec), token = run_first(
        order[3], token, in_hbm(level_scale[None]), in_hbm(own), other, mean, var, w, gains, shifts,
        in_hbm(head_bias[None]), hw, hk, hg,
    )
    sums = [None] * LAYERS
    sums[3] = Sum(3, 12, order[3], bits, keep, send, vec)
    out = None
    for l, step in timeline(bits, sums[3].steps):
        if l == FEATURES:
            (feature_grad,), token = call(
                features_kernel, token, (keep_half, got_half, var), [VMEM] * 3,
                [shape((PIX, C // 2), bf16)], [VMEM], "feature_gradient",
            )
        elif l == HEADS:
            (dhead, dbias, dscale), token = call(
                heads_kernel, token, (heads, got_heads, sums[3].vec), [VMEM] * 3,
                [shape((3, 3, HEAD, C), f32), shape((1, HEAD), f32), shape((1, len(COUNTS)), f32)], [VMEM] * 3,
                "head_gradients",
            )
        elif step == 0:
            (*grads, keep, send, vec), token = run_middle(l, order[l], token, dy, dy_sums, z, a, stats, gains, shifts, w)
            sums[l] = Sum(l, 9, order[l], bits, keep, send, vec)
            if l:
                dy, dy_sums = grads
            else:
                keep_half, send_half = grads
                got_half = lax.ppermute(send_half, "tower", swap)
        elif step <= sums[l].steps:
            token = sums[l].advance(step, token)
        elif step == sums[l].steps + 1:
            assert l or all(one.done >= bits for one in sums)
            (out, *more), token = sums[l].finish(token, out, True, [one.vec for one in sums])
            if l == 0:
                dgain, dshift = more
        else:
            (out, *more), token = sums[l].finish(token, out, False, None)
            if l == 3:
                (heads,) = more
                got_heads = lax.ppermute(heads, "tower", swap)
    return (
        feature_grad[None],
        out.reshape(1, LAYERS, 3, 3, C, C),
        dgain[None],
        dshift[None],
        jnp.swapaxes(dhead, 2, 3),
        dbias[0],
        dscale[0],
    )


def solution(mesh):
    return jax.shard_map(
        functools.partial(body, dp=mesh.shape["dp"]),
        mesh=mesh,
        in_specs=(
            P("dp", None, "tower"),
            P(),
            P(),
            P("tower", None, None, None, None, None),
            P("tower", None, None),
            P("tower", None, None),
            P(),
            P(),
            P(),
            P("dp", None, None),
            P("dp", None, None),
            P("dp", None),
        ),
        out_specs=(
            P("dp", None, "tower"),
            P("tower", None, None, None, None, None),
            P("tower", None, None),
            P("tower", None, None),
            P(),
            P(),
            P(),
        ),
        check_vma=False,
    )
```

```python
import functools

import jax
import jax.numpy as jnp
from jax import lax
from jax.experimental import pallas as pl
from jax.experimental.pallas import tpu as pltpu
from jax.sharding import PartitionSpec as P

C = 256
GROUP = 8
CLASSES = 80
HEAD = 85
LANES = 128
LAYERS = 4
CELLS = 1408
PIX = 1364
COUNTS = (1024, 256, 64, 16, 4)
PARTS = ((0, 1024, 64, 64), (1024, 256, 1152, 32), (1280, 128, 1440, 16))
PADDED = 1584
GAPS = ((0, 64), (1088, 64), (1408, 32), (1568, 16))
TILE = 64
BLOCKS = tuple((256 * i, 256, 64 + 256 * i, 64, 0) for i in range(4)) + ((1024, 256, 1152, 32, 1), (1280, 128, 1440, 16, 2))
EPS = 1e-05
f32 = jnp.float32
bf16 = jnp.bfloat16
VMEM = pl.BlockSpec(memory_space=pltpu.VMEM)
SMEM = pl.BlockSpec(memory_space=pltpu.SMEM)
HBM = pl.BlockSpec(memory_space=pltpu.HBM)


VEC = 32
FEATURES, HEADS = 8, 9
COST = 1500000000
COSTS = {
    "write_3_own": 100000000,
    "layer_gradients_2": 3000000000,
    "join_1_6": 1000000000,
    "halve_1_1": 2000000000,
    "write_2_own": 3000000000,
    "join_2_6": 3000000000,
    "halve_0_1": 300000000,
    "feature_gradient": 1000000000,
    "halve_3_1": 1500000000,
    "halve_2_1": 2000000000,
    "write_1_own": 100000000,
    "add_0_4": 1000000000,
    "head_gradients": 1500000000,
    "layer_gradients_1": 5000000000,
    "add_0_3": 5000000000,
    "layer_gradients_0": 2000000000,
    "write_0_got": 3000000000,
    "write_3_got": 1000000,
    "join_3_6": 1000000000,
    "halve_0_2": 1500000000,
    "write_1_got": 2000000000,
    "join_0_5": 1000000,
    "join_1_5": 2000000000,
    "halve_2_2": 2000000000,
    "join_0_6": 3000000000,
    "add_3_4": 300000000,
    "join_3_5": 3000000000,
    "add_1_4": 100000000,
    "halve_3_2": 2000000000,
    "halve_1_2": 1500000000,
}
FIRST_MIB = 32
MIDDLE_MIB = 24
SPLITS = 3


def params(mib=56):
    return pltpu.CompilerParams(vmem_limit_bytes=mib << 20)


def tail_masks():
    row = lax.broadcasted_iota(jnp.int32, (TILE, C), 0)
    third = ((row >= 16) & (row < 24)) | ((row >= 32) & (row < 40))
    fourth = (row >= 26) & (row < 30)
    return third, fourth


def pick(third, fourth, vec):
    return jnp.where(third, vec[3:4], jnp.where(fourth, vec[4:5], 0.0))


def fold(tile):
    return jnp.sum(tile.reshape(TILE // 8, 8, tile.shape[1]), axis=0)


def group_sum(vec):
    lane = lax.broadcasted_iota(jnp.int32, vec.shape, 1)
    for step in (1, 2, 4):
        up = pltpu.roll(vec, vec.shape[1] - step, 1)
        down = pltpu.roll(vec, step, 1)
        vec = vec + jnp.where((lane & step) == 0, up, down)
    return vec


def counts_column():
    row = lax.broadcasted_iota(jnp.int32, (8, C), 0)
    out = jnp.full((8, C), 1.0, f32)
    for level, cells in enumerate(COUNTS):
        out = jnp.where(row == level, 1.0 / (cells * GROUP), out)
    return out


def stack_rows(rows):
    row = lax.broadcasted_iota(jnp.int32, (8, rows[0].shape[1]), 0)
    out = jnp.zeros((8, rows[0].shape[1]), f32)
    for place, value in enumerate(rows):
        out = jnp.where(row == place, jnp.sum(value, axis=0, keepdims=True), out)
    return out


def moved(tile, width):
    row = lax.broadcasted_iota(jnp.int32, (8, tile.shape[1]), 0)
    before, after = pltpu.roll(tile, 1, 0), pltpu.roll(tile, TILE - 1, 0)
    first, last = [], []
    for at in range(0, TILE, 8):
        one, two = before[at : at + 8], after[at : at + 8]
        first.append(jnp.where(row == 0, 0.0, one) if at % width == 0 else one)
        last.append(jnp.where(row == 7, 0.0, two) if (at + 8) % width == 0 else two)
    return jnp.concatenate(first, axis=0), jnp.concatenate(last, axis=0)


def write_shifted(buf, row, width, tile, lanes, flip):
    before, after = moved(tile, width)
    if flip:
        before, after = after, before
    rows = pl.ds(row, TILE)
    buf[rows, 0:lanes] = before.astype(bf16)
    buf[rows, lanes : 2 * lanes] = tile.astype(bf16)
    buf[rows, 2 * lanes : 3 * lanes] = after.astype(bf16)


def clear_gaps(buf):
    for row, rows in GAPS:
        buf[row : row + rows, :] = jnp.zeros((rows, buf.shape[1]), bf16)


def conv_block(block, buf, weight):
    _, cells, row, width, _ = block
    left = jnp.concatenate([buf[row + d * width : row + d * width + cells, :] for d in (-1, 0, 1)], axis=1)
    return jnp.dot(left, weight, preferred_element_type=f32)


def conv_back_block(block, buf, weight):
    _, cells, row, width, _ = block
    total = None
    for i in range(3):
        at = row - (i - 1) * width
        for j in range(3):
            term = lax.dot_general(
                buf[at : at + cells, j * C : (j + 1) * C],
                weight(i * 3 + j),
                (((1,), (1,)), ((), ())),
                preferred_element_type=f32,
            )
            total = term if total is None else total + term
    return total


def kernel_grad(turned, buf, i):
    total = None
    for cell, cells, row, width in PARTS:
        at = row - (i - 1) * width
        term = jnp.dot(turned[:, cell : cell + cells], buf[at : at + cells, :], preferred_element_type=f32)
        total = term if total is None else total + term
    return total


def tiles_of(block):
    cell, cells, row, width, level = block
    return [(level if at == 0 or level < 2 else 3, cell + at, row + at, width, at) for at in range(0, cells, TILE)]


def pipelined(produce, consume, ready=lambda: None):
    produce(BLOCKS[0])
    for i, block in enumerate(BLOCKS):
        if i + 1 < len(BLOCKS):
            produce(BLOCKS[i + 1])
        if i == 0:
            ready()
        consume(block)


class Stats:
    def __init__(self):
        self.center = None
        self.sums = [jnp.zeros((8, C), f32), jnp.zeros((8, C), f32)]
        self.rows = []

    def own(self, tile, cells, mask=None):
        kept = tile if mask is None else jnp.where(mask, tile, 0.0)
        mean = jnp.sum(kept, axis=0, keepdims=True) * (1.0 / cells)
        d = tile - mean
        d = d if mask is None else jnp.where(mask, d, 0.0)
        self.rows.append((mean, jnp.sum(d * d, axis=0, keepdims=True)))

    def add(self, block, z):
        level = block[4]
        if level == 0:
            if self.center is None:
                self.center = jnp.sum(z, axis=0, keepdims=True) * (1.0 / z.shape[0])
            d = z - self.center
            wide = lambda v: jnp.sum(v.reshape(z.shape[0] // 8, 8, C), axis=0)
            self.sums = [self.sums[0] + wide(d), self.sums[1] + wide(d * d)]
        elif level == 1:
            self.own(z, COUNTS[1])
        else:
            third, fourth = tail_masks()
            self.own(z[:TILE], COUNTS[2])
            self.own(z[TILE:], COUNTS[3], third)
            self.own(z[TILE:], COUNTS[4], fourth)

    def finish(self):
        first, second = (jnp.sum(v, axis=0, keepdims=True) for v in self.sums)
        shift = first * (1.0 / COUNTS[0])
        rows = [(self.center + shift, second - first * shift)] + self.rows
        means = stack_rows([r[0] for r in rows])
        squares = stack_rows([r[1] for r in rows])
        inv_counts = counts_column()
        mean = group_sum(means) * (1.0 / GROUP)
        d = means - mean
        var = group_sum(squares * inv_counts + d * d * (1.0 / GROUP))
        return mean, lax.rsqrt(var + EPS)


def level_rows(level, vec, masks):
    if level < 3:
        return vec[level : level + 1]
    return pick(*masks, vec)


def act_tiles(block, z, scale, offset, buf, keep=None):
    masks = tail_masks()
    for level, cell, row, width, _ in tiles_of(block):
        h = z[cell : cell + TILE, :] * level_rows(level, scale, masks) + level_rows(level, offset, masks)
        a = h * jnp.tanh(h) + h
        if level == 3:
            a = jnp.where(masks[0] | masks[1], a, 0.0)
        write_shifted(buf, row, width, a, C, False)
        if keep is not None:
            keep[cell : cell + TILE, :] = a.astype(bf16)


class Upward:
    def __init__(self, dy_out, z, mean, rstd, gain, shift):
        self.dy_out, self.z, self.rstd, self.neg, self.gain, self.shift = dy_out, z, rstd, -mean * rstd, 0.5 * gain, 0.5 * shift
        self.sums = [[jnp.zeros((8, C), f32), jnp.zeros((8, C), f32)] for _ in COUNTS]

    def add(self, block, da):
        masks = tail_masks()
        for level, cell, _, _, at in tiles_of(block):
            zhat = self.z[cell : cell + TILE, :] * level_rows(level, self.rstd, masks) + level_rows(level, self.neg, masks)
            h = zhat * self.gain + self.shift
            t = jnp.tanh(h)
            dy = da[at : at + TILE] * ((1.0 + t) * (1.0 + h * (1.0 - t)))
            self.dy_out[cell : cell + TILE, :] = dy
            dyz = dy * zhat
            if level < 3:
                parts = [(level, dy, dyz)]
            else:
                parts = [(3 + k, jnp.where(m, dy, 0.0), jnp.where(m, dyz, 0.0)) for k, m in enumerate(masks)]
            for to, one, two in parts:
                self.sums[to] = [self.sums[to][0] + fold(one), self.sums[to][1] + fold(two)]

    def finish(self, sums_out):
        sums_out[0:8, :] = 0.5 * stack_rows([v[0] for v in self.sums])
        sums_out[8:16, :] = 0.5 * stack_rows([v[1] for v in self.sums])


def norm_back(dy, z, mean, rstd, gain, sums, buf):
    sum_dy, sum_dyz = sums[0:8, :], sums[8:16, :]
    inv_counts = counts_column()
    mean_e = group_sum(sum_dy * gain) * inv_counts
    mean_ez = group_sum(sum_dyz * gain) * inv_counts
    on_dy = 0.5 * rstd * gain
    on_zhat = rstd * mean_ez
    on_z = -on_zhat * rstd
    flat = on_zhat * mean * rstd - rstd * mean_e

    def produce(block):
        masks = tail_masks()
        for level, cell, row, width, _ in tiles_of(block):
            at = slice(cell, cell + TILE)
            dz = (
                dy[at, :] * level_rows(level, on_dy, masks)
                + z[at, :] * level_rows(level, on_z, masks)
                + level_rows(level, flat, masks)
            )
            write_shifted(buf, row, width, dz, C, True)

    return produce, [jnp.sum(v, axis=0, keepdims=True) for v in (sum_dyz, sum_dy)]


def center(buf, cells, row, lanes):
    return buf[row : row + cells, lanes : 2 * lanes]


def shape(dims, dtype):
    return jax.ShapeDtypeStruct(dims, dtype)


def pack(vec):
    high = vec.astype(bf16).astype(f32)
    middle = (vec - high).astype(bf16).astype(f32)
    low = vec - high - middle
    return jnp.concatenate([high, middle, low, jnp.zeros_like(vec)], axis=0).astype(bf16)


def unpack(block):
    parts = block.astype(f32)
    return parts[0:8] + parts[8:16] + parts[16:24]


def bit_of(order, step):
    dp = lax.axis_index("dp")
    return jnp.where(lax.axis_index("tower") == 0, dp >> order[0][step], dp >> order[1][step]) & 1


def call(kernel, token, ins, in_specs, outs, out_specs, name, scratch=(), mib=16, alias=None):
    n_in, n_out = len(ins), len(outs)

    def ordered(*refs):
        kernel(*refs[:n_in], *refs[n_in + 1 : n_in + 1 + n_out], *refs[n_in + n_out + 2 :])

    *results, token = pl.pallas_call(
        ordered,
        out_shape=list(outs) + [shape((8, LANES), f32)],
        in_specs=list(in_specs) + [HBM],
        out_specs=list(out_specs) + [HBM],
        scratch_shapes=list(scratch),
        input_output_aliases=alias or {},
        compiler_params=params(mib),
        cost_estimate=pl.CostEstimate(flops=COSTS.get(name, COST), bytes_accessed=1, transcendentals=0),
        name=name,
    )(*ins, token)
    return results, token


def split_store(bit, tap, grad, keep, send):
    half = C // 2
    low, high = grad[:half], grad[half:]
    keep[tap * half : (tap + 1) * half, :] = jnp.where(bit == 1, high, low).astype(bf16)
    send[tap * half : (tap + 1) * half, :] = jnp.where(bit == 1, low, high).astype(bf16)


def halve_kernel(taps, rows, order, step, keep, got, vec, keep_out, send_out, vec_out):
    bit = bit_of(order, step)
    half = rows // 2

    def one(t, _):
        for out, side in ((keep_out, bit), (send_out, 1 - bit)):
            at = pl.ds(pl.multiple_of(t * rows + side * half, half), half)
            to = pl.ds(pl.multiple_of(t * half, half), half)
            out[to, :] = (keep[at, :].astype(f32) + got[at, :].astype(f32)).astype(bf16)
        return 0

    lax.fori_loop(0, taps, one, 0)
    total = vec[...] + unpack(got[taps * rows :, :])
    vec_out[...] = total
    send_out[taps * half :, :] = pack(total)


def add_kernel(taps, rows, keep, got, vec, sum_out, vec_out):
    def one(t, _):
        at = pl.ds(pl.multiple_of(t * rows, rows), rows)
        sum_out[at, :] = (keep[at, :].astype(f32) + got[at, :].astype(f32)).astype(bf16)
        return 0

    lax.fori_loop(0, taps, one, 0)
    total = vec[...] + unpack(got[taps * rows :, :])
    vec_out[...] = total
    sum_out[taps * rows :, :] = pack(total)


def join_kernel(taps, rows, order, step, own, got, out):
    bit = bit_of(order, step)

    def one(t, _):
        at = pl.ds(pl.multiple_of(t * rows, rows), rows)
        out[pl.ds(pl.multiple_of((2 * t + bit) * rows, rows), rows), :] = own[at, :]
        out[pl.ds(pl.multiple_of((2 * t + 1 - bit) * rows, rows), rows), :] = got[at, :]
        return 0

    lax.fori_loop(0, taps, one, 0)


def write_half(layer, side, half_rows, out, wide, sems):
    half = C // 2
    copies = []
    for t in range(9):
        rows = slice(t * half, (t + 1) * half)
        wide[rows, :] = half_rows[rows, :].astype(f32)
        to = pl.multiple_of((layer * 9 + t) * C + side * half, half)
        copies.append(pltpu.make_async_copy(wide.at[rows], out.at[pl.ds(to, half)], sems.at[t]))
        copies[-1].start()
    return copies


def write_own_kernel(layer, order, own, *refs):
    out, wide, sems = refs[-3 - (2 if not layer else 0) :][:1] + refs[-2:]
    copies = write_half(layer, bit_of(order, 0), own, out, wide, sems)
    if not layer:
        vecs, (gains_out, shifts_out) = refs[:LAYERS], refs[-4:-2]
        gains_out[...] = jnp.concatenate([v[0:1, :] for v in vecs], axis=0)
        shifts_out[...] = jnp.concatenate([v[1:2, :] for v in vecs], axis=0)
    for copy in copies:
        copy.wait()


def write_got_kernel(layer, order, extra, got, *refs):
    bit = bit_of(order, 0)
    out, wide, sems = refs[-3 - (1 if extra else 0) :][:1] + refs[-2:]
    copies = write_half(layer, 1 - bit, got, out, wide, sems)
    half = C // 2
    if extra:
        own, vec, _, _, rest, _, _ = refs
        for t in range(extra):
            rest[pl.ds(pl.multiple_of(t * C + bit * half, half), half), :] = own[(9 + t) * half : (10 + t) * half, :]
            rest[pl.ds(pl.multiple_of(t * C + (1 - bit) * half, half), half), :] = got[(9 + t) * half : (10 + t) * half, :]
        rest[extra * C :, :] = pack(vec[...])
    for copy in copies:
        copy.wait()


def heads_kernel(own, got, vec, dhead_out, bias_out, scale_out):
    for i in range(3):
        at = slice(i * C, (i + 1) * C)
        turned = (own[at, :].astype(f32) + got[at, :].astype(f32)).T
        for j in range(3):
            dhead_out[i, j] = turned[j * HEAD : (j + 1) * HEAD, :]
    both = vec[...] + unpack(got[3 * C :, :])
    bias_out[...] = both[2:3, 0:HEAD]
    lane = lax.broadcasted_iota(jnp.int32, (8, LANES), 1)
    row = lax.broadcasted_iota(jnp.int32, (8, LANES), 0)
    sums = jnp.sum(both[:, 0:LANES], axis=1, keepdims=True)
    line = jnp.sum(jnp.where((row >= 3) & (lane == row - 3), sums, 0.0), axis=0, keepdims=True)
    scale_out[...] = line[:, 0 : len(COUNTS)]


def features_kernel(keep, got, var, out):
    half = C // 2
    inverse = lax.rsqrt(jnp.where(lax.axis_index("tower") == 0, var[:, :half], var[:, half:]) + EPS)

    def scaled(cell, cells):
        return (keep[pl.ds(cell, cells), :].astype(f32) + got[pl.ds(cell, cells), :].astype(f32)) * inverse

    def one(t, _):
        at = pl.multiple_of(t * TILE, TILE)
        out[pl.ds(at, TILE), :] = scaled(at, TILE).astype(bf16)
        return 0

    lax.fori_loop(0, 1344 // TILE, one, 0)
    tail = scaled(1344, TILE)
    out[1344:PIX, :] = jnp.concatenate([tail[16:24], tail[32:40], tail[26:30]], axis=0).astype(bf16)


def gradients_out(bit, turned, buf, keep, send):
    for i in range(3):
        grad = kernel_grad(turned, buf, i)
        for j in range(3):
            split_store(bit, i * 3 + j, grad[:, j * C : (j + 1) * C], keep, send)


def vector_rows(rows):
    row = lax.broadcasted_iota(jnp.int32, (8, C), 0)
    out = jnp.zeros((8, C), f32)
    for at, value in enumerate(rows):
        out = jnp.where(row == at, value, out)
    return out


def spread_tail(tile, scratch):
    scratch[...] = jnp.zeros(scratch.shape, f32)
    scratch[16:24, :] = tile[0:8]
    scratch[32:40, :] = tile[8:16]
    scratch[26:30, :] = tile[16:20]


class Heads:
    def __init__(self, hg, hk, hbuf, bias, scale):
        self.hg, self.hk, self.hbuf, self.scale = hg, hk, hbuf, scale
        self.bias = jnp.concatenate([bias[...], jnp.zeros((1, LANES - HEAD), f32)], axis=1)
        self.total = jnp.zeros((8, LANES), f32)
        self.scales = [jnp.zeros((8, LANES), f32) for _ in COUNTS]

    def add(self, block, buf):
        _, cells, first, width, _ = block
        raw_block = None
        for i in range(3):
            at = first + (i - 1) * width
            for j in range(3):
                tap = (i * 3 + j) * LANES
                term = lax.dot_general(
                    buf[at : at + cells, j * C : (j + 1) * C],
                    self.hk[tap : tap + LANES, :],
                    (((1,), (1,)), ((), ())),
                    preferred_element_type=f32,
                )
                raw_block = term if raw_block is None else raw_block + term
        lane = lax.broadcasted_iota(jnp.int32, (TILE, LANES), 1)
        dist = (lane >= CLASSES) & (lane < CLASSES + 4) & (lax.axis_index("tower") == 1)
        third, fourth = (m[:, :LANES] for m in tail_masks())
        for level, cell, row, width, at in tiles_of(block):
            raw = raw_block[at : at + TILE] + self.bias
            g = self.hg[cell : cell + TILE, :]
            if level < 3:
                ls, use = self.scale[0:1, level : level + 1], dist
            else:
                ls = jnp.where(third, self.scale[0:1, 3:4], self.scale[0:1, 4:5])
                use = dist & (third | fourth)
            weighted = jnp.where(use, g * jnp.exp(ls * raw), 0.0)
            term = weighted * raw
            parts = [(level, term)] if level < 3 else [(3, jnp.where(third, term, 0.0)), (4, jnp.where(fourth, term, 0.0))]
            for to, value in parts:
                self.scales[to] = self.scales[to] + fold(value)
            tile = jnp.where(dist, weighted * ls, g).astype(bf16).astype(f32)
            self.total = self.total + fold(tile)
            after, before = moved(tile, width)
            middle = pltpu.roll(tile, HEAD, 1)
            after = pltpu.roll(after, 2 * HEAD - LANES, 1)
            rows = slice(row, row + TILE)
            self.hbuf[rows, 0:LANES] = jnp.where(lane < HEAD, before, middle).astype(bf16)
            self.hbuf[rows, LANES : 2 * LANES] = jnp.where(lane < 2 * HEAD - LANES, middle, after).astype(bf16)

    def rows(self):
        return [jnp.sum(v, axis=0, keepdims=True) for v in [self.total] + self.scales]


def prepare_kernel(head, cls, reg, pos, hw, hk, hg, tail):
    box = reg[...].astype(f32) * pos[...].astype(f32)
    is_class = lax.axis_index("tower") == 0
    rows = jnp.concatenate(
        [
            jnp.where(is_class, cls[...].astype(f32), 0.0),
            jnp.where(is_class, 0.0, jnp.concatenate([box, jnp.zeros((3, PIX), f32)], axis=0)),
            jnp.zeros((LANES - CLASSES - 8, PIX), f32),
        ],
        axis=0,
    )
    rows = jnp.concatenate([rows, jnp.zeros((LANES, CELLS - PIX), f32)], axis=1)
    hg[...] = rows.T
    spread_tail(jnp.concatenate([hg[1344:PIX, :]] * 2, axis=1), tail)
    hg[1344:CELLS, :] = tail[:, 0:LANES]
    for i in range(3):
        three = jnp.concatenate([head[i, j].astype(f32) for j in range(3)] + [jnp.zeros((1, C), f32)], axis=0)
        hw[i * C : (i + 1) * C, :] = three.astype(bf16)
        for j in range(3):
            one = jnp.concatenate([head[i, j].astype(f32), jnp.zeros((LANES - HEAD, C), f32)], axis=0)
            hk[(i * 3 + j) * LANES : (i * 3 + j + 1) * LANES, :] = one.astype(bf16)


def first_kernel(
    order, scale, own, other, bn_mean, bn_var, w_hbm, gains, shifts, head_bias, hw, hk, hg,
    w, z_out, a_out, stats_out, dy_out, sums_out, keep_out, send_out, vec_out,
    buf, z_last, a_last, dy, sums, hbuf, turned, tail, sems,
):
    loads = [pltpu.make_async_copy(w_hbm.at[l], w.at[l], sems.at[l]) for l in range(LAYERS)]
    for load in loads:
        load.start()
    half = C // 2
    tower = lax.axis_index("tower")
    clear_gaps(buf)
    clear_gaps(hbuf)
    inverse = lax.rsqrt(bn_var[...] + EPS)
    mean0 = bn_mean[...]

    def halves(rows):
        left = jnp.where(tower == 0, own[rows, :].astype(f32), other[rows, :].astype(f32))
        right = jnp.where(tower == 0, other[rows, :].astype(f32), own[rows, :].astype(f32))
        return (jnp.concatenate([left, right], axis=1) - mean0) * inverse

    def base(block):
        for level, cell, row, width, _ in tiles_of(block):
            if level < 3:
                tile = halves(slice(cell, cell + TILE))
            else:
                spread_tail(halves(slice(1344, PIX)), tail)
                tile = tail[...]
            write_shifted(buf, row, width, tile, C, False)
            a_out[0, cell : cell + TILE, :] = tile.astype(bf16)

    scale_rows = offset_rows = None
    for l in range(LAYERS):
        z = z_out.at[l] if l < LAYERS - 1 else z_last
        stats = Stats()

        def consume(block, l=l, z=z, stats=stats):
            out = conv_block(block, buf, w[l])
            z[block[0] : block[0] + block[1], :] = out
            stats.add(block, out)

        if l == 0:
            produce = base
        else:
            keep = a_out.at[l] if l < LAYERS - 1 else a_last
            before = z_out.at[l - 1]
            produce = lambda block: act_tiles(block, before, scale_rows, offset_rows, buf, keep)
        pipelined(produce, consume, loads[l].wait)
        mean, rstd = stats.finish()
        if l < LAYERS - 1:
            stats_out[l, 0:8, :] = mean
            stats_out[l, 8:16, :] = rstd
        scale_rows = 0.5 * rstd * gains[l : l + 1]
        offset_rows = 0.5 * shifts[l : l + 1] - mean * scale_rows
    l = LAYERS - 1
    heads = Heads(hg, hk, hbuf, head_bias, scale)
    up = Upward(dy, z_last, mean, rstd, gains[l : l + 1], shifts[l : l + 1])
    for i in range(len(BLOCKS) + 2):
        if i < len(BLOCKS):
            act_tiles(BLOCKS[i], z_last, scale_rows, offset_rows, buf)
        if 1 <= i <= len(BLOCKS):
            heads.add(BLOCKS[i - 1], buf)
        if i >= 2:
            _, cells, row, width, _ = BLOCKS[i - 2]
            left = jnp.concatenate([hbuf[row - d * width : row - d * width + cells, :] for d in (-1, 0, 1)], axis=1)
            up.add(BLOCKS[i - 2], jnp.dot(left, hw[...], preferred_element_type=f32))
    up.finish(sums)
    bit = bit_of(order, 0)
    a4t = jnp.concatenate([center(buf, n, r, C).T for _, n, r, _ in PARTS], axis=1)
    for i in range(3):
        split_store(bit, 9 + i, kernel_grad(a4t, hbuf, i), keep_out, send_out)
    produce, norm_sums = norm_back(dy, z_last, mean, rstd, gains[l : l + 1], sums, buf)
    wide = lambda v: jnp.concatenate([v, jnp.zeros_like(v)], axis=1)
    vec = vector_rows(norm_sums + [wide(row) for row in heads.rows()])
    vec_out[...] = vec
    send_out[12 * half :, :] = pack(vec)
    turned[...] = a_last[...].T
    layer_down(l, produce, buf, lambda tap: w[l, tap * C : (tap + 1) * C, :], z_out, stats_out, gains, shifts, dy_out, sums_out)
    gradients_out(bit, turned, buf, keep_out, send_out)


def layer_down(l, produce, buf, weight, z, stats, gains, shifts, dy_out, sums_out):
    k = l - 1
    up = Upward(dy_out, z.at[k], stats[k, 0:8, :], stats[k, 8:16, :], gains[k : k + 1], shifts[k : k + 1])
    pipelined(produce, lambda block: up.add(block, conv_back_block(block, buf, weight)))
    up.finish(sums_out)


def middle_kernel(l, order, dy, sums, z, a, stats, gains, shifts, w, *refs):
    if l:
        dy_out, sums_out, keep_out, send_out, vec_out, buf, turned = refs
    else:
        keep_half, send_half, keep_out, send_out, vec_out, buf, turned = refs
    half = C // 2
    bit = bit_of(order, 0)
    clear_gaps(buf)
    produce, norm_sums = norm_back(
        dy, z.at[l], stats[l, 0:8, :], stats[l, 8:16, :], gains[l : l + 1], sums, buf
    )
    vec = vector_rows(norm_sums)
    vec_out[...] = vec
    send_out[9 * half :, :] = pack(vec)
    turned[...] = a[l].T
    weight = lambda tap: w[l, tap * C : (tap + 1) * C, :]
    if l:
        layer_down(l, produce, buf, weight, z, stats, gains, shifts, dy_out, sums_out)
    else:
        mine = lax.axis_index("tower")

        def consume(block):
            da = conv_back_block(block, buf, weight)
            at = slice(block[0], block[0] + block[1])
            keep_half[at, :] = jnp.where(mine == 0, da[:, :half], da[:, half:])
            send_half[at, :] = jnp.where(mine == 0, da[:, half:], da[:, :half]).astype(bf16)

        pipelined(produce, consume)
    gradients_out(bit, turned, buf, keep_out, send_out)


def run_prepare(token, head, cls, reg, pos):
    return call(
        prepare_kernel,
        token,
        (head, cls, reg, pos),
        [VMEM] * 4,
        [pltpu.VMEM((3 * C, C), bf16), pltpu.VMEM((9 * LANES, C), bf16), pltpu.VMEM((CELLS, LANES), f32)],
        [VMEM] * 3,
        "prepare",
        [pltpu.VMEM((TILE, C), f32)],
        16,
    )


def run_first(order, token, scale, own, other, mean, var, w, gains, shifts, bias, hw, hk, hg):
    half = C // 2
    return call(
        functools.partial(first_kernel, order),
        token,
        (scale, own, other, mean, var, w, gains, shifts, bias, hw, hk, hg),
        [VMEM] * 5 + [HBM] + [VMEM] * 6,
        [
            pltpu.VMEM((LAYERS, 9 * C, C), bf16),
            pltpu.VMEM((LAYERS - 1, CELLS, C), f32),
            pltpu.VMEM((LAYERS - 1, CELLS, C), bf16),
            pltpu.VMEM((LAYERS - 1, 16, C), f32),
            pltpu.VMEM((CELLS, C), f32),
            pltpu.VMEM((16, C), f32),
            pltpu.VMEM((12 * half, C), bf16),
            pltpu.VMEM((12 * half + VEC, C), bf16),
            pltpu.VMEM((8, C), f32),
        ],
        [VMEM] * 9,
        "forward_and_heads",
        [
            pltpu.VMEM((PADDED, 3 * C), bf16),
            pltpu.VMEM((CELLS, C), f32),
            pltpu.VMEM((CELLS, C), bf16),
            pltpu.VMEM((CELLS, C), f32),
            pltpu.VMEM((16, C), f32),
            pltpu.VMEM((PADDED, 2 * LANES), bf16),
            pltpu.VMEM((C, CELLS), bf16),
            pltpu.VMEM((TILE, C), f32),
            pltpu.SemaphoreType.DMA((LAYERS,)),
        ],
        FIRST_MIB,
    )


def run_middle(l, order, token, dy, sums, z, a, stats, gains, shifts, w):
    half = C // 2
    outs = [shape((CELLS, C), f32), shape((16, C), f32)] if l else [shape((CELLS, half), f32), shape((CELLS, half), bf16)]
    outs += [shape((9 * half, C), bf16), shape((9 * half + VEC, C), bf16), shape((8, C), f32)]
    scratch = [
        pltpu.VMEM((PADDED, 3 * C), bf16),
        pltpu.VMEM((C, CELLS), bf16),
    ]
    return call(
        functools.partial(middle_kernel, l, order),
        token,
        (dy, sums, z, a, stats, gains, shifts, w),
        [VMEM] * 8,
        outs,
        [VMEM] * len(outs),
        f"layer_gradients_{l}",
        scratch,
        MIDDLE_MIB,
    )


class Sum:
    def __init__(self, layer, taps, order, bits, keep, send, vec):
        self.layer, self.taps, self.order, self.bits = layer, taps, order, bits
        self.keep, self.vec = keep, vec
        self.splits = min(SPLITS, bits)
        self.rows = C // 2
        self.steps = bits + self.splits - 1
        self.got = self.partner(send, 0)

    def partner(self, value, step):
        pairs = []
        for d in range(1 << self.bits):
            for t in range(2):
                pairs.append((2 * d + t, 2 * (d ^ (1 << self.order[t][step])) + t))
        return lax.ppermute(value, ("dp", "tower"), pairs)

    def advance(self, step, token):
        taps, rows = self.taps, self.rows
        self.done = step
        vec = shape((8, C), f32)
        if step < self.splits:
            half = rows // 2
            (self.keep, send, self.vec), token = call(
                functools.partial(halve_kernel, taps, rows, self.order, step),
                token, (self.keep, self.got, self.vec), [VMEM] * 3,
                [shape((taps * half, C), bf16), shape((taps * half + VEC, C), bf16), vec], [VMEM] * 3,
                f"halve_{self.layer}_{step}",
            )
            self.rows = half
            bit = step
        elif step <= self.bits:
            (send, self.vec), token = call(
                functools.partial(add_kernel, taps, rows),
                token, (self.keep, self.got, self.vec), [VMEM] * 3,
                [shape((taps * rows + VEC, C), bf16), vec], [VMEM] * 2,
                f"add_{self.layer}_{step}",
            )
            self.keep = send
            bit = step if step < self.bits else self.splits - 1
        else:
            bit = self.steps - step
            (send,), token = call(
                functools.partial(join_kernel, taps, rows, self.order, bit + 1),
                token, (self.keep, self.got), [VMEM] * 2,
                [shape((taps * 2 * rows, C), bf16)], [VMEM],
                f"join_{self.layer}_{step}",
            )
            self.keep = send
            self.rows = 2 * rows
        self.got = self.partner(send, bit)
        return token

    def finish(self, token, out, own, vecs):
        extra = 0 if own else self.taps - 9
        outs, out_specs = [shape((LAYERS * 9 * C, C), f32)], [HBM]
        ins, specs = [self.keep if own else self.got], [VMEM]
        if extra:
            ins, specs = ins + [self.keep, self.vec], specs + [VMEM] * 2
            outs.append(shape((extra * C + VEC, C), bf16))
            out_specs.append(VMEM)
        elif own and not self.layer:
            ins, specs = ins + vecs, specs + [VMEM] * LAYERS
            outs += [shape((LAYERS, C), f32)] * 2
            out_specs += [VMEM] * 2
        alias = {}
        if out is not None:
            alias = {len(ins): 0}
            ins, specs = ins + [out], specs + [HBM]
        if own:
            kernel = functools.partial(write_own_kernel, self.layer, self.order)
        else:
            kernel = functools.partial(write_got_kernel, self.layer, self.order, extra)
        return call(
            kernel, token, ins, specs, outs, out_specs, f"write_{self.layer}_{'own' if own else 'got'}",
            [pltpu.VMEM((9 * C // 2, C), f32), pltpu.SemaphoreType.DMA((9,))], 16, alias,
        )


TIMELINE = (
    (2, 0), (1, 0), (3, 1), (0, 0), (2, 1), (3, 2), (2, 2), (3, 3), (1, 1), (0, 1), (3, 4), (2, 3),
    (1, 2), (3, 5), (0, 2), (2, 4), (1, 3), (0, 3), (3, 6), (1, 4), (2, 5), (0, 4), (1, 5), (3, 7),
    (0, 5), (2, 6), (3, 8), (1, 6), (8, 0), (0, 6), (9, 0), (0, 7), (1, 7), (2, 7), (2, 8), (1, 8),
    (0, 8),
)
ORDERS = (
    ((2, 0, 1, 3), (0, 1, 2, 3)),
    ((0, 2, 1, 3), (1, 0, 2, 3)),
    ((1, 2, 0, 3), (2, 0, 1, 3)),
    ((0, 2, 1, 3), (1, 0, 2, 3)),
)


def orders(bits):
    if bits == 4:
        return ORDERS
    line = tuple(range(bits))
    return (((line, line[1:] + line[:1]),) * LAYERS)


def timeline(bits, steps):
    if bits == 4:
        return TIMELINE
    late = [(l, step) for step in range(1, steps + 3) for l in (3, 2, 1, 0)]
    return [(2, 0), (1, 0), (0, 0)] + late + [(FEATURES, 0), (HEADS, 0)]


def body(
    features, bn_mean, bn_var, tower_weight, norm_gain, norm_bias, head_weight, head_bias, level_scale,
    cls_cot, reg_cot, positive, *, dp,
):
    bits = dp.bit_length() - 1
    assert dp == 1 << bits and bits >= 1
    order = orders(bits)
    in_hbm = lambda v: pltpu.with_memory_space_constraint(v, pltpu.HBM)
    own = features[0]
    swap = [(0, 1), (1, 0)]
    other = lax.ppermute(own, "tower", swap)
    w = in_hbm(tower_weight[0].reshape(LAYERS, 9 * C, C))
    gains, shifts = in_hbm(norm_gain[0]), in_hbm(norm_bias[0])
    mean, var = in_hbm(bn_mean[None]), in_hbm(bn_var[None])
    head = in_hbm(jnp.swapaxes(head_weight, 2, 3))
    (hw, hk, hg), token = run_prepare(
        mean, head, in_hbm(jnp.swapaxes(cls_cot[0], 0, 1)), in_hbm(jnp.swapaxes(reg_cot[0], 0, 1)), in_hbm(positive)
    )
    (w, z, a, stats, dy, dy_sums, keep, send, vec), token = run_first(
        order[3], token, in_hbm(level_scale[None]), in_hbm(own), other, mean, var, w, gains, shifts,
        in_hbm(head_bias[None]), hw, hk, hg,
    )
    sums = [None] * LAYERS
    sums[3] = Sum(3, 12, order[3], bits, keep, send, vec)
    out = None
    for l, step in timeline(bits, sums[3].steps):
        if l == FEATURES:
            (feature_grad,), token = call(
                features_kernel, token, (keep_half, got_half, var), [VMEM] * 3,
                [shape((PIX, C // 2), bf16)], [VMEM], "feature_gradient",
            )
        elif l == HEADS:
            (dhead, dbias, dscale), token = call(
                heads_kernel, token, (heads, got_heads, sums[3].vec), [VMEM] * 3,
                [shape((3, 3, HEAD, C), f32), shape((1, HEAD), f32), shape((1, len(COUNTS)), f32)], [VMEM] * 3,
                "head_gradients",
            )
        elif step == 0:
            (*grads, keep, send, vec), token = run_middle(l, order[l], token, dy, dy_sums, z, a, stats, gains, shifts, w)
            sums[l] = Sum(l, 9, order[l], bits, keep, send, vec)
            if l:
                dy, dy_sums = grads
            else:
                keep_half, send_half = grads
                got_half = lax.ppermute(send_half, "tower", swap)
        elif step <= sums[l].steps:
            token = sums[l].advance(step, token)
        elif step == sums[l].steps + 1:
            assert l or all(one.done >= bits for one in sums)
            (out, *more), token = sums[l].finish(token, out, True, [one.vec for one in sums])
            if l == 0:
                dgain, dshift = more
        else:
            (out, *more), token = sums[l].finish(token, out, False, None)
            if l == 3:
                (heads,) = more
                got_heads = lax.ppermute(heads, "tower", swap)
    return (
        feature_grad[None],
        out.reshape(1, LAYERS, 3, 3, C, C),
        dgain[None],
        dshift[None],
        jnp.swapaxes(dhead, 2, 3),
        dbias[0],
        dscale[0],
    )


def solution(mesh):
    return jax.shard_map(
        functools.partial(body, dp=mesh.shape["dp"]),
        mesh=mesh,
        in_specs=(
            P("dp", None, "tower"),
            P(),
            P(),
            P("tower", None, None, None, None, None),
            P("tower", None, None),
            P("tower", None, None),
            P(),
            P(),
            P(),
            P("dp", None, None),
            P("dp", None, None),
            P("dp", None),
        ),
        out_specs=(
            P("dp", None, "tower"),
            P("tower", None, None, None, None, None),
            P("tower", None, None),
            P("tower", None, None),
            P(),
            P(),
            P(),
        ),
        check_vma=False,
    )
```

```python
import functools

import jax
import jax.numpy as jnp
from jax import lax
from jax.experimental import pallas as pl
from jax.experimental.pallas import tpu as pltpu
from jax.sharding import PartitionSpec as P

C = 256
GROUP = 8
CLASSES = 80
HEAD = 85
LANES = 128
LAYERS = 4
CELLS = 1408
PIX = 1364
COUNTS = (1024, 256, 64, 16, 4)
PARTS = ((0, 1024, 64, 64), (1024, 256, 1152, 32), (1280, 128, 1440, 16))
PADDED = 1584
GAPS = ((0, 64), (1088, 64), (1408, 32), (1568, 16))
TILE = 64
BLOCKS = tuple((256 * i, 256, 64 + 256 * i, 64, 0) for i in range(4)) + ((1024, 256, 1152, 32, 1), (1280, 128, 1440, 16, 2))
EPS = 1e-05
f32 = jnp.float32
bf16 = jnp.bfloat16
VMEM = pl.BlockSpec(memory_space=pltpu.VMEM)
SMEM = pl.BlockSpec(memory_space=pltpu.SMEM)
HBM = pl.BlockSpec(memory_space=pltpu.HBM)


VEC = 32
FEATURES, HEADS = 8, 9
COST = 1500000000
COSTS = {
    "write_3_own": 100000000,
    "layer_gradients_2": 3000000000,
    "join_1_6": 1000000000,
    "halve_1_1": 2000000000,
    "write_2_own": 3000000000,
    "join_2_6": 3000000000,
    "halve_0_1": 300000000,
    "feature_gradient": 1000000000,
    "halve_3_1": 1500000000,
    "halve_2_1": 2000000000,
    "write_1_own": 100000000,
    "add_0_4": 1000000000,
    "head_gradients": 1500000000,
    "layer_gradients_1": 5000000000,
    "add_0_3": 5000000000,
    "layer_gradients_0": 2000000000,
    "write_0_got": 3000000000,
    "write_3_got": 1000000,
    "join_3_6": 1000000000,
    "halve_0_2": 1500000000,
    "write_1_got": 2000000000,
    "join_0_5": 1000000,
    "join_1_5": 2000000000,
    "halve_2_2": 2000000000,
    "join_0_6": 3000000000,
    "add_3_4": 300000000,
    "join_3_5": 3000000000,
    "add_1_4": 100000000,
    "halve_3_2": 2000000000,
    "halve_1_2": 1500000000,
}
FIRST_MIB = 32
MIDDLE_MIB = 24
SPLITS = 3


def params(mib=56):
    return pltpu.CompilerParams(vmem_limit_bytes=mib << 20)


def tail_masks():
    row = lax.broadcasted_iota(jnp.int32, (TILE, C), 0)
    third = ((row >= 16) & (row < 24)) | ((row >= 32) & (row < 40))
    fourth = (row >= 26) & (row < 30)
    return third, fourth


def pick(third, fourth, vec):
    return jnp.where(third, vec[3:4], jnp.where(fourth, vec[4:5], 0.0))


def fold(tile):
    return jnp.sum(tile.reshape(TILE // 8, 8, tile.shape[1]), axis=0)


def group_sum(vec):
    lane = lax.broadcasted_iota(jnp.int32, vec.shape, 1)
    for step in (1, 2, 4):
        up = pltpu.roll(vec, vec.shape[1] - step, 1)
        down = pltpu.roll(vec, step, 1)
        vec = vec + jnp.where((lane & step) == 0, up, down)
    return vec


def counts_column():
    row = lax.broadcasted_iota(jnp.int32, (8, C), 0)
    out = jnp.full((8, C), 1.0, f32)
    for level, cells in enumerate(COUNTS):
        out = jnp.where(row == level, 1.0 / (cells * GROUP), out)
    return out


def stack_rows(rows):
    row = lax.broadcasted_iota(jnp.int32, (8, rows[0].shape[1]), 0)
    out = jnp.zeros((8, rows[0].shape[1]), f32)
    for place, value in enumerate(rows):
        out = jnp.where(row == place, jnp.sum(value, axis=0, keepdims=True), out)
    return out


def moved(tile, width):
    row = lax.broadcasted_iota(jnp.int32, (8, tile.shape[1]), 0)
    before, after = pltpu.roll(tile, 1, 0), pltpu.roll(tile, TILE - 1, 0)
    first, last = [], []
    for at in range(0, TILE, 8):
        one, two = before[at : at + 8], after[at : at + 8]
        first.append(jnp.where(row == 0, 0.0, one) if at % width == 0 else one)
        last.append(jnp.where(row == 7, 0.0, two) if (at + 8) % width == 0 else two)
    return jnp.concatenate(first, axis=0), jnp.concatenate(last, axis=0)


def write_shifted(buf, row, width, tile, lanes, flip):
    before, after = moved(tile, width)
    if flip:
        before, after = after, before
    rows = pl.ds(row, TILE)
    buf[rows, 0:lanes] = before.astype(bf16)
    buf[rows, lanes : 2 * lanes] = tile.astype(bf16)
    buf[rows, 2 * lanes : 3 * lanes] = after.astype(bf16)


def clear_gaps(buf):
    for row, rows in GAPS:
        buf[row : row + rows, :] = jnp.zeros((rows, buf.shape[1]), bf16)


def conv_block(block, buf, weight):
    _, cells, row, width, _ = block
    left = jnp.concatenate([buf[row + d * width : row + d * width + cells, :] for d in (-1, 0, 1)], axis=1)
    return jnp.dot(left, weight, preferred_element_type=f32)


def conv_back_block(block, buf, weight):
    _, cells, row, width, _ = block
    total = None
    for i in range(3):
        at = row - (i - 1) * width
        for j in range(3):
            term = lax.dot_general(
                buf[at : at + cells, j * C : (j + 1) * C],
                weight(i * 3 + j),
                (((1,), (1,)), ((), ())),
                preferred_element_type=f32,
            )
            total = term if total is None else total + term
    return total


def kernel_grad(turned, buf, i):
    total = None
    for cell, cells, row, width in PARTS:
        at = row - (i - 1) * width
        term = jnp.dot(turned[:, cell : cell + cells], buf[at : at + cells, :], preferred_element_type=f32)
        total = term if total is None else total + term
    return total


def tiles_of(block):
    cell, cells, row, width, level = block
    return [(level if at == 0 or level < 2 else 3, cell + at, row + at, width, at) for at in range(0, cells, TILE)]


def pipelined(produce, consume, ready=lambda: None):
    produce(BLOCKS[0])
    for i, block in enumerate(BLOCKS):
        if i + 1 < len(BLOCKS):
            produce(BLOCKS[i + 1])
        if i == 0:
            ready()
        consume(block)


class Stats:
    def __init__(self):
        self.center = None
        self.sums = [jnp.zeros((8, C), f32), jnp.zeros((8, C), f32)]
        self.rows = []

    def own(self, tile, cells, mask=None):
        kept = tile if mask is None else jnp.where(mask, tile, 0.0)
        mean = jnp.sum(kept, axis=0, keepdims=True) * (1.0 / cells)
        d = tile - mean
        d = d if mask is None else jnp.where(mask, d, 0.0)
        self.rows.append((mean, jnp.sum(d * d, axis=0, keepdims=True)))

    def add(self, block, z):
        level = block[4]
        if level == 0:
            if self.center is None:
                self.center = jnp.sum(z, axis=0, keepdims=True) * (1.0 / z.shape[0])
            d = z - self.center
            wide = lambda v: jnp.sum(v.reshape(z.shape[0] // 8, 8, C), axis=0)
            self.sums = [self.sums[0] + wide(d), self.sums[1] + wide(d * d)]
        elif level == 1:
            self.own(z, COUNTS[1])
        else:
            third, fourth = tail_masks()
            self.own(z[:TILE], COUNTS[2])
            self.own(z[TILE:], COUNTS[3], third)
            self.own(z[TILE:], COUNTS[4], fourth)

    def finish(self):
        first, second = (jnp.sum(v, axis=0, keepdims=True) for v in self.sums)
        shift = first * (1.0 / COUNTS[0])
        rows = [(self.center + shift, second - first * shift)] + self.rows
        means = stack_rows([r[0] for r in rows])
        squares = stack_rows([r[1] for r in rows])
        inv_counts = counts_column()
        mean = group_sum(means) * (1.0 / GROUP)
        d = means - mean
        var = group_sum(squares * inv_counts + d * d * (1.0 / GROUP))
        return mean, lax.rsqrt(var + EPS)


def level_rows(level, vec, masks):
    if level < 3:
        return vec[level : level + 1]
    return pick(*masks, vec)


def act_tiles(block, z, scale, offset, buf, keep=None):
    masks = tail_masks()
    for level, cell, row, width, _ in tiles_of(block):
        h = z[cell : cell + TILE, :] * level_rows(level, scale, masks) + level_rows(level, offset, masks)
        a = h * jnp.tanh(h) + h
        if level == 3:
            a = jnp.where(masks[0] | masks[1], a, 0.0)
        write_shifted(buf, row, width, a, C, False)
        if keep is not None:
            keep[cell : cell + TILE, :] = a.astype(bf16)


class Upward:
    def __init__(self, dy_out, z, mean, rstd, gain, shift):
        self.dy_out, self.z, self.rstd, self.neg, self.gain, self.shift = dy_out, z, rstd, -mean * rstd, 0.5 * gain, 0.5 * shift
        self.sums = [[jnp.zeros((8, C), f32), jnp.zeros((8, C), f32)] for _ in COUNTS]

    def add(self, block, da):
        masks = tail_masks()
        for level, cell, _, _, at in tiles_of(block):
            zhat = self.z[cell : cell + TILE, :] * level_rows(level, self.rstd, masks) + level_rows(level, self.neg, masks)
            h = zhat * self.gain + self.shift
            t = jnp.tanh(h)
            dy = da[at : at + TILE] * ((1.0 + t) * (1.0 + h * (1.0 - t)))
            self.dy_out[cell : cell + TILE, :] = dy
            dyz = dy * zhat
            if level < 3:
                parts = [(level, dy, dyz)]
            else:
                parts = [(3 + k, jnp.where(m, dy, 0.0), jnp.where(m, dyz, 0.0)) for k, m in enumerate(masks)]
            for to, one, two in parts:
                self.sums[to] = [self.sums[to][0] + fold(one), self.sums[to][1] + fold(two)]

    def finish(self, sums_out):
        sums_out[0:8, :] = 0.5 * stack_rows([v[0] for v in self.sums])
        sums_out[8:16, :] = 0.5 * stack_rows([v[1] for v in self.sums])


def norm_back(dy, z, mean, rstd, gain, sums, buf):
    sum_dy, sum_dyz = sums[0:8, :], sums[8:16, :]
    inv_counts = counts_column()
    mean_e = group_sum(sum_dy * gain) * inv_counts
    mean_ez = group_sum(sum_dyz * gain) * inv_counts
    on_dy = 0.5 * rstd * gain
    on_zhat = rstd * mean_ez
    on_z = -on_zhat * rstd
    flat = on_zhat * mean * rstd - rstd * mean_e

    def produce(block):
        masks = tail_masks()
        for level, cell, row, width, _ in tiles_of(block):
            at = slice(cell, cell + TILE)
            dz = (
                dy[at, :] * level_rows(level, on_dy, masks)
                + z[at, :] * level_rows(level, on_z, masks)
                + level_rows(level, flat, masks)
            )
            write_shifted(buf, row, width, dz, C, True)

    return produce, [jnp.sum(v, axis=0, keepdims=True) for v in (sum_dyz, sum_dy)]


def center(buf, cells, row, lanes):
    return buf[row : row + cells, lanes : 2 * lanes]


def shape(dims, dtype):
    return jax.ShapeDtypeStruct(dims, dtype)


def pack(vec):
    high = vec.astype(bf16).astype(f32)
    middle = (vec - high).astype(bf16).astype(f32)
    low = vec - high - middle
    return jnp.concatenate([high, middle, low, jnp.zeros_like(vec)], axis=0).astype(bf16)


def unpack(block):
    parts = block.astype(f32)
    return parts[0:8] + parts[8:16] + parts[16:24]


def bit_of(order, step):
    dp = lax.axis_index("dp")
    return jnp.where(lax.axis_index("tower") == 0, dp >> order[0][step], dp >> order[1][step]) & 1


def call(kernel, token, ins, in_specs, outs, out_specs, name, scratch=(), mib=16, alias=None):
    n_in, n_out = len(ins), len(outs)

    def ordered(*refs):
        kernel(*refs[:n_in], *refs[n_in + 1 : n_in + 1 + n_out], *refs[n_in + n_out + 2 :])

    *results, token = pl.pallas_call(
        ordered,
        out_shape=list(outs) + [shape((8, LANES), f32)],
        in_specs=list(in_specs) + [HBM],
        out_specs=list(out_specs) + [HBM],
        scratch_shapes=list(scratch),
        input_output_aliases=alias or {},
        compiler_params=params(mib),
        cost_estimate=pl.CostEstimate(flops=COSTS.get(name, COST), bytes_accessed=1, transcendentals=0),
        name=name,
    )(*ins, token)
    return results, token


def split_store(bit, tap, grad, keep, send):
    half = C // 2
    low, high = grad[:half], grad[half:]
    keep[tap * half : (tap + 1) * half, :] = jnp.where(bit == 1, high, low).astype(bf16)
    send[tap * half : (tap + 1) * half, :] = jnp.where(bit == 1, low, high).astype(bf16)


def halve_kernel(taps, rows, order, step, keep, got, vec, keep_out, send_out, vec_out):
    bit = bit_of(order, step)
    half = rows // 2

    def one(t, _):
        for out, side in ((keep_out, bit), (send_out, 1 - bit)):
            at = pl.ds(pl.multiple_of(t * rows + side * half, half), half)
            to = pl.ds(pl.multiple_of(t * half, half), half)
            out[to, :] = (keep[at, :].astype(f32) + got[at, :].astype(f32)).astype(bf16)
        return 0

    lax.fori_loop(0, taps, one, 0)
    total = vec[...] + unpack(got[taps * rows :, :])
    vec_out[...] = total
    send_out[taps * half :, :] = pack(total)


def add_kernel(taps, rows, keep, got, vec, sum_out, vec_out):
    def one(t, _):
        at = pl.ds(pl.multiple_of(t * rows, rows), rows)
        sum_out[at, :] = (keep[at, :].astype(f32) + got[at, :].astype(f32)).astype(bf16)
        return 0

    lax.fori_loop(0, taps, one, 0)
    total = vec[...] + unpack(got[taps * rows :, :])
    vec_out[...] = total
    sum_out[taps * rows :, :] = pack(total)


def join_kernel(taps, rows, order, step, own, got, out):
    bit = bit_of(order, step)

    def one(t, _):
        at = pl.ds(pl.multiple_of(t * rows, rows), rows)
        out[pl.ds(pl.multiple_of((2 * t + bit) * rows, rows), rows), :] = own[at, :]
        out[pl.ds(pl.multiple_of((2 * t + 1 - bit) * rows, rows), rows), :] = got[at, :]
        return 0

    lax.fori_loop(0, taps, one, 0)


def write_half(layer, side, half_rows, out, wide, sems):
    half = C // 2
    copies = []
    for t in range(9):
        rows = slice(t * half, (t + 1) * half)
        wide[rows, :] = half_rows[rows, :].astype(f32)
        to = pl.multiple_of((layer * 9 + t) * C + side * half, half)
        copies.append(pltpu.make_async_copy(wide.at[rows], out.at[pl.ds(to, half)], sems.at[t]))
        copies[-1].start()
    return copies


def write_own_kernel(layer, order, own, *refs):
    out, wide, sems = refs[-3 - (2 if not layer else 0) :][:1] + refs[-2:]
    copies = write_half(layer, bit_of(order, 0), own, out, wide, sems)
    if not layer:
        vecs, (gains_out, shifts_out) = refs[:LAYERS], refs[-4:-2]
        gains_out[...] = jnp.concatenate([v[0:1, :] for v in vecs], axis=0)
        shifts_out[...] = jnp.concatenate([v[1:2, :] for v in vecs], axis=0)
    for copy in copies:
        copy.wait()


def write_got_kernel(layer, order, extra, got, *refs):
    bit = bit_of(order, 0)
    out, wide, sems = refs[-3 - (1 if extra else 0) :][:1] + refs[-2:]
    copies = write_half(layer, 1 - bit, got, out, wide, sems)
    half = C // 2
    if extra:
        own, vec, _, _, rest, _, _ = refs
        for t in range(extra):
            rest[pl.ds(pl.multiple_of(t * C + bit * half, half), half), :] = own[(9 + t) * half : (10 + t) * half, :]
            rest[pl.ds(pl.multiple_of(t * C + (1 - bit) * half, half), half), :] = got[(9 + t) * half : (10 + t) * half, :]
        rest[extra * C :, :] = pack(vec[...])
    for copy in copies:
        copy.wait()


def write_last_kernel(layers, orders, *refs):
    n = len(layers)
    out, wides, sems = refs[n + 1], refs[n + 2 : 2 * n + 2], refs[-1]
    copies = []
    for k, layer in enumerate(layers):
        copies += write_half(layer, 1 - bit_of(orders[k], 0), refs[k], out, wides[k], sems.at[k])
    for copy in copies:
        copy.wait()


def heads_kernel(own, got, vec, dhead_out, bias_out, scale_out):
    for i in range(3):
        at = slice(i * C, (i + 1) * C)
        turned = (own[at, :].astype(f32) + got[at, :].astype(f32)).T
        for j in range(3):
            dhead_out[i, j] = turned[j * HEAD : (j + 1) * HEAD, :]
    both = vec[...] + unpack(got[3 * C :, :])
    bias_out[...] = both[2:3, 0:HEAD]
    lane = lax.broadcasted_iota(jnp.int32, (8, LANES), 1)
    row = lax.broadcasted_iota(jnp.int32, (8, LANES), 0)
    sums = jnp.sum(both[:, 0:LANES], axis=1, keepdims=True)
    line = jnp.sum(jnp.where((row >= 3) & (lane == row - 3), sums, 0.0), axis=0, keepdims=True)
    scale_out[...] = line[:, 0 : len(COUNTS)]


def features_kernel(keep, got, var, out):
    half = C // 2
    inverse = lax.rsqrt(jnp.where(lax.axis_index("tower") == 0, var[:, :half], var[:, half:]) + EPS)

    def scaled(cell, cells):
        return (keep[pl.ds(cell, cells), :].astype(f32) + got[pl.ds(cell, cells), :].astype(f32)) * inverse

    def one(t, _):
        at = pl.multiple_of(t * TILE, TILE)
        out[pl.ds(at, TILE), :] = scaled(at, TILE).astype(bf16)
        return 0

    lax.fori_loop(0, 1344 // TILE, one, 0)
    tail = scaled(1344, TILE)
    out[1344:PIX, :] = jnp.concatenate([tail[16:24], tail[32:40], tail[26:30]], axis=0).astype(bf16)


def gradients_out(bit, turned, buf, keep, send):
    for i in range(3):
        grad = kernel_grad(turned, buf, i)
        for j in range(3):
            split_store(bit, i * 3 + j, grad[:, j * C : (j + 1) * C], keep, send)


def vector_rows(rows):
    row = lax.broadcasted_iota(jnp.int32, (8, C), 0)
    out = jnp.zeros((8, C), f32)
    for at, value in enumerate(rows):
        out = jnp.where(row == at, value, out)
    return out


def spread_tail(tile, scratch):
    scratch[...] = jnp.zeros(scratch.shape, f32)
    scratch[16:24, :] = tile[0:8]
    scratch[32:40, :] = tile[8:16]
    scratch[26:30, :] = tile[16:20]


class Heads:
    def __init__(self, hg, hk, hbuf, bias, scale):
        self.hg, self.hk, self.hbuf, self.scale = hg, hk, hbuf, scale
        self.bias = jnp.concatenate([bias[...], jnp.zeros((1, LANES - HEAD), f32)], axis=1)
        self.total = jnp.zeros((8, LANES), f32)
        self.scales = [jnp.zeros((8, LANES), f32) for _ in COUNTS]

    def add(self, block, buf):
        _, cells, first, width, _ = block
        raw_block = None
        for i in range(3):
            at = first + (i - 1) * width
            for j in range(3):
                tap = (i * 3 + j) * LANES
                term = lax.dot_general(
                    buf[at : at + cells, j * C : (j + 1) * C],
                    self.hk[tap : tap + LANES, :],
                    (((1,), (1,)), ((), ())),
                    preferred_element_type=f32,
                )
                raw_block = term if raw_block is None else raw_block + term
        lane = lax.broadcasted_iota(jnp.int32, (TILE, LANES), 1)
        dist = (lane >= CLASSES) & (lane < CLASSES + 4) & (lax.axis_index("tower") == 1)
        third, fourth = (m[:, :LANES] for m in tail_masks())
        for level, cell, row, width, at in tiles_of(block):
            raw = raw_block[at : at + TILE] + self.bias
            g = self.hg[cell : cell + TILE, :]
            if level < 3:
                ls, use = self.scale[0:1, level : level + 1], dist
            else:
                ls = jnp.where(third, self.scale[0:1, 3:4], self.scale[0:1, 4:5])
                use = dist & (third | fourth)
            weighted = jnp.where(use, g * jnp.exp(ls * raw), 0.0)
            term = weighted * raw
            parts = [(level, term)] if level < 3 else [(3, jnp.where(third, term, 0.0)), (4, jnp.where(fourth, term, 0.0))]
            for to, value in parts:
                self.scales[to] = self.scales[to] + fold(value)
            tile = jnp.where(dist, weighted * ls, g).astype(bf16).astype(f32)
            self.total = self.total + fold(tile)
            after, before = moved(tile, width)
            middle = pltpu.roll(tile, HEAD, 1)
            after = pltpu.roll(after, 2 * HEAD - LANES, 1)
            rows = slice(row, row + TILE)
            self.hbuf[rows, 0:LANES] = jnp.where(lane < HEAD, before, middle).astype(bf16)
            self.hbuf[rows, LANES : 2 * LANES] = jnp.where(lane < 2 * HEAD - LANES, middle, after).astype(bf16)

    def rows(self):
        return [jnp.sum(v, axis=0, keepdims=True) for v in [self.total] + self.scales]


def prepare_kernel(head, cls, reg, pos, hw, hk, hg, tail):
    box = reg[...].astype(f32) * pos[...].astype(f32)
    is_class = lax.axis_index("tower") == 0
    rows = jnp.concatenate(
        [
            jnp.where(is_class, cls[...].astype(f32), 0.0),
            jnp.where(is_class, 0.0, jnp.concatenate([box, jnp.zeros((3, PIX), f32)], axis=0)),
            jnp.zeros((LANES - CLASSES - 8, PIX), f32),
        ],
        axis=0,
    )
    rows = jnp.concatenate([rows, jnp.zeros((LANES, CELLS - PIX), f32)], axis=1)
    hg[...] = rows.T
    spread_tail(jnp.concatenate([hg[1344:PIX, :]] * 2, axis=1), tail)
    hg[1344:CELLS, :] = tail[:, 0:LANES]
    for i in range(3):
        three = jnp.concatenate([head[i, j].astype(f32) for j in range(3)] + [jnp.zeros((1, C), f32)], axis=0)
        hw[i * C : (i + 1) * C, :] = three.astype(bf16)
        for j in range(3):
            one = jnp.concatenate([head[i, j].astype(f32), jnp.zeros((LANES - HEAD, C), f32)], axis=0)
            hk[(i * 3 + j) * LANES : (i * 3 + j + 1) * LANES, :] = one.astype(bf16)


def first_kernel(
    order, scale, own, other, bn_mean, bn_var, w_hbm, gains, shifts, head_bias, hw, hk, hg,
    w, z_out, a_out, stats_out, dy_out, sums_out, keep_out, send_out, vec_out,
    buf, z_last, a_last, dy, sums, hbuf, turned, tail, sems,
):
    loads = [pltpu.make_async_copy(w_hbm.at[l], w.at[l], sems.at[l]) for l in range(LAYERS)]
    for load in loads:
        load.start()
    half = C // 2
    tower = lax.axis_index("tower")
    clear_gaps(buf)
    clear_gaps(hbuf)
    inverse = lax.rsqrt(bn_var[...] + EPS)
    mean0 = bn_mean[...]

    def halves(rows):
        left = jnp.where(tower == 0, own[rows, :].astype(f32), other[rows, :].astype(f32))
        right = jnp.where(tower == 0, other[rows, :].astype(f32), own[rows, :].astype(f32))
        return (jnp.concatenate([left, right], axis=1) - mean0) * inverse

    def base(block):
        for level, cell, row, width, _ in tiles_of(block):
            if level < 3:
                tile = halves(slice(cell, cell + TILE))
            else:
                spread_tail(halves(slice(1344, PIX)), tail)
                tile = tail[...]
            write_shifted(buf, row, width, tile, C, False)
            a_out[0, cell : cell + TILE, :] = tile.astype(bf16)

    scale_rows = offset_rows = None
    for l in range(LAYERS):
        z = z_out.at[l] if l < LAYERS - 1 else z_last
        stats = Stats()

        def consume(block, l=l, z=z, stats=stats):
            out = conv_block(block, buf, w[l])
            z[block[0] : block[0] + block[1], :] = out
            stats.add(block, out)

        if l == 0:
            produce = base
        else:
            keep = a_out.at[l] if l < LAYERS - 1 else a_last
            before = z_out.at[l - 1]
            produce = lambda block: act_tiles(block, before, scale_rows, offset_rows, buf, keep)
        pipelined(produce, consume, loads[l].wait)
        mean, rstd = stats.finish()
        if l < LAYERS - 1:
            stats_out[l, 0:8, :] = mean
            stats_out[l, 8:16, :] = rstd
        scale_rows = 0.5 * rstd * gains[l : l + 1]
        offset_rows = 0.5 * shifts[l : l + 1] - mean * scale_rows
    l = LAYERS - 1
    heads = Heads(hg, hk, hbuf, head_bias, scale)
    up = Upward(dy, z_last, mean, rstd, gains[l : l + 1], shifts[l : l + 1])
    for i in range(len(BLOCKS) + 2):
        if i < len(BLOCKS):
            act_tiles(BLOCKS[i], z_last, scale_rows, offset_rows, buf)
        if 1 <= i <= len(BLOCKS):
            heads.add(BLOCKS[i - 1], buf)
        if i >= 2:
            _, cells, row, width, _ = BLOCKS[i - 2]
            left = jnp.concatenate([hbuf[row - d * width : row - d * width + cells, :] for d in (-1, 0, 1)], axis=1)
            up.add(BLOCKS[i - 2], jnp.dot(left, hw[...], preferred_element_type=f32))
    up.finish(sums)
    bit = bit_of(order, 0)
    a4t = jnp.concatenate([center(buf, n, r, C).T for _, n, r, _ in PARTS], axis=1)
    for i in range(3):
        split_store(bit, 9 + i, kernel_grad(a4t, hbuf, i), keep_out, send_out)
    produce, norm_sums = norm_back(dy, z_last, mean, rstd, gains[l : l + 1], sums, buf)
    wide = lambda v: jnp.concatenate([v, jnp.zeros_like(v)], axis=1)
    vec = vector_rows(norm_sums + [wide(row) for row in heads.rows()])
    vec_out[...] = vec
    send_out[12 * half :, :] = pack(vec)
    turned[...] = a_last[...].T
    layer_down(l, produce, buf, lambda tap: w[l, tap * C : (tap + 1) * C, :], z_out, stats_out, gains, shifts, dy_out, sums_out)
    gradients_out(bit, turned, buf, keep_out, send_out)


def layer_down(l, produce, buf, weight, z, stats, gains, shifts, dy_out, sums_out):
    k = l - 1
    up = Upward(dy_out, z.at[k], stats[k, 0:8, :], stats[k, 8:16, :], gains[k : k + 1], shifts[k : k + 1])
    pipelined(produce, lambda block: up.add(block, conv_back_block(block, buf, weight)))
    up.finish(sums_out)


def middle_kernel(l, order, dy, sums, z, a, stats, gains, shifts, w, *refs):
    if l:
        dy_out, sums_out, keep_out, send_out, vec_out, buf, turned = refs
    else:
        keep_half, send_half, keep_out, send_out, vec_out, buf, turned = refs
    half = C // 2
    bit = bit_of(order, 0)
    clear_gaps(buf)
    produce, norm_sums = norm_back(
        dy, z.at[l], stats[l, 0:8, :], stats[l, 8:16, :], gains[l : l + 1], sums, buf
    )
    vec = vector_rows(norm_sums)
    vec_out[...] = vec
    send_out[9 * half :, :] = pack(vec)
    turned[...] = a[l].T
    weight = lambda tap: w[l, tap * C : (tap + 1) * C, :]
    if l:
        layer_down(l, produce, buf, weight, z, stats, gains, shifts, dy_out, sums_out)
    else:
        mine = lax.axis_index("tower")

        def consume(block):
            da = conv_back_block(block, buf, weight)
            at = slice(block[0], block[0] + block[1])
            keep_half[at, :] = jnp.where(mine == 0, da[:, :half], da[:, half:])
            send_half[at, :] = jnp.where(mine == 0, da[:, half:], da[:, :half]).astype(bf16)

        pipelined(produce, consume)
    gradients_out(bit, turned, buf, keep_out, send_out)


def run_prepare(token, head, cls, reg, pos):
    return call(
        prepare_kernel,
        token,
        (head, cls, reg, pos),
        [VMEM] * 4,
        [pltpu.VMEM((3 * C, C), bf16), pltpu.VMEM((9 * LANES, C), bf16), pltpu.VMEM((CELLS, LANES), f32)],
        [VMEM] * 3,
        "prepare",
        [pltpu.VMEM((TILE, C), f32)],
        16,
    )


def run_first(order, token, scale, own, other, mean, var, w, gains, shifts, bias, hw, hk, hg):
    half = C // 2
    return call(
        functools.partial(first_kernel, order),
        token,
        (scale, own, other, mean, var, w, gains, shifts, bias, hw, hk, hg),
        [VMEM] * 5 + [HBM] + [VMEM] * 6,
        [
            pltpu.VMEM((LAYERS, 9 * C, C), bf16),
            pltpu.VMEM((LAYERS - 1, CELLS, C), f32),
            pltpu.VMEM((LAYERS - 1, CELLS, C), bf16),
            pltpu.VMEM((LAYERS - 1, 16, C), f32),
            pltpu.VMEM((CELLS, C), f32),
            pltpu.VMEM((16, C), f32),
            pltpu.VMEM((12 * half, C), bf16),
            pltpu.VMEM((12 * half + VEC, C), bf16),
            pltpu.VMEM((8, C), f32),
        ],
        [VMEM] * 9,
        "forward_and_heads",
        [
            pltpu.VMEM((PADDED, 3 * C), bf16),
            pltpu.VMEM((CELLS, C), f32),
            pltpu.VMEM((CELLS, C), bf16),
            pltpu.VMEM((CELLS, C), f32),
            pltpu.VMEM((16, C), f32),
            pltpu.VMEM((PADDED, 2 * LANES), bf16),
            pltpu.VMEM((C, CELLS), bf16),
            pltpu.VMEM((TILE, C), f32),
            pltpu.SemaphoreType.DMA((LAYERS,)),
        ],
        FIRST_MIB,
    )


def run_middle(l, order, token, dy, sums, z, a, stats, gains, shifts, w):
    half = C // 2
    outs = [shape((CELLS, C), f32), shape((16, C), f32)] if l else [shape((CELLS, half), f32), shape((CELLS, half), bf16)]
    outs += [shape((9 * half, C), bf16), shape((9 * half + VEC, C), bf16), shape((8, C), f32)]
    scratch = [
        pltpu.VMEM((PADDED, 3 * C), bf16),
        pltpu.VMEM((C, CELLS), bf16),
    ]
    return call(
        functools.partial(middle_kernel, l, order),
        token,
        (dy, sums, z, a, stats, gains, shifts, w),
        [VMEM] * 8,
        outs,
        [VMEM] * len(outs),
        f"layer_gradients_{l}",
        scratch,
        MIDDLE_MIB,
    )


class Sum:
    def __init__(self, layer, taps, order, bits, keep, send, vec):
        self.layer, self.taps, self.order, self.bits = layer, taps, order, bits
        self.keep, self.vec = keep, vec
        self.splits = min(SPLITS, bits)
        self.rows = C // 2
        self.steps = bits + self.splits - 1
        self.got = self.partner(send, 0)

    def partner(self, value, step):
        pairs = []
        for d in range(1 << self.bits):
            for t in range(2):
                pairs.append((2 * d + t, 2 * (d ^ (1 << self.order[t][step])) + t))
        return lax.ppermute(value, ("dp", "tower"), pairs)

    def advance(self, step, token):
        taps, rows = self.taps, self.rows
        self.done = step
        vec = shape((8, C), f32)
        if step < self.splits:
            half = rows // 2
            (self.keep, send, self.vec), token = call(
                functools.partial(halve_kernel, taps, rows, self.order, step),
                token, (self.keep, self.got, self.vec), [VMEM] * 3,
                [shape((taps * half, C), bf16), shape((taps * half + VEC, C), bf16), vec], [VMEM] * 3,
                f"halve_{self.layer}_{step}",
            )
            self.rows = half
            bit = step
        elif step <= self.bits:
            (send, self.vec), token = call(
                functools.partial(add_kernel, taps, rows),
                token, (self.keep, self.got, self.vec), [VMEM] * 3,
                [shape((taps * rows + VEC, C), bf16), vec], [VMEM] * 2,
                f"add_{self.layer}_{step}",
            )
            self.keep = send
            bit = step if step < self.bits else self.splits - 1
        else:
            bit = self.steps - step
            (send,), token = call(
                functools.partial(join_kernel, taps, rows, self.order, bit + 1),
                token, (self.keep, self.got), [VMEM] * 2,
                [shape((taps * 2 * rows, C), bf16)], [VMEM],
                f"join_{self.layer}_{step}",
            )
            self.keep = send
            self.rows = 2 * rows
        self.got = self.partner(send, bit)
        return token

    def finish(self, token, out, own, vecs):
        extra = 0 if own else self.taps - 9
        outs, out_specs = [shape((LAYERS * 9 * C, C), f32)], [HBM]
        ins, specs = [self.keep if own else self.got], [VMEM]
        if extra:
            ins, specs = ins + [self.keep, self.vec], specs + [VMEM] * 2
            outs.append(shape((extra * C + VEC, C), bf16))
            out_specs.append(VMEM)
        elif own and not self.layer:
            ins, specs = ins + vecs, specs + [VMEM] * LAYERS
            outs += [shape((LAYERS, C), f32)] * 2
            out_specs += [VMEM] * 2
        alias = {}
        if out is not None:
            alias = {len(ins): 0}
            ins, specs = ins + [out], specs + [HBM]
        if own:
            kernel = functools.partial(write_own_kernel, self.layer, self.order)
        else:
            kernel = functools.partial(write_got_kernel, self.layer, self.order, extra)
        return call(
            kernel, token, ins, specs, outs, out_specs, f"write_{self.layer}_{'own' if own else 'got'}",
            [pltpu.VMEM((9 * C // 2, C), f32), pltpu.SemaphoreType.DMA((9,))], 16, alias,
        )


TIMELINE = (
    (2, 0), (1, 0), (3, 1), (0, 0), (2, 1), (3, 2), (2, 2), (3, 3), (1, 1), (0, 1), (3, 4), (2, 3),
    (1, 2), (3, 5), (0, 2), (2, 4), (1, 3), (0, 3), (3, 6), (1, 4), (2, 5), (0, 4), (1, 5), (3, 7),
    (0, 5), (2, 6), (3, 8), (1, 6), (8, 0), (0, 6), (9, 0), (0, 7), (1, 7), (2, 7), (2, 8), (1, 8),
    (0, 8),
)
ORDERS = (
    ((2, 0, 1, 3), (0, 1, 2, 3)),
    ((0, 2, 1, 3), (1, 0, 2, 3)),
    ((1, 2, 0, 3), (2, 0, 1, 3)),
    ((0, 2, 1, 3), (1, 0, 2, 3)),
)


def orders(bits):
    if bits == 4:
        return ORDERS
    line = tuple(range(bits))
    return (((line, line[1:] + line[:1]),) * LAYERS)


def timeline(bits, steps):
    if bits == 4:
        return TIMELINE
    late = [(l, step) for step in range(1, steps + 3) for l in (3, 2, 1, 0)]
    return [(2, 0), (1, 0), (0, 0)] + late + [(FEATURES, 0), (HEADS, 0)]


def body(
    features, bn_mean, bn_var, tower_weight, norm_gain, norm_bias, head_weight, head_bias, level_scale,
    cls_cot, reg_cot, positive, *, dp,
):
    bits = dp.bit_length() - 1
    assert dp == 1 << bits and bits >= 1
    order = orders(bits)
    in_hbm = lambda v: pltpu.with_memory_space_constraint(v, pltpu.HBM)
    own = features[0]
    swap = [(0, 1), (1, 0)]
    other = lax.ppermute(own, "tower", swap)
    w = in_hbm(tower_weight[0].reshape(LAYERS, 9 * C, C))
    gains, shifts = in_hbm(norm_gain[0]), in_hbm(norm_bias[0])
    mean, var = in_hbm(bn_mean[None]), in_hbm(bn_var[None])
    head = in_hbm(jnp.swapaxes(head_weight, 2, 3))
    (hw, hk, hg), token = run_prepare(
        mean, head, in_hbm(jnp.swapaxes(cls_cot[0], 0, 1)), in_hbm(jnp.swapaxes(reg_cot[0], 0, 1)), in_hbm(positive)
    )
    (w, z, a, stats, dy, dy_sums, keep, send, vec), token = run_first(
        order[3], token, in_hbm(level_scale[None]), in_hbm(own), other, mean, var, w, gains, shifts,
        in_hbm(head_bias[None]), hw, hk, hg,
    )
    sums = [None] * LAYERS
    sums[3] = Sum(3, 12, order[3], bits, keep, send, vec)
    out = None
    for l, step in timeline(bits, sums[3].steps):
        if l == FEATURES:
            (feature_grad,), token = call(
                features_kernel, token, (keep_half, got_half, var), [VMEM] * 3,
                [shape((PIX, C // 2), bf16)], [VMEM], "feature_gradient",
            )
        elif l == HEADS:
            (dhead, dbias, dscale), token = call(
                heads_kernel, token, (heads, got_heads, sums[3].vec), [VMEM] * 3,
                [shape((3, 3, HEAD, C), f32), shape((1, HEAD), f32), shape((1, len(COUNTS)), f32)], [VMEM] * 3,
                "head_gradients",
            )
        elif step == 0:
            (*grads, keep, send, vec), token = run_middle(l, order[l], token, dy, dy_sums, z, a, stats, gains, shifts, w)
            sums[l] = Sum(l, 9, order[l], bits, keep, send, vec)
            if l:
                dy, dy_sums = grads
            else:
                keep_half, send_half = grads
                got_half = lax.ppermute(send_half, "tower", swap)
        elif step <= sums[l].steps:
            token = sums[l].advance(step, token)
        elif step == sums[l].steps + 1:
            assert l or all(one.done >= bits for one in sums)
            (out, *more), token = sums[l].finish(token, out, True, [one.vec for one in sums])
            if l == 0:
                dgain, dshift = more
        elif l == 3:
            (out, heads), token = sums[l].finish(token, out, False, None)
            got_heads = lax.ppermute(heads, "tower", swap)
        elif l == 0:
            last = (2, 1, 0)
            (out,), token = call(
                functools.partial(write_last_kernel, last, [order[k] for k in last]), token,
                [sums[k].got for k in last] + [out], [VMEM] * 3 + [HBM], [shape((LAYERS * 9 * C, C), f32)], [HBM],
                "write_0_got", [pltpu.VMEM((9 * C // 2, C), f32)] * 3 + [pltpu.SemaphoreType.DMA((3, 9))], 24, {3: 0},
            )
    return (
        feature_grad[None],
        out.reshape(1, LAYERS, 3, 3, C, C),
        dgain[None],
        dshift[None],
        jnp.swapaxes(dhead, 2, 3),
        dbias[0],
        dscale[0],
    )


def solution(mesh):
    return jax.shard_map(
        functools.partial(body, dp=mesh.shape["dp"]),
        mesh=mesh,
        in_specs=(
            P("dp", None, "tower"),
            P(),
            P(),
            P("tower", None, None, None, None, None),
            P("tower", None, None),
            P("tower", None, None),
            P(),
            P(),
            P(),
            P("dp", None, None),
            P("dp", None, None),
            P("dp", None),
        ),
        out_specs=(
            P("dp", None, "tower"),
            P("tower", None, None, None, None, None),
            P("tower", None, None),
            P("tower", None, None),
            P(),
            P(),
            P(),
        ),
        check_vma=False,
    )
```
